32 devices in a mesh: dp: 8 (over z, y), mp: 4 (over x, core).
Axes of the slice: x: 2, y: 2, z: 4, core: 2. Of those that a mesh axis runs over, the one named last changes fastest.
Arguments:
- layer_input: bfloat16 [4096, 2048], P(('dp', 'mp')), may hold values from -6 to 6
- output_grad: bfloat16 [4096, 2048], P(('dp', 'mp')), may hold values from -6 to 6
- attention_gain: bfloat16 [2048], P('dp'), may hold values from 0.25 to 1.75
- query_weight: bfloat16 [2048, 2048], P('dp', 'mp'), may hold values from -0.125 to 0.125
- key_weight: bfloat16 [2048, 256], P('dp'), may hold values from -0.125 to 0.125
- value_weight: bfloat16 [2048, 256], P('dp'), may hold values from -0.125 to 0.125
- output_weight: bfloat16 [2048, 2048], P('mp', 'dp'), may hold values from -0.5 to 0.5
- query_shrink: bfloat16 [2048, 256], P('dp'), may hold values from -0.125 to 0.125
- query_expand: bfloat16 [256, 2048], P('dp', 'mp'), may hold values from -0.375 to 0.375
- key_shrink: bfloat16 [2048, 256], P('dp'), may hold values from -0.125 to 0.125
- key_expand: bfloat16 [256, 256], P('dp'), may hold values from -0.375 to 0.375
- value_shrink: bfloat16 [2048, 256], P('dp'), may hold values from -0.125 to 0.125
- value_expand: bfloat16 [256, 256], P('dp'), may hold values from -0.375 to 0.375
- output_shrink: bfloat16 [2048, 256], P(('mp', 'dp')), may hold values from -0.5 to 0.5
- output_expand: bfloat16 [256, 2048], P('dp'), may hold values from -0.375 to 0.375
- feedforward_gain: bfloat16 [2048], P('dp'), may hold values from 0.25 to 1.75
- gate_weight: bfloat16 [2048, 16384], P('dp', 'mp'), may hold values from -0.125 to 0.125
- up_weight: bfloat16 [2048, 16384], P('dp', 'mp'), may hold values from -0.125 to 0.125
- down_weight: bfloat16 [16384, 2048], P('mp', 'dp'), may hold values from -0.046875 to 0.046875
- gate_shrink: bfloat16 [2048, 256], P('dp'), may hold values from -0.125 to 0.125
- gate_expand: bfloat16 [256, 16384], P('dp', 'mp'), may hold values from -0.375 to 0.375
- up_shrink: bfloat16 [2048, 256], P('dp'), may hold values from -0.125 to 0.125
- up_expand: bfloat16 [256, 16384], P('dp', 'mp'), may hold values from -0.375 to 0.375
- down_shrink: bfloat16 [16384, 256], P(('mp', 'dp')), may hold values from -0.046875 to 0.046875
- down_expand: bfloat16 [256, 2048], P('dp'), may hold values from -0.375 to 0.375
- group_ids: int32 [4096], P('dp'), may hold values from 0 to 15, as said below
- positions: int32 [4096], P('dp'), may hold values from 0 to 191, as said below
- segments: int32 [4096], P('dp'), may hold values from 0 to 2, as said below
Outputs:
- layer_output: bfloat16 [4096, 2048], P(('dp', 'mp'))
- input_grad: float32 [4096, 2048], P(('dp', 'mp'))
- attention_gain_grad: float32 [2048], P(('dp', 'mp'))
- query_weight_grad: float32 [2048, 2048], P('dp', 'mp')
- key_weight_grad: float32 [2048, 256], P(('dp', 'mp'))
- value_weight_grad: float32 [2048, 256], P(('dp', 'mp'))
- output_weight_grad: float32 [2048, 2048], P('mp', 'dp')
- query_shrink_grad: float32 [2048, 256], P(('dp', 'mp'))
- query_expand_grad: float32 [256, 2048], P('dp', 'mp')
- key_shrink_grad: float32 [2048, 256], P(('dp', 'mp'))
- key_expand_grad: float32 [256, 256], P(('dp', 'mp'))
- value_shrink_grad: float32 [2048, 256], P(('dp', 'mp'))
- value_expand_grad: float32 [256, 256], P(('dp', 'mp'))
- output_shrink_grad: float32 [2048, 256], P(('mp', 'dp'))
- output_expand_grad: float32 [256, 2048], P('dp')
- feedforward_gain_grad: float32 [2048], P(('dp', 'mp'))
- gate_weight_grad: float32 [2048, 16384], P('dp', 'mp')
- up_weight_grad: float32 [2048, 16384], P('dp', 'mp')
- down_weight_grad: float32 [16384, 2048], P('mp', 'dp')
- gate_shrink_grad: float32 [2048, 256], P(('dp', 'mp'))
- gate_expand_grad: float32 [256, 16384], P('dp', 'mp')
- up_shrink_grad: float32 [2048, 256], P(('dp', 'mp'))
- up_expand_grad: float32 [256, 16384], P('dp', 'mp')
- down_shrink_grad: float32 [16384, 256], P(('mp', 'dp'))
- down_expand_grad: float32 [256, 2048], P('dp')
The draws below stay inside these ranges and needn't reach their ends.
Inputs may be any that keep to these rules, and one draw needn't show every extreme that they name: `group_ids`: the rows of each index of dp hold 2 whole groups, with ids that index times 2 up to 2 more, the groups' tokens mixed in an order drawn from the seed; a group has 128 prompt tokens and 2 continuations of 64 tokens. A group's prompt tokens have positions 0 to 127 once each; each continuation's tokens have 128 to 191 once each. `segments`: 0 on prompt tokens; the continuations of a group are numbered 1 to 2.
All inputs are finite; a program needn't handle non-finite values.
Results may differ from the reference program's by a relative error of at most 0.024.
Values may be sent and summed in bfloat16 or wider, within the bound.
A program may use at most 320 MiB of HBM per device.

```python
import jax
import jax.numpy as jnp
from jax import lax

D = 2048
HEADS = 8
HD = 256
FF = 16384
R = 256
PROMPT = 128
CLEN = 64
GROUPS_DEV = 2
HQ = 2048
GROUP = 256
TOK_DEV = 512
TOKENS = 4096


def group_layout(key):
    devices_count = TOKENS // TOK_DEV
    keys = jax.random.split(jax.random.fold_in(key, 11), devices_count)
    order = jax.vmap(lambda single: jax.random.permutation(single, TOK_DEV))(keys)
    offset = order % GROUP
    local = order // GROUP
    device = jnp.arange(devices_count, dtype=jnp.int32)[:, None]
    group = device * GROUPS_DEV + local
    later = offset - PROMPT
    segment = jnp.where(offset < PROMPT, 0, 1 + later // CLEN)
    place = jnp.where(offset < PROMPT, offset, PROMPT + later % CLEN)
    return (group.reshape(-1).astype(jnp.int32), place.reshape(-1).astype(jnp.int32), segment.reshape(-1).astype(jnp.int32))


def draw_group_ids(key, part):
    return group_layout(key)[0]


def draw_positions(key, part):
    return group_layout(key)[1]


def draw_segments(key, part):
    return group_layout(key)[2]


def block_levels(rng, shape, shards, low, high):
    def one(position, blocks):
        draws = jax.random.uniform(jax.random.fold_in(jax.random.fold_in(rng, 6), position), (blocks,), jnp.float32, low / len(shards), high / len(shards))
        return jnp.repeat(jnp.exp(draws), shape[position] // blocks).reshape((-1,) + (1,) * (len(shape) - position - 1))

    factor_of = one(*shards[0])
    for cut in shards[1:]:
        factor_of = factor_of * one(*cut)
    return factor_of


def noise(stream_key, dims, scale, most, cuts=(), kind=jnp.bfloat16):
    loudness = block_levels(stream_key, dims, cuts, -0.22, 0.18) if cuts else 1.0
    drawn = jax.random.normal(stream_key, dims, jnp.float32) * scale * loudness
    return jnp.minimum(jnp.maximum(drawn, -most), most).astype(kind)


def setup_inputs(seed: int = 0) -> dict:
    key_list = jax.random.split(jax.random.key(seed), 29)
    layer_input = noise(key_list[0], (TOKENS, D), 1.0, 6.0, ((0, 32),))
    output_grad = noise(key_list[1], (TOKENS, D), 1.0, 6.0, ((0, 32),))
    attention_gain = jnp.clip(1.0 + 0.15 * jax.random.normal(key_list[2], (D,), jnp.float32), 0.25, 1.75).astype(jnp.bfloat16)
    query_weight = noise(key_list[3], (D, HQ), D ** -0.5, 0.125, ((0, 8), (1, 4)))
    key_weight = noise(key_list[4], (D, HD), D ** -0.5, 0.125, ((0, 8),))
    value_weight = noise(key_list[5], (D, HD), D ** -0.5, 0.125, ((0, 8),))
    output_weight = noise(key_list[6], (HQ, D), (HQ // 16) ** -0.5, 0.5, ((0, 4), (1, 8)))
    query_shrink = noise(key_list[7], (D, R), D ** -0.5, 0.125, ((0, 8),))
    query_expand = noise(key_list[8], (R, HQ), R ** -0.5, 0.375, ((0, 8), (1, 4)))
    key_shrink = noise(key_list[9], (D, R), D ** -0.5, 0.125, ((0, 8),))
    key_expand = noise(key_list[10], (R, HD), R ** -0.5, 0.375, ((0, 8),))
    value_shrink = noise(key_list[11], (D, R), D ** -0.5, 0.125, ((0, 8),))
    value_expand = noise(key_list[12], (R, HD), R ** -0.5, 0.375, ((0, 8),))
    output_shrink = noise(key_list[13], (HQ, R), (HQ // 16) ** -0.5, 0.5, ((0, 32),))
    output_expand = noise(key_list[14], (R, D), R ** -0.5, 0.375, ((0, 8),))
    feedforward_gain = jnp.clip(1.0 + 0.15 * jax.random.normal(key_list[15], (D,), jnp.float32), 0.25, 1.75).astype(jnp.bfloat16)
    gate_weight = noise(key_list[16], (D, FF), D ** -0.5, 0.125, ((0, 8), (1, 4)))
    up_weight = noise(key_list[17], (D, FF), D ** -0.5, 0.125, ((0, 8), (1, 4)))
    down_weight = noise(key_list[18], (FF, D), FF ** -0.5, 0.046875, ((0, 4), (1, 8)))
    gate_shrink = noise(key_list[19], (D, R), D ** -0.5, 0.125, ((0, 8),))
    gate_expand = noise(key_list[20], (R, FF), R ** -0.5, 0.375, ((0, 8), (1, 4)))
    up_shrink = noise(key_list[21], (D, R), D ** -0.5, 0.125, ((0, 8),))
    up_expand = noise(key_list[22], (R, FF), R ** -0.5, 0.375, ((0, 8), (1, 4)))
    down_shrink = noise(key_list[23], (FF, R), FF ** -0.5, 0.046875, ((0, 32),))
    down_expand = noise(key_list[24], (R, D), R ** -0.5, 0.375, ((0, 8),))
    group_ids = draw_group_ids(jax.random.fold_in(key_list[28], 71), 0)
    positions = draw_positions(jax.random.fold_in(key_list[28], 71), 0)
    segments = draw_segments(jax.random.fold_in(key_list[28], 71), 0)
    return dict(layer_input=layer_input, output_grad=output_grad, attention_gain=attention_gain, query_weight=query_weight, key_weight=key_weight, value_weight=value_weight, output_weight=output_weight, query_shrink=query_shrink, query_expand=query_expand, key_shrink=key_shrink, key_expand=key_expand, value_shrink=value_shrink, value_expand=value_expand, output_shrink=output_shrink, output_expand=output_expand, feedforward_gain=feedforward_gain, gate_weight=gate_weight, up_weight=up_weight, down_weight=down_weight, gate_shrink=gate_shrink, gate_expand=gate_expand, up_shrink=up_shrink, up_expand=up_expand, down_shrink=down_shrink, down_expand=down_expand, group_ids=group_ids, positions=positions, segments=segments)


EPS = 1e-06

@jax.custom_vjp
def low(v):
    return lax.optimization_barrier(v.astype(jnp.bfloat16)).astype(jnp.float32)

@jax.custom_vjp
def low_back(v):
    return v

def low_keep(v):
    return (low(v), None)

def low_pass(kept, grad):
    return (grad,)

def back_keep(v):
    return (v, None)

def back_low(kept, grad):
    return (low(grad),)
low.defvjp(low_keep, low_pass)
low_back.defvjp(back_keep, back_low)

def matmul(left, right):
    return jnp.dot(left, right, precision=lax.Precision.HIGHEST)

def rms_scale(rows, gain):
    return rows * lax.rsqrt(lax.optimization_barrier(jnp.mean(rows * rows, axis=-1, keepdims=True)) + EPS) * gain

def rotary(entries, places, sign):
    half = entries.shape[-1] // 2
    freq = 10000.0 ** (-jnp.arange(half).astype(jnp.float32) * 2.0 / entries.shape[-1])
    angle = places.astype(jnp.float32)[:, None] * freq[None, :]
    cosine = jnp.cos(angle)[:, None, :]
    sine = sign * jnp.sin(angle)[:, None, :]
    first = entries[..., :half]
    second = entries[..., half:]
    return jnp.concatenate([first * cosine - second * sine, second * cosine + first * sine], axis=-1)

def attend(block):
    queries, keys_rot, values, groups, places, parts = block
    allowed = (groups[:, None] == groups[None, :]) & (places[None, :] <= places[:, None]) & ((parts[None, :] == 0) | (parts[None, :] == parts[:, None]))
    scores = low_back(jnp.einsum('thd,sd->hts', queries, keys_rot, precision=lax.Precision.HIGHEST))
    scores = jnp.where(allowed[None], scores, -1e+30)
    shifted = scores - lax.optimization_barrier(jnp.max(scores, axis=-1, keepdims=True))
    expo = jnp.exp(shifted)
    probability = expo / lax.optimization_barrier(jnp.sum(expo, axis=-1, keepdims=True))
    return jnp.einsum('hts,sd->thd', low(probability), values, precision=lax.Precision.HIGHEST)

def reference(layer_input, output_grad, attention_gain, query_weight, key_weight, value_weight, output_weight, query_shrink, query_expand, key_shrink, key_expand, value_shrink, value_expand, output_shrink, output_expand, feedforward_gain, gate_weight, up_weight, down_weight, gate_shrink, gate_expand, up_shrink, up_expand, down_shrink, down_expand, group_ids, positions, segments):
    blocks = TOKENS // TOK_DEV

    def forward(inputs, gain_one, w_query, w_key, w_value, w_output, query_a, query_b, key_a, key_b, value_a, value_b, output_a, output_b, gain_two, w_gate, w_up, w_down, gate_a, gate_b, up_a, up_b, down_a, down_b):
        normed = low(rms_scale(inputs, gain_one))
        query_lin = matmul(normed, w_query) + matmul(low(matmul(normed, query_a)), query_b)
        key_lin = matmul(normed, w_key) + matmul(low(matmul(normed, key_a)), key_b)
        value_lin = matmul(normed, w_value) + matmul(low(matmul(normed, value_a)), value_b)
        queries = low(rotary(low_back(query_lin).reshape(TOKENS, HEADS, HD), positions, 1.0) * HD ** (-0.5))
        keys_rot = low(rotary(key_lin.reshape(TOKENS, 1, HD), positions, 1.0)).reshape(TOKENS, HD)
        values = low(value_lin)
        mixed = lax.map(jax.checkpoint(attend), (queries.reshape(blocks, TOK_DEV, HEADS, HD), keys_rot.reshape(blocks, TOK_DEV, HD), values.reshape(blocks, TOK_DEV, HD), group_ids.reshape(blocks, TOK_DEV), positions.reshape(blocks, TOK_DEV), segments.reshape(blocks, TOK_DEV)))
        mixed = low(low_back(mixed.reshape(TOKENS, HQ)))
        reduced = low(low_back(matmul(mixed, output_a)))
        middle = inputs + low_back(matmul(mixed, w_output) + matmul(reduced, output_b))
        normed_feed = low(rms_scale(middle, gain_two))
        gate_pre = low_back(matmul(normed_feed, w_gate) + matmul(low(matmul(normed_feed, gate_a)), gate_b))
        up_pre = low_back(matmul(normed_feed, w_up) + matmul(low(matmul(normed_feed, up_a)), up_b))
        hidden = low(jax.nn.gelu(gate_pre, approximate=True) * up_pre)
        reduced_feed = low(low_back(matmul(hidden, down_a)))
        return middle + low_back(matmul(hidden, w_down) + matmul(reduced_feed, down_b))
    floats = [v.astype(jnp.float32) for v in (layer_input, attention_gain, query_weight, key_weight, value_weight, output_weight, query_shrink, query_expand, key_shrink, key_expand, value_shrink, value_expand, output_shrink, output_expand, feedforward_gain, gate_weight, up_weight, down_weight, gate_shrink, gate_expand, up_shrink, up_expand, down_shrink, down_expand)]
    result, pullback = jax.vjp(forward, *floats)
    grads = pullback(output_grad.astype(jnp.float32))
    return (result.astype(jnp.bfloat16), grads[0], grads[1], grads[2], grads[3], grads[4], grads[5], grads[6], grads[7], grads[8], grads[9], grads[10], grads[11], grads[12], grads[13], grads[14], grads[15], grads[16], grads[17], grads[18], grads[19], grads[20], grads[21], grads[22], grads[23])
```

```python
import functools
from types import SimpleNamespace

import jax
import jax.numpy as jnp
from jax import lax
from jax.experimental import pallas as pl
from jax.experimental.pallas import tpu as pltpu
from jax.sharding import PartitionSpec as P

MESH = pl.DeviceIdType.MESH
MIB = 1 << 20

EPS = 1e-06


def matmul(left, right):
    return jnp.dot(left, right, preferred_element_type=jnp.float32)


def against(left, right):
    return lax.dot_general(
        left, right, (((1,), (1,)), ((), ())), preferred_element_type=jnp.float32
    )


def outer_sum(left, right):
    return lax.dot_general(
        left, right, (((0,), (0,)), ((), ())), preferred_element_type=jnp.float32
    )


def against_exact(left, right):
    return lax.dot_general(
        left,
        right,
        (((1,), (1,)), ((), ())),
        precision=lax.Precision.HIGHEST,
        preferred_element_type=jnp.float32,
    )


def outer_exact(left, right):
    return lax.dot_general(
        left,
        right,
        (((0,), (0,)), ((), ())),
        precision=lax.Precision.HIGHEST,
        preferred_element_type=jnp.float32,
    )


def norm_rows(rows, gain):
    return rows * lax.rsqrt(jnp.mean(rows * rows, axis=-1, keepdims=True) + EPS) * gain


def rotary(entries, places, sign):
    half = entries.shape[-1] // 2
    freq = 10000.0 ** (-jnp.arange(half).astype(jnp.float32) * 2.0 / entries.shape[-1])
    angle = places.astype(jnp.float32)[:, None] * freq[None, :]
    cosine = jnp.cos(angle)[:, None, :]
    sine = sign * jnp.sin(angle)[:, None, :]
    first = entries[..., :half]
    second = entries[..., half:]
    return jnp.concatenate(
        [first * cosine - second * sine, second * cosine + first * sine], axis=-1
    )


class Wires:
    def __init__(self, levels, sends, lands, locals_=None):
        self.sends, self.lands, self.locals = sends, lands, locals_
        self.levels = levels
        self.count = self.local_count = 0
        self.open = []
        dp, mp = lax.axis_index("dp"), lax.axis_index("mp")
        self.dp, self.mp = dp, mp
        self.z, self.y, self.x, self.c = dp // 2, dp % 2, mp // 2, mp % 2

    def take(self, number=1):
        first = self.count
        self.count += number
        assert self.count <= self.sends.shape[0], self.count
        return first

    def at(self, z, y, x, c):
        return (z * 2 + y, x * 2 + c)

    def up(self):
        return self.at(self.z + 1, self.y, self.x, self.c)

    def down(self):
        return self.at(self.z - 1, self.y, self.x, self.c)

    def over_x(self):
        return self.at(self.z, self.y, 1 - self.x, self.c)

    def over_y(self):
        return self.at(self.z, 1 - self.y, self.x, self.c)

    def over_core(self):
        return self.at(self.z, self.y, self.x, 1 - self.c)

    def copy(self, source, target, out, land, device):
        return pltpu.make_async_remote_copy(
            src_ref=source,
            dst_ref=target,
            send_sem=self.sends.at[out],
            recv_sem=self.lands.at[land],
            device_id=device,
            device_id_type=MESH,
        )

    def send(self, source, target, out, land, device, when=True):
        made = self.copy(source, target, out, land, device)
        under(when, made.start)
        self.open.append((when, made.wait_send))

    def landed(self, target, land):
        self.copy(target, target, land, land, self.over_x()).wait_recv()

    def local(self, source, target):
        made = pltpu.make_async_copy(source, target, self.locals.at[self.local_count])
        self.local_count += 1
        assert self.local_count <= self.locals.shape[0], self.local_count
        made.start()
        return made

    def finish(self):
        for when, wait in self.open:
            under(when, wait)

    def greet(self, far=False, flat=False):
        barrier = pltpu.get_barrier_semaphore()

        def call(device):
            pl.semaphore_signal(barrier, inc=1, device_id=device, device_id_type=MESH)

        call(self.over_x())
        call(self.over_core())
        if far:
            call(self.at(self.z, self.y, 1 - self.x, 1 - self.c))
            for step in range(1, 2 * self.levels):
                call((lax.rem(self.dp + step, 2 * self.levels), self.mp))
            pl.semaphore_wait(barrier, 2 + 2 * self.levels)
            return
        if flat:
            pl.semaphore_wait(barrier, 2)
            return
        call(self.over_y())
        pl.when(self.z > 0)(lambda: call(self.down()))
        pl.when(self.z < self.levels - 1)(lambda: call(self.up()))
        ends = jnp.where(self.z > 0, 1, 0) + jnp.where(self.z < self.levels - 1, 1, 0)
        pl.semaphore_wait(barrier, 3 + ends)


def under(when, act):
    if when is True:
        act()
    else:
        pl.when(when)(act)


def sides(w, step):
    yield (True, w.z - step, w.z >= step)
    yield (False, w.z + step, w.z < w.levels - step)


def gather_all(w, own, at, parts):
    z, y, x, c = w.z, w.y, w.x, w.c
    n = w.levels
    rise, fall, by_x, by_y, last_x, last_y = (w.take(n) for _ in range(6))
    by_core = w.take(4 * n)

    def core(block, zs, ys, xs):
        place = by_core + zs * 4 + ys * 2 + xs
        return (block, block, place, place, w.over_core())

    here = at(z, y, x, c)
    kept = w.local(own, here)
    w.send(own, here, rise + z, rise + z, w.up(), z < n - 1)
    w.send(own, here, fall + z, fall + z, w.down(), z > 0)
    w.send(own, here, by_x + z, by_x + z, w.over_x())
    w.send(own, here, by_y + z, by_y + z, w.over_y())
    place = by_core + z * 4 + y * 2 + x
    w.send(own, here, place, place, w.over_core())
    yield

    def plane(zs, ok):
        block = at(zs, y, 1 - x, c)
        under(ok, lambda: w.landed(block, by_x + zs))
        for piece in parts(block)[:1]:
            if piece is not None:
                w.send(piece, piece, last_y + zs, last_y + zs, w.over_y(), ok)
        w.send(*core(block, zs, y, 1 - x), ok)
        block = at(zs, 1 - y, x, c)
        under(ok, lambda: w.landed(block, by_y + zs))
        for piece in parts(block)[1:]:
            if piece is not None:
                w.send(piece, piece, last_x + zs, last_x + zs, w.over_x(), ok)
        w.send(*core(block, zs, 1 - y, x), ok)

    plane(z, True)
    yield
    for step in range(1, n):
        for rising, zs, ok in sides(w, step):
            block = at(zs, y, x, c)
            lane = rise if rising else fall
            under(ok, lambda: w.landed(block, lane + zs))
            if rising:
                w.send(block, block, rise + zs, rise + zs, w.up(), jnp.logical_and(ok, z < n - 1))
            else:
                w.send(block, block, fall + zs, fall + zs, w.down(), jnp.logical_and(ok, z > 0))
            w.send(block, block, by_x + zs, by_x + zs, w.over_x(), ok)
            w.send(block, block, by_y + zs, by_y + zs, w.over_y(), ok)
            w.send(*core(block, zs, y, x), ok)
        yield
        for _, zs, ok in sides(w, step):
            plane(zs, ok)
        yield
    for step in range(n):
        for _, zs, ok in sides(w, step) if step else [(True, z, True)]:
            block = at(zs, 1 - y, 1 - x, c)
            for piece, lane in zip(parts(block), (last_y, last_x)):
                if piece is not None:
                    under(ok, lambda: w.landed(piece, lane + zs))
            w.send(*core(block, zs, 1 - y, 1 - x), ok)
        yield
    for zs in range(n):
        for ys in range(2):
            for xs in range(2):
                w.landed(at(zs, ys, xs, 1 - c), by_core + zs * 4 + ys * 2 + xs)
    kept.wait()


def gather_dp(w, own, at):
    z, y, n = w.z, w.y, w.levels
    rise, fall, by_y = (w.take(n) for _ in range(3))
    here = at(z, y)
    kept = w.local(own, here)
    w.send(own, here, rise + z, rise + z, w.up(), z < n - 1)
    w.send(own, here, fall + z, fall + z, w.down(), z > 0)
    w.send(own, here, by_y + z, by_y + z, w.over_y())
    yield
    yield
    for step in range(1, n):
        for rising, zs, ok in sides(w, step):
            block = at(zs, y)
            lane = rise if rising else fall
            under(ok, lambda: w.landed(block, lane + zs))
            if rising:
                w.send(block, block, rise + zs, rise + zs, w.up(), jnp.logical_and(ok, z < n - 1))
            else:
                w.send(block, block, fall + zs, fall + zs, w.down(), jnp.logical_and(ok, z > 0))
            w.send(block, block, by_y + zs, by_y + zs, w.over_y(), ok)
        yield
        yield
    for zs in range(n):
        w.landed(at(zs, 1 - y), by_y + zs)
    kept.wait()


def gather_mp(w, own, at):
    x, c = w.x, w.c
    first, second = w.take(), w.take(2)
    here = at(x, c)
    kept = w.local(own, here)
    w.send(own, here, first, first, w.over_x())
    w.send(own, here, second, second, w.over_core())
    yield
    block = at(1 - x, c)
    w.landed(block, first)
    w.send(block, block, second + 1, second + 1, w.over_core())
    yield
    w.landed(at(x, 1 - c), second)
    w.landed(at(1 - x, 1 - c), second + 1)
    kept.wait()


def exchange_dp(w, source, target):
    count = 2 * w.levels
    first = w.take(count)
    kept = w.local(source(w.dp), target(w.dp))
    for step in range(1, count):
        there = lax.rem(w.dp + step, count)
        w.send(source(there), target(w.dp), first + step, first + step, (there, w.mp))
        yield
    for step in range(1, count):
        w.landed(target(lax.rem(w.dp + count - step, count)), first + step)
    kept.wait()


PACE = 6


def turn(steps, after=()):
    spare = [one for one in after for _ in range(7)]
    turn_on(steps, spare)
    for one in spare:
        next(one)
    turn_on(after)


def turn_on(steps, spare=()):
    steps = list(steps)
    while steps:
        for _ in range(min(PACE, len(spare))):
            next(spare.pop(0))
        left = []
        for one in steps:
            try:
                next(one)
                left.append(one)
            except StopIteration:
                pass
        steps = left


CHUNK = 16


def add_up(target, *sources):
    rows = target.shape[0]

    def one(i, unused):
        part = pl.ds(pl.multiple_of(i * CHUNK, CHUNK), CHUNK)
        total = sources[0][part, :].astype(jnp.float32)
        for source in sources[1:]:
            total = total + source[part, :].astype(jnp.float32)
        target[part, :] = total.astype(target.dtype)
        return unused

    lax.fori_loop(0, rows // CHUNK, one, 0)


def chain_z(w, own, below, above, out):
    z, n = w.z, w.levels
    rise, fall = w.take(n), w.take(n)
    for step in range(n - 1, 0, -1):
        for rising, zt, ok in ((True, z + step, z < n - step), (False, z - step, z >= step)):
            lane = rise if rising else fall
            slot = below(zt) if rising else above(zt)
            inner = jnp.logical_and(ok, (z > 0) if rising else (z < n - 1))

            def take_in():
                w.landed(slot, lane + zt)
                add_up(own(zt), own(zt), slot)

            under(inner, take_in)
            w.send(own(zt), slot, lane + zt, lane + zt, w.up() if rising else w.down(), ok)
        yield
    under(z > 0, lambda: w.landed(below(z), rise + z))
    under(z < n - 1, lambda: w.landed(above(z), fall + z))
    under(z == 0, lambda: add_up(out, own(z), above(z)))
    under(z == n - 1, lambda: add_up(out, own(z), below(z)))
    under(
        jnp.logical_and(z > 0, z < n - 1), lambda: add_up(out, own(z), below(z), above(z))
    )


def scatter_all(w, part, own, core, half_x, half_y, full_x, full_y, below, above, out):
    z, y, x, c, n = w.z, w.y, w.x, w.c, w.levels
    lanes = {name: w.take(n) for name in ("hx", "hy", "fx", "fy")}
    to_core = w.take(4 * n)
    rows = own.shape[1]
    cut = rows // 2 // CHUNK * CHUNK
    halves = (pl.ds(0, cut), pl.ds(cut, rows - cut))

    def slot(zs, ys, xs):
        return zs * 4 + ys * 2 + xs

    kinds = ((1 - y, 1 - x), (1 - y, x), (y, 1 - x), (y, x))
    order = [(True, z, True)] if n == 1 else []
    for step in range(n - 1, 0, -1):
        order += [side for side in sides(w, step)]
    order.append((True, z, True))
    kept = {}
    for kind, (ys, xs) in enumerate(kinds):
        for place, (_, zs, ok) in enumerate(order):
            here = slot(zs, ys, xs)
            w.send(
                part.at[(zs * 2 + ys) * 4 + xs * 2 + (1 - c)],
                core.at[here],
                to_core + here,
                to_core + here,
                w.over_core(),
                ok,
            )
            made = pltpu.make_async_copy(
                part.at[(zs * 2 + ys) * 4 + xs * 2 + c], own.at[here], w.locals.at[here]
            )
            under(ok, made.start)
            kept[kind, place] = made
    yield
    for kind, (ys, xs) in enumerate(kinds):
        for place, (_, zs, ok) in enumerate(order):
            here = slot(zs, ys, xs)

            def act():
                kept[kind, place].wait()
                w.landed(core.at[here], to_core + here)
                add_up(own.at[here], own.at[here], core.at[here])
                if kind == 1:
                    w.landed(half_x.at[zs], lanes["hx"] + zs)
                    add_up(own.at[here, halves[0]], own.at[here, halves[0]], half_x.at[zs])
                if kind == 2:
                    w.landed(half_y.at[zs], lanes["hy"] + zs)
                    add_up(own.at[here, halves[1]], own.at[here, halves[1]], half_y.at[zs])
                if kind == 3:
                    w.landed(full_x.at[zs], lanes["fx"] + zs)
                    w.landed(full_y.at[zs], lanes["fy"] + zs)
                    add_up(own.at[here], own.at[here], full_x.at[zs], full_y.at[zs])

            under(ok, act)
            if kind == 0:
                for name, half, target, device in (
                    ("hx", halves[0], half_x, w.over_x()),
                    ("hy", halves[1], half_y, w.over_y()),
                ):
                    lane = lanes[name] + zs
                    w.send(own.at[here, half], target.at[zs], lane, lane, device, ok)
            if kind == 1:
                w.send(own.at[here], full_y.at[zs], lanes["fy"] + zs, lanes["fy"] + zs, w.over_y(), ok)
            if kind == 2:
                w.send(own.at[here], full_x.at[zs], lanes["fx"] + zs, lanes["fx"] + zs, w.over_x(), ok)
        yield

    yield from chain_z(
        w, lambda zt: own.at[slot(zt, y, x)], lambda zt: below.at[zt], lambda zt: above.at[zt], out
    )


def scatter_all_scratch(n, rows, columns):
    cut = rows // 2 // CHUNK * CHUNK
    shapes = [(4 * n, rows)] * 2 + [(n, cut), (n, rows - cut)] + [(n, rows)] * 4
    return [pltpu.VMEM(shape + (columns,), jnp.bfloat16) for shape in shapes]


def scatter_dp(w, part, own, over, below, above, out):
    z, y, n = w.z, w.y, w.levels
    by_y = w.take(n)
    kept = []
    order = []
    for step in range(n - 1, 0, -1):
        order += [side for side in sides(w, step)]
    order.append((True, z, True))
    for _, zs, ok in order:
        w.send(part.at[zs * 2 + 1 - y], over.at[zs], by_y + zs, by_y + zs, w.over_y(), ok)
        made = pltpu.make_async_copy(part.at[zs * 2 + y], own.at[zs], w.locals.at[4 * n + zs])
        under(ok, made.start)
        kept.append(made)
    yield
    for made, (_, zs, ok) in zip(kept, order):

        def act():
            made.wait()
            w.landed(over.at[zs], by_y + zs)
            add_up(own.at[zs], own.at[zs], over.at[zs])

        under(ok, act)
    yield
    yield from chain_z(
        w, lambda zt: own.at[zt], lambda zt: below.at[zt], lambda zt: above.at[zt], out
    )


def scatter_mp(w, part, own, first, second, out):
    x, c = w.x, w.c
    core, cross = w.take(2), w.take()
    kept = []
    for i, xs in enumerate((1 - x, x)):
        w.send(part.at[xs * 2 + 1 - c], first.at[i], core + i, core + i, w.over_core())
        kept.append(w.local(part.at[xs * 2 + c], own.at[i]))
    kept[0].wait()
    w.landed(first.at[0], core)
    add_up(own.at[0], own.at[0], first.at[0])
    w.send(own.at[0], second, cross, cross, w.over_x())
    kept[1].wait()
    w.landed(first.at[1], core + 1)
    w.landed(second, cross)
    add_up(out, own.at[1], first.at[1], second)


ANY = pl.BlockSpec(memory_space=pl.ANY)
WHOLE = pl.BlockSpec(memory_space=pltpu.VMEM)


def call(kernel, identity, arrays, outs, scratch, signals, locals_, in_vmem=False, name=None):
    return pl.pallas_call(
        kernel,
        out_shape=[jax.ShapeDtypeStruct(shape, kind) for shape, kind, _ in outs],
        in_specs=[ANY] * len(arrays),
        out_specs=[WHOLE if near else ANY for _, _, near in outs],
        scratch_shapes=list(scratch)
        + [
            pltpu.SemaphoreType.DMA((signals,)),
            pltpu.SemaphoreType.DMA((signals,)),
            pltpu.SemaphoreType.DMA((max(locals_, 1),)),
        ],
        compiler_params=pltpu.CompilerParams(
            collective_id=identity, has_side_effects=True, vmem_limit_bytes=60 * MIB
        ),
        name=name,
    )(*arrays)


def halves(block):
    rows = block.shape[0]
    cut = rows // 2 // CHUNK * CHUNK
    return (block.at[pl.ds(0, cut)], block.at[pl.ds(cut, rows - cut)])


def by_x_last(block):
    return (None, block)


def rows_of(ref, index, rows):
    return ref.at[pl.ds(pl.multiple_of(index * rows, rows), rows)]


def columns_of(ref, index, columns):
    return ref.at[:, pl.ds(pl.multiple_of(index * columns, columns), columns)]


def flat(z, y, x, c):
    return (z * 2 + y) * 4 + x * 2 + c


def begin(levels, tensors):
    names = list(vars(tensors))
    count = 2 * levels
    wide = tensors.query_weight.shape[1]
    unit = tensors.gate_weight.shape[1] // count
    deep = tensors.gate_weight.shape[0] * count
    rows = tensors.layer_input.shape[0]
    packed = tensors.maps.shape
    low = tensors.gate_expand.shape[0] * count
    piece = deep // 4
    shapes = dict(
        layer_input=(4, rows, deep),
        maps=(4 * count * packed[0], packed[1]),
        output_expand=(low, deep),
        down_expand=(low, deep),
        query_weight=(deep, wide),
        output_weight=(wide, deep),
        expands=(low, tensors.expands.shape[1]),
        output_shrink=(tensors.output_shrink.shape[0] * count, low),
        output_grad=(4 * count, rows, deep),
        gate_weight=(deep, unit),
        up_weight=(deep, unit),
        down_weight=(unit, deep),
        gate_expand=(low, unit),
        up_expand=(low, unit),
    )

    def kernel(*refs):
        given = SimpleNamespace(**dict(zip(names, refs)))
        got = SimpleNamespace(**dict(zip(shapes, refs[len(names) :])))
        w = Wires(levels, *refs[len(names) + len(shapes) :])
        w.greet(far=True)

        def expand_at(into):
            def at(z, y, x, c):
                return into.at[
                    pl.ds(pl.multiple_of((z * 2 + y) * (low // count), low // count), low // count),
                    pl.ds(pl.multiple_of((x * 2 + c) * piece, piece), piece),
                ]

            return at

        steps = [
            gather_mp(w, given.layer_input, lambda x, c: got.layer_input.at[x * 2 + c]),
            gather_dp(w, given.query_weight, lambda z, y: rows_of(got.query_weight, z * 2 + y, deep // count)),
            gather_dp(w, given.output_weight, lambda z, y: columns_of(got.output_weight, z * 2 + y, deep // count)),
            gather_all(w, given.maps, lambda z, y, x, c: rows_of(got.maps, flat(z, y, x, c), packed[0]), halves),
            gather_dp(w, given.expands, lambda z, y: rows_of(got.expands, z * 2 + y, low // count)),
            gather_dp(
                w,
                given.output_shrink,
                lambda z, y: rows_of(got.output_shrink, z * 2 + y, given.output_shrink.shape[0]),
            ),
        ]
        for own, into in ((given.output_expand, got.output_expand), (given.down_expand, got.down_expand)):
            steps.append(gather_all(w, columns_of(own, w.mp, piece), expand_at(into), halves))
        steps.append(gather_all(w, given.output_grad, lambda z, y, x, c: got.output_grad.at[flat(z, y, x, c)], halves))
        after = [
            exchange_dp(w, lambda dp: columns_of(given.gate_weight, dp, unit), lambda dp: rows_of(got.gate_weight, dp, deep // count)),
            exchange_dp(w, lambda dp: columns_of(given.up_weight, dp, unit), lambda dp: rows_of(got.up_weight, dp, deep // count)),
            exchange_dp(w, lambda dp: rows_of(given.down_weight, dp, unit), lambda dp: columns_of(got.down_weight, dp, deep // count)),
            exchange_dp(w, lambda dp: columns_of(given.gate_expand, dp, unit), lambda dp: rows_of(got.gate_expand, dp, low // count)),
            exchange_dp(w, lambda dp: columns_of(given.up_expand, dp, unit), lambda dp: rows_of(got.up_expand, dp, low // count)),
        ]
        turn(steps, after)
        w.finish()

    kind = jnp.bfloat16
    given = call(
        kernel,
        0,
        list(vars(tensors).values()),
        [(shape, kind, False) for shape in shapes.values()],
        [],
        64 * levels + 48 * levels * 3,
        32,
        name="begin",
    )
    return SimpleNamespace(**dict(zip(shapes, given)))


def spread(levels, rows):
    here, wide = rows.shape

    def kernel(own, out, *sems):
        w = Wires(levels, *sems)
        w.greet()
        turn([gather_all(w, own, lambda z, y, x, c: out.at[flat(z, y, x, c)], halves)])
        w.finish()

    (out,) = call(
        kernel, 1, [rows], [((8 * levels, here, wide), rows.dtype, False)], [], 40 * levels, 4, name="spread"
    )
    return out


def collect(levels, part):
    _, here, wide = part.shape

    def kernel(given, out, *refs):
        w = Wires(levels, *refs[-3:])
        w.greet()
        turn([scatter_all(w, given, *refs[:-3], out)])
        w.finish()

    (out,) = call(
        kernel,
        2,
        [part],
        [((here, wide), jnp.float32, True)],
        scatter_all_scratch(levels, here, wide),
        40 * levels,
        4 * levels,
        name="collect",
    )
    return out


def share_mp(levels, rows):
    def kernel(own, out, *sems):
        w = Wires(levels, *sems)
        w.greet(flat=True)
        turn([gather_mp(w, own, lambda x, c: out.at[x * 2 + c])])
        w.finish()

    (out,) = call(kernel, 3, [rows], [((4,) + rows.shape, rows.dtype, False)], [], 16, 4, name="share_mp")
    return out


def sum_mp(levels, part):
    _, here, wide = part.shape

    def kernel(given, out, own, first, second, *sems):
        w = Wires(levels, *sems)
        w.greet(flat=True)
        scatter_mp(w, given, own, first, second, out)
        w.finish()

    (out,) = call(
        kernel,
        4,
        [part],
        [((here, wide), jnp.float32, True)],
        [pltpu.VMEM((2, here, wide), part.dtype)] * 2 + [pltpu.VMEM((here, wide), part.dtype)],
        16,
        4,
        name="sum_mp",
    )
    return out


def end(levels, small, split, units, share):
    names = list(vars(units))
    count = 2 * levels
    deep, unit = units.gate_weight.shape
    low = units.gate_expand.shape[0]
    shapes = dict(
        gate_weight=(deep // count, unit * count),
        up_weight=(deep // count, unit * count),
        down_weight=(unit * count, deep // count),
        gate_expand=(low // count, unit * count),
        up_expand=(low // count, unit * count),
    )
    few, wide = small.shape[1:]
    many, flatly = split.shape[1:]
    scratch = scatter_all_scratch(levels, few, wide)
    scratch += [pltpu.VMEM((levels, many, flatly), jnp.bfloat16)] * 4
    first = len(names) + 2

    def kernel(*refs):
        small_ref, split_ref = refs[:2]
        given = SimpleNamespace(**dict(zip(names, refs[2:])))
        got = SimpleNamespace(**dict(zip(shapes, refs[first:])))
        after = first + len(shapes)
        small_out, split_out, shared = refs[after : after + 3]
        buffers = refs[after + 3 : -3]
        w = Wires(levels, *refs[-3:])
        w.local_count = 5 * levels
        w.greet(far=True)

        def over_all():
            yield from scatter_all(w, small_ref, *buffers[:8], small_out)
            mine = small_out.at[:, pl.ds(wide - share, share)]
            yield from gather_mp(w, mine, lambda x, c: shared.at[x * 2 + c])

        steps = [
            scatter_dp(w, split_ref, *buffers[8:], split_out),
            over_all(),
        ]
        after = [
            exchange_dp(w, lambda dp: rows_of(given.gate_weight, dp, deep // count), lambda dp: columns_of(got.gate_weight, dp, unit)),
            exchange_dp(w, lambda dp: rows_of(given.up_weight, dp, deep // count), lambda dp: columns_of(got.up_weight, dp, unit)),
            exchange_dp(w, lambda dp: columns_of(given.down_weight, dp, deep // count), lambda dp: rows_of(got.down_weight, dp, unit)),
            exchange_dp(w, lambda dp: rows_of(given.gate_expand, dp, low // count), lambda dp: columns_of(got.gate_expand, dp, unit)),
            exchange_dp(w, lambda dp: rows_of(given.up_expand, dp, low // count), lambda dp: columns_of(got.up_expand, dp, unit)),
        ]
        turn(steps, after)
        w.finish()

    outs = [(shape, jnp.bfloat16, False) for shape in shapes.values()]
    outs += [((few, wide), jnp.float32, True), ((many, flatly), jnp.float32, True), ((4, few, share), jnp.float32, True)]
    made = call(
        kernel,
        5,
        [small, split] + list(vars(units).values()),
        outs,
        scratch,
        64 * levels + 40 * levels,
        5 * levels + 16,
        name="end",
    )
    return SimpleNamespace(**dict(zip(shapes, made))), made[-3], made[-2], made[-1]


def low(rows):
    return rows.astype(jnp.bfloat16)


def unit_rows(rows):
    scale = lax.rsqrt(jnp.mean(rows * rows, axis=-1, keepdims=True) + EPS)
    return rows * scale, scale


def norm_back(grad, normed, scale):
    return scale * (grad - normed * jnp.mean(grad * normed, axis=-1, keepdims=True))


def by_unit(
    levels,
    layer_input,
    output_grad,
    attention_gain,
    query_weight,
    key_weight,
    value_weight,
    output_weight,
    query_shrink,
    query_expand,
    key_shrink,
    key_expand,
    value_shrink,
    value_expand,
    output_shrink,
    output_expand,
    feedforward_gain,
    gate_weight,
    up_weight,
    down_weight,
    gate_shrink,
    gate_expand,
    up_shrink,
    up_expand,
    down_shrink,
    down_expand,
    group_ids,
    positions,
    segments,
):
    count = 2 * levels
    rows = layer_input.shape[0]
    tokens = 4 * rows
    deep = layer_input.shape[1]
    head = key_weight.shape[1]
    heads = query_weight.shape[1] // head
    rank = query_expand.shape[0] * count
    mp = lax.axis_index("mp")
    share = query_shrink.shape[0] // 4

    gains = jnp.stack([attention_gain, feedforward_gain], axis=1)
    gains = jnp.pad(gains, ((0, 0), (0, 126)))
    maps = jnp.concatenate(
        [key_weight, value_weight, query_shrink, key_shrink, value_shrink, gate_shrink, up_shrink, gains],
        axis=1,
    )
    maps = lax.dynamic_slice_in_dim(maps, mp * share, share, 0)
    expands = jnp.concatenate([query_expand, key_expand, value_expand], axis=1)
    got = begin(
        levels,
        SimpleNamespace(
            layer_input=layer_input,
            maps=maps,
            output_expand=output_expand,
            down_expand=down_expand,
            query_weight=query_weight,
            output_weight=output_weight,
            expands=expands,
            output_shrink=output_shrink,
            output_grad=output_grad,
            gate_weight=gate_weight,
            up_weight=up_weight,
            down_weight=down_weight,
            gate_expand=gate_expand,
            up_expand=up_expand,
        ),
    )
    maps = got.maps
    key_w, value_w = maps[:, :head], maps[:, head : 2 * head]
    query_a, key_a, value_a, gate_a, up_a = (
        maps[:, 2 * head + i * rank : 2 * head + (i + 1) * rank] for i in range(5)
    )
    gain_one = maps[:, 2 * head + 5 * rank : 2 * head + 5 * rank + 1].astype(jnp.float32)
    gain_two = maps[:, 2 * head + 5 * rank + 1 : 2 * head + 5 * rank + 2].astype(jnp.float32)
    query_b = got.expands[:, : heads * head]
    key_b = got.expands[:, heads * head : (heads + 1) * head]
    value_b = got.expands[:, (heads + 1) * head :]
    output_a, output_b = got.output_shrink, got.output_expand
    query_full = low(gain_one * (got.query_weight.astype(jnp.float32) + matmul(query_a, query_b)))
    key_full = low(gain_one * (key_w.astype(jnp.float32) + matmul(key_a, key_b)))
    value_full = low(gain_one * (value_w.astype(jnp.float32) + matmul(value_a, value_b)))
    inward = jnp.concatenate([query_full, key_full, value_full], axis=1)
    outward = low(got.output_weight.astype(jnp.float32) + matmul(output_a, output_b))

    allowed = (
        (group_ids[:, None] == group_ids[None, :])
        & (positions[None, :] <= positions[:, None])
        & ((segments[None, :] == 0) | (segments[None, :] == segments[:, None]))
    )
    group_rows = got.layer_input.reshape(tokens, deep).astype(jnp.float32)
    normed = low(unit_rows(group_rows)[0])
    lin = matmul(normed, inward)
    wide = heads * head
    queries = low(rotary(lin[:, :wide].reshape(tokens, heads, head), positions, 1.0) * head ** (-0.5))
    keys = low(rotary(lin[:, None, wide : wide + head], positions, 1.0)[:, 0, :])
    values = low(lin[:, wide + head :])
    scores = jnp.einsum("thd,sd->hts", queries, keys, preferred_element_type=jnp.float32)
    scores = jnp.where(allowed[None], scores, -1e30)
    expo = jnp.exp(scores - jnp.max(scores, axis=-1, keepdims=True))
    probability = expo / jnp.sum(expo, axis=-1, keepdims=True)
    probability_low = low(probability)
    mixed = low(
        jnp.einsum("hts,sd->thd", probability_low, values, preferred_element_type=jnp.float32)
    ).reshape(tokens, wide)
    branch = sum_mp(levels, low(matmul(mixed, outward)).reshape(4, rows, deep))
    own_rows = layer_input.astype(jnp.float32)
    middle = own_rows + branch

    gate_up = low(
        gain_two
        * (
            jnp.concatenate([got.gate_weight, got.up_weight], axis=1).astype(jnp.float32)
            + jnp.concatenate([matmul(gate_a, got.gate_expand), matmul(up_a, got.up_expand)], axis=1)
        )
    )
    unit = got.gate_weight.shape[1]
    down_a, down_b = down_shrink, got.down_expand
    down_full = low(got.down_weight.astype(jnp.float32) + matmul(down_a, down_b))
    normed_middle, scale_middle = unit_rows(middle)
    feed = spread(levels, low(normed_middle)).reshape(4 * count * rows, deep)
    grads = got.output_grad.reshape(4 * count * rows, deep)
    pre = matmul(feed, gate_up)
    hidden_wide, pull = jax.vjp(
        lambda gate, up: jax.nn.gelu(gate, approximate=True) * up, pre[:, :unit], pre[:, unit:]
    )
    hidden = low(hidden_wide)
    grad_pre = low(jnp.concatenate(pull(against(grads, down_full)), axis=1))
    blocks = (4 * count, rows, deep)
    branch = collect(levels, low(matmul(hidden, down_full)).reshape(blocks))
    grad_normed = collect(levels, low(against(grad_pre, gate_up)).reshape(blocks))
    result = low(middle + branch)
    grad_middle = output_grad.astype(jnp.float32) + norm_back(grad_normed, normed_middle, scale_middle)

    down_grad = outer_sum(hidden, grads)
    gate_up_normed = outer_sum(feed, grad_pre)
    feed_gain = jnp.sum(gate_up_normed * gate_up.astype(jnp.float32), axis=1, keepdims=True) / gain_two
    gate_up_grad = low(gate_up_normed * gain_two)
    down_grad_low = low(down_grad)
    down_shrink_grad = against(down_grad_low, down_b)
    down_b_part = outer_sum(down_a, down_grad_low)
    gate_b_grad = low(outer_sum(gate_a, gate_up_grad[:, :unit]))
    up_b_grad = low(outer_sum(up_a, gate_up_grad[:, unit:]))
    gate_a_part = against(gate_up_grad[:, :unit], got.gate_expand)
    up_a_part = against(gate_up_grad[:, unit:], got.up_expand)

    grad_branch = share_mp(levels, low(grad_middle)).reshape(tokens, deep)
    output_grad_w = outer_sum(mixed, grad_branch)
    grad_mixed = low(against(grad_branch, outward)).reshape(tokens, heads, head)
    grad_values = jnp.einsum("hts,thd->sd", probability_low, grad_mixed, preferred_element_type=jnp.float32)
    grad_probability = jnp.einsum("thd,sd->hts", grad_mixed, values, preferred_element_type=jnp.float32)
    grad_scores = low(
        probability * (grad_probability - jnp.sum(probability * grad_probability, axis=-1, keepdims=True))
    )
    grad_queries = jnp.einsum("hts,sd->thd", grad_scores, keys, preferred_element_type=jnp.float32)
    grad_keys = jnp.einsum("hts,thd->sd", grad_scores, queries, preferred_element_type=jnp.float32)
    grad_query = rotary(grad_queries * head ** (-0.5), positions, -1.0).reshape(tokens, wide)
    grad_key = rotary(grad_keys[:, None, :], positions, -1.0)[:, 0, :]
    grad_lin = low(jnp.concatenate([grad_query, grad_key, grad_values], axis=1))
    grad_rows = sum_mp(levels, low(against(grad_lin, inward)).reshape(4, rows, deep))
    normed_own, scale_own = unit_rows(own_rows)
    input_grad = grad_middle + norm_back(grad_rows, normed_own, scale_own)

    lin_normed = outer_sum(normed, grad_lin)
    attention_gain_part = jnp.sum(lin_normed * inward.astype(jnp.float32), axis=1, keepdims=True) / gain_one
    lin_grad = low(lin_normed * gain_one)
    query_part, key_part, value_part = (
        lin_grad[:, :wide],
        lin_grad[:, wide : wide + head],
        lin_grad[:, wide + head :],
    )
    query_b_part = outer_sum(query_a, query_part)
    key_b_part = outer_sum(key_a, key_part)
    value_b_part = outer_sum(value_a, value_part)
    query_a_part = against(query_part, query_b)
    output_low = low(output_grad_w)
    output_a_part = against(output_low, output_b)
    output_b_part = outer_sum(output_a, output_low)

    def by_device(array):
        return low(array).reshape(4 * count, array.shape[0] // (4 * count), array.shape[1])

    def fold(array):
        return by_device(array).reshape(4 * count, share, -1)

    def fold_wide(array):
        cut = low(array).reshape(count, array.shape[0] // count, 4, array.shape[1] // 4)
        return cut.transpose(0, 2, 1, 3).reshape(4 * count, share, -1)

    gain_part = jnp.pad(jnp.concatenate([attention_gain_part, feed_gain], axis=1), ((0, 0), (0, 62)))
    small = jnp.concatenate(
        [
            by_device(key_part),
            by_device(value_part),
            by_device(query_a_part),
            by_device(gate_a_part),
            by_device(up_a_part),
            by_device(gain_part),
            fold(key_b_part),
            fold(value_b_part),
            fold_wide(output_b_part),
            fold_wide(down_b_part),
        ],
        axis=2,
    )
    split = jnp.concatenate(
        [
            low(query_part).reshape(count, -1, wide),
            output_low.reshape(wide, count, deep // count).transpose(1, 0, 2).reshape(count, -1, wide),
            low(query_b_part).reshape(count, -1, wide),
            low(output_a_part).reshape(count, -1, wide),
        ],
        axis=1,
    )
    wide_share = 2 * (rank // count) * (deep // 4) // share
    units, few, many, shared = end(
        levels,
        small,
        split,
        SimpleNamespace(
            gate_weight=gate_up_grad[:, :unit],
            up_weight=gate_up_grad[:, unit:],
            down_weight=down_grad_low,
            gate_expand=gate_b_grad,
            up_expand=up_b_grad,
        ),
        wide_share,
    )
    key_own, value_own = few[:, :head], few[:, head : 2 * head]
    query_a_own, gate_a_own, up_a_own = (
        few[:, 2 * head + i * rank : 2 * head + (i + 1) * rank] for i in range(3)
    )
    place = 2 * head + 3 * rank
    key_b_own = few[:, place + 64 : place + 96].reshape(-1, head)
    value_b_own = few[:, place + 96 : place + 128].reshape(-1, head)
    half = wide_share // 2

    def unfold(array):
        return array.reshape(4, rank // count, deep // 4).transpose(1, 0, 2).reshape(-1, deep)

    key_a_own = against(low(key_own), key_b)
    value_a_own = against(low(value_own), value_b)
    first = query_weight.shape[0]
    second = first + output_weight.size // wide
    third = second + query_expand.shape[0]
    wider = jnp.float32
    return (
        result,
        input_grad,
        few[:, place],
        many[:first],
        key_own,
        value_own,
        many[first:second].reshape(output_weight.shape),
        query_a_own,
        many[second:third],
        key_a_own,
        key_b_own,
        value_a_own,
        value_b_own,
        many[third:].reshape(output_shrink.shape),
        unfold(shared[:, :, :half]),
        few[:, place + 1],
        units.gate_weight.astype(wider),
        units.up_weight.astype(wider),
        units.down_weight.astype(wider),
        gate_a_own,
        units.gate_expand.astype(wider),
        up_a_own,
        units.up_expand.astype(wider),
        down_shrink_grad,
        unfold(shared[:, :, half:]),
    )


def body(
    layer_input,
    output_grad,
    attention_gain,
    query_weight,
    key_weight,
    value_weight,
    output_weight,
    query_shrink,
    query_expand,
    key_shrink,
    key_expand,
    value_shrink,
    value_expand,
    output_shrink,
    output_expand,
    feedforward_gain,
    gate_weight,
    up_weight,
    down_weight,
    gate_shrink,
    gate_expand,
    up_shrink,
    up_expand,
    down_shrink,
    down_expand,
    group_ids,
    positions,
    segments,
):
    rows_local = layer_input.shape[0]
    own_start = lax.axis_index("mp") * rows_local
    allowed = (
        (group_ids[:, None] == group_ids[None, :])
        & (positions[None, :] <= positions[:, None])
        & ((segments[None, :] == 0) | (segments[None, :] == segments[:, None]))
    )

    def gather_attention():
        return (
            lax.all_gather(attention_gain, "dp", axis=0, tiled=True),
            lax.all_gather(query_weight, "dp", axis=0, tiled=True),
            lax.all_gather(key_weight, "dp", axis=0, tiled=True),
            lax.all_gather(value_weight, "dp", axis=0, tiled=True),
            lax.all_gather(output_weight, "dp", axis=1, tiled=True),
            lax.all_gather(query_shrink, "dp", axis=0, tiled=True),
            lax.all_gather(query_expand, "dp", axis=0, tiled=True),
            lax.all_gather(key_shrink, "dp", axis=0, tiled=True),
            lax.all_gather(key_expand, "dp", axis=0, tiled=True),
            lax.all_gather(value_shrink, "dp", axis=0, tiled=True),
            lax.all_gather(value_expand, "dp", axis=0, tiled=True),
            lax.all_gather(output_shrink, "dp", axis=0, tiled=True),
            lax.all_gather(output_expand, "dp", axis=0, tiled=True),
        )

    def gather_feed():
        return (
            lax.all_gather(feedforward_gain, "dp", axis=0, tiled=True),
            lax.all_gather(gate_weight, "dp", axis=0, tiled=True),
            lax.all_gather(up_weight, "dp", axis=0, tiled=True),
            lax.all_gather(down_weight, "dp", axis=1, tiled=True),
            lax.all_gather(gate_shrink, "dp", axis=0, tiled=True),
            lax.all_gather(gate_expand, "dp", axis=0, tiled=True),
            lax.all_gather(up_shrink, "dp", axis=0, tiled=True),
            lax.all_gather(up_expand, "dp", axis=0, tiled=True),
            lax.all_gather(down_shrink, "dp", axis=0, tiled=True),
            lax.all_gather(down_expand, "dp", axis=0, tiled=True),
        )

    def gather_rows(rows):
        return lax.all_gather(rows, "mp", axis=0, tiled=True)

    def gather_grads(rows):
        return lax.all_gather(rows, "mp", axis=0, tiled=True)

    def scatter_grads(term):
        return lax.psum_scatter(
            term(jnp.int32(0), lax.axis_size("mp") * rows_local),
            "mp",
            scatter_dimension=0,
            tiled=True,
        )

    def project_out(mixed, weight, shrink, expand):
        reduced = lax.psum(matmul(mixed, shrink), "mp").astype(jnp.bfloat16)

        def term(start, count):
            return matmul(mixed, weight)

        branch = lax.psum_scatter(
            term(jnp.int32(0), lax.axis_size("mp") * rows_local),
            "mp",
            scatter_dimension=0,
            tiled=True,
        )
        own = lax.dynamic_slice_in_dim(reduced, own_start, rows_local, 0)
        return (branch + matmul(own, expand), reduced)

    def masked_scores(queries, keys_rot):
        scores = jnp.einsum("thd,sd->hts", queries, keys_rot, preferred_element_type=jnp.float32)
        return jnp.where(allowed[None], scores, -1e30)

    def attention_forward(rows_in, params):
        (
            gain_one,
            w_query,
            w_key,
            w_value,
            w_output,
            query_a,
            query_b,
            key_a,
            key_b,
            value_a,
            value_b,
            output_a,
            output_b,
        ) = params
        normed = gather_rows(norm_rows(rows_in, gain_one.astype(jnp.float32)).astype(jnp.bfloat16))
        tokens = normed.shape[0]
        head_size = w_key.shape[1]
        heads = w_query.shape[1] // head_size
        query_low = matmul(normed, query_a).astype(jnp.bfloat16)
        key_low = matmul(normed, key_a).astype(jnp.bfloat16)
        value_low = matmul(normed, value_a).astype(jnp.bfloat16)
        query_lin = matmul(normed, w_query) + matmul(query_low, query_b)
        key_lin = matmul(normed, w_key) + matmul(key_low, key_b)
        value_lin = matmul(normed, w_value) + matmul(value_low, value_b)
        queries = (
            rotary(query_lin.reshape(tokens, heads, head_size), positions, 1.0)
            * head_size ** (-0.5)
        ).astype(jnp.bfloat16)
        keys_rot = rotary(key_lin[:, None, :], positions, 1.0)[:, 0, :].astype(jnp.bfloat16)
        values = value_lin.astype(jnp.bfloat16)
        scores = masked_scores(queries, keys_rot)
        highest = jnp.max(scores, axis=-1, keepdims=True)
        expo = jnp.exp(scores - highest)
        totals = jnp.sum(expo, axis=-1, keepdims=True)
        probability = expo / totals
        logsum = highest + jnp.log(totals)
        mixed = jnp.einsum(
            "hts,sd->thd",
            probability.astype(jnp.bfloat16),
            values,
            preferred_element_type=jnp.float32,
        )
        mixed = mixed.reshape(tokens, heads * head_size).astype(jnp.bfloat16)
        branch, reduced = project_out(mixed, w_output, output_a, output_b)
        saved = (
            normed,
            query_low,
            key_low,
            value_low,
            queries,
            keys_rot,
            values,
            logsum,
            mixed,
            reduced,
        )
        return (rows_in + branch, saved)

    def feed_forward(middle, params):
        gain_two, w_gate, w_up, w_down, gate_a, gate_b, up_a, up_b, down_a, down_b = params
        normed = gather_rows(norm_rows(middle, gain_two.astype(jnp.float32)).astype(jnp.bfloat16))
        gate_low = matmul(normed, gate_a).astype(jnp.bfloat16)
        up_low = matmul(normed, up_a).astype(jnp.bfloat16)
        gate_pre = matmul(normed, w_gate) + matmul(gate_low, gate_b)
        up_pre = matmul(normed, w_up) + matmul(up_low, up_b)
        hidden = (jax.nn.gelu(gate_pre, approximate=True) * up_pre).astype(jnp.bfloat16)
        branch, reduced = project_out(hidden, w_down, down_a, down_b)
        return (middle + branch, (normed, gate_low, up_low, gate_pre, up_pre, hidden, reduced))

    rows_in = layer_input.astype(jnp.float32)
    attention_params = gather_attention()
    middle, attention_saved = attention_forward(rows_in, attention_params)
    feed_params = gather_feed()
    result, feed_saved = feed_forward(middle, feed_params)
    feed_params = gather_feed()
    feed_saved = feed_forward(middle, feed_params)[1]
    gain_two, w_gate, w_up, w_down, gate_a, gate_b, up_a, up_b, down_a, down_b = feed_params
    normed_feed, gate_low, up_low, gate_pre, up_pre, hidden, reduced_feed = feed_saved
    grad_branch_feed = gather_grads(output_grad)
    down_weight_grad = outer_sum(hidden, grad_branch_feed)
    down_expand_grad = outer_sum(reduced_feed, grad_branch_feed)
    grad_reduced_feed = against(grad_branch_feed, down_b).astype(jnp.bfloat16)
    down_shrink_grad = outer_sum(hidden, grad_reduced_feed)
    grad_hidden = against(grad_branch_feed, w_down) + against(grad_reduced_feed, down_a)
    unused, gelu_pull = jax.vjp(
        lambda gated, upper: jax.nn.gelu(gated, approximate=True) * upper, gate_pre, up_pre
    )
    grad_gate, grad_up = gelu_pull(grad_hidden)
    grad_gate = grad_gate.astype(jnp.bfloat16)
    grad_up = grad_up.astype(jnp.bfloat16)
    gate_expand_grad = outer_sum(gate_low, grad_gate)
    up_expand_grad = outer_sum(up_low, grad_up)
    grad_gate_low = against(grad_gate, gate_b)
    grad_up_low = against(grad_up, up_b)
    feed_wide = normed_feed.astype(jnp.float32)
    gate_shrink_grad = outer_exact(feed_wide, grad_gate_low)
    up_shrink_grad = outer_exact(feed_wide, grad_up_low)
    gate_a_wide = gate_a.astype(jnp.float32)
    up_a_wide = up_a.astype(jnp.float32)

    def feed_term(start, count):

        def pick(rows):
            return rows

        total = against(pick(grad_gate), w_gate) + against(pick(grad_up), w_up)
        return (
            total
            + against_exact(pick(grad_gate_low), gate_a_wide)
            + against_exact(pick(grad_up_low), up_a_wide)
        )

    grad_normed_feed = scatter_grads(feed_term)
    unused, norm_pull = jax.vjp(norm_rows, middle, gain_two.astype(jnp.float32))
    grad_middle_part, feed_gain_grad = norm_pull(grad_normed_feed)
    grad_middle = output_grad.astype(jnp.float32) + grad_middle_part
    gate_weight_grad = outer_sum(normed_feed, grad_gate)
    up_weight_grad = outer_sum(normed_feed, grad_up)
    feed_split = (
        lax.psum_scatter(
            gate_weight_grad.astype(jnp.bfloat16), "dp", scatter_dimension=0, tiled=True
        ).astype(jnp.float32),
        lax.psum_scatter(
            up_weight_grad.astype(jnp.bfloat16), "dp", scatter_dimension=0, tiled=True
        ).astype(jnp.float32),
        lax.psum_scatter(
            down_weight_grad.astype(jnp.bfloat16), "dp", scatter_dimension=1, tiled=True
        ).astype(jnp.float32),
        lax.psum_scatter(
            gate_expand_grad.astype(jnp.bfloat16), "dp", scatter_dimension=0, tiled=True
        ).astype(jnp.float32),
        lax.psum_scatter(
            up_expand_grad.astype(jnp.bfloat16), "dp", scatter_dimension=0, tiled=True
        ).astype(jnp.float32),
        lax.psum_scatter(
            down_shrink_grad.astype(jnp.bfloat16), "dp", scatter_dimension=0, tiled=True
        ).astype(jnp.float32),
        lax.psum_scatter(
            down_expand_grad.astype(jnp.bfloat16), "dp", scatter_dimension=0, tiled=True
        ).astype(jnp.float32),
    )
    gate_weight_own, up_weight_own = (feed_split[0], feed_split[1])
    down_weight_own, gate_expand_own, up_expand_own, down_shrink_own, down_expand_own = (
        feed_split[2],
        feed_split[3],
        feed_split[4],
        feed_split[5],
        feed_split[6],
    )
    feed_shared = (
        lax.psum_scatter(feed_gain_grad, ("dp", "mp"), scatter_dimension=0, tiled=True),
        lax.psum_scatter(gate_shrink_grad, ("dp", "mp"), scatter_dimension=0, tiled=True),
        lax.psum_scatter(up_shrink_grad, ("dp", "mp"), scatter_dimension=0, tiled=True),
    )
    attention_params = gather_attention()
    attention_saved = attention_forward(rows_in, attention_params)[1]
    (
        gain_one,
        w_query,
        w_key,
        w_value,
        w_output,
        query_a,
        query_b,
        key_a,
        key_b,
        value_a,
        value_b,
        output_a,
        output_b,
    ) = attention_params
    normed, query_low, key_low, value_low, queries, keys_rot, values, logsum, mixed, reduced = (
        attention_saved
    )
    tokens = normed.shape[0]
    head_size = w_key.shape[1]
    heads = w_query.shape[1] // head_size
    grad_branch = gather_grads(grad_middle.astype(jnp.bfloat16))
    output_weight_grad = outer_sum(mixed, grad_branch)
    output_expand_grad = outer_sum(reduced, grad_branch)
    grad_reduced = against(grad_branch, output_b).astype(jnp.bfloat16)
    output_shrink_grad = outer_sum(mixed, grad_reduced)
    grad_mixed = (against(grad_branch, w_output) + against(grad_reduced, output_a)).astype(
        jnp.bfloat16
    )
    grad_mixed = grad_mixed.reshape(tokens, heads, head_size)
    probability = jnp.exp(masked_scores(queries, keys_rot) - logsum)
    grad_values = jnp.einsum(
        "hts,thd->sd",
        probability.astype(jnp.bfloat16),
        grad_mixed,
        preferred_element_type=jnp.float32,
    )
    grad_probability = jnp.einsum(
        "thd,sd->hts", grad_mixed, values, preferred_element_type=jnp.float32
    )
    grad_scores = probability * (
        grad_probability - jnp.sum(probability * grad_probability, axis=-1, keepdims=True)
    )
    grad_scores = grad_scores.astype(jnp.bfloat16)
    grad_queries_rot = jnp.einsum(
        "hts,sd->thd", grad_scores, keys_rot, preferred_element_type=jnp.float32
    )
    grad_keys_rot = jnp.einsum(
        "hts,thd->sd", grad_scores, queries, preferred_element_type=jnp.float32
    )
    grad_query = (
        rotary(grad_queries_rot * head_size ** (-0.5), positions, -1.0)
        .reshape(tokens, heads * head_size)
        .astype(jnp.bfloat16)
    )
    grad_key = rotary(grad_keys_rot[:, None, :], positions, -1.0)[:, 0, :]
    normed_wide = normed.astype(jnp.float32)
    query_weight_grad = outer_sum(normed, grad_query)
    query_expand_grad = outer_sum(query_low, grad_query)
    grad_query_low = against(grad_query, query_b)
    query_shrink_grad = outer_exact(normed_wide, grad_query_low)
    key_weight_grad = outer_exact(normed_wide, grad_key)
    key_expand_grad = outer_exact(key_low.astype(jnp.float32), grad_key)
    grad_key_low = against_exact(grad_key, key_b.astype(jnp.float32))
    key_shrink_grad = outer_exact(normed_wide, grad_key_low)
    value_weight_grad = outer_exact(normed_wide, grad_values)
    value_expand_grad = outer_exact(value_low.astype(jnp.float32), grad_values)
    grad_value_low = against_exact(grad_values, value_b.astype(jnp.float32))
    value_shrink_grad = outer_exact(normed_wide, grad_value_low)
    query_a_wide = query_a.astype(jnp.float32)
    key_wide = w_key.astype(jnp.float32)
    key_a_wide = key_a.astype(jnp.float32)
    value_wide = w_value.astype(jnp.float32)
    value_a_wide = value_a.astype(jnp.float32)

    def attention_term(start, count):

        def pick(rows):
            return rows

        total = against(pick(grad_query), w_query) + against_exact(
            pick(grad_query_low), query_a_wide
        )
        total = (
            total
            + against_exact(pick(grad_key), key_wide)
            + against_exact(pick(grad_key_low), key_a_wide)
        )
        return (
            total
            + against_exact(pick(grad_values), value_wide)
            + against_exact(pick(grad_value_low), value_a_wide)
        )

    grad_normed = scatter_grads(attention_term)
    unused, norm_pull_one = jax.vjp(norm_rows, rows_in, gain_one.astype(jnp.float32))
    grad_input_part, attention_gain_grad = norm_pull_one(grad_normed)
    input_grad = grad_middle + grad_input_part
    attention_split = (
        lax.psum_scatter(
            query_weight_grad.astype(jnp.bfloat16), "dp", scatter_dimension=0, tiled=True
        ).astype(jnp.float32),
        lax.psum_scatter(
            output_weight_grad.astype(jnp.bfloat16), "dp", scatter_dimension=1, tiled=True
        ).astype(jnp.float32),
        lax.psum_scatter(
            query_expand_grad.astype(jnp.bfloat16), "dp", scatter_dimension=0, tiled=True
        ).astype(jnp.float32),
        lax.psum_scatter(
            output_shrink_grad.astype(jnp.bfloat16), "dp", scatter_dimension=0, tiled=True
        ).astype(jnp.float32),
        lax.psum_scatter(
            output_expand_grad.astype(jnp.bfloat16), "dp", scatter_dimension=0, tiled=True
        ).astype(jnp.float32),
    )
    attention_shared = (
        lax.psum_scatter(attention_gain_grad, ("dp", "mp"), scatter_dimension=0, tiled=True),
        lax.psum_scatter(key_weight_grad, ("dp", "mp"), scatter_dimension=0, tiled=True),
        lax.psum_scatter(value_weight_grad, ("dp", "mp"), scatter_dimension=0, tiled=True),
        lax.psum_scatter(query_shrink_grad, ("dp", "mp"), scatter_dimension=0, tiled=True),
        lax.psum_scatter(key_shrink_grad, ("dp", "mp"), scatter_dimension=0, tiled=True),
        lax.psum_scatter(key_expand_grad, ("dp", "mp"), scatter_dimension=0, tiled=True),
        lax.psum_scatter(value_shrink_grad, ("dp", "mp"), scatter_dimension=0, tiled=True),
        lax.psum_scatter(value_expand_grad, ("dp", "mp"), scatter_dimension=0, tiled=True),
    )
    return (
        result.astype(jnp.bfloat16),
        input_grad,
        attention_shared[0],
        attention_split[0],
        attention_shared[1],
        attention_shared[2],
        attention_split[1],
        attention_shared[3],
        attention_split[2],
        attention_shared[4],
        attention_shared[5],
        attention_shared[6],
        attention_shared[7],
        attention_split[3],
        attention_split[4],
        feed_shared[0],
        gate_weight_own,
        up_weight_own,
        down_weight_own,
        feed_shared[1],
        gate_expand_own,
        feed_shared[2],
        up_expand_own,
        down_shrink_own,
        down_expand_own,
    )


def solution(mesh):
    levels = mesh.shape["dp"] // 2
    few = mesh.shape["mp"] == 4 and mesh.shape["dp"] % 2 == 0 and levels <= 4
    step = functools.partial(by_unit, levels) if few else body
    placed = (
        P(("dp", "mp"), None),
        P(("dp", "mp"), None),
        P("dp"),
        P("dp", "mp"),
        P("dp", None),
        P("dp", None),
        P("mp", "dp"),
        P("dp", None),
        P("dp", "mp"),
        P("dp", None),
        P("dp", None),
        P("dp", None),
        P("dp", None),
        P(("mp", "dp"), None),
        P("dp", None),
        P("dp"),
        P("dp", "mp"),
        P("dp", "mp"),
        P("mp", "dp"),
        P("dp", None),
        P("dp", "mp"),
        P("dp", None),
        P("dp", "mp"),
        P(("mp", "dp"), None),
        P("dp", None),
        P("dp"),
        P("dp"),
        P("dp"),
    )
    return jax.shard_map(
        step,
        mesh=mesh,
        in_specs=placed,
        out_specs=(
            P(("dp", "mp"), None),
            P(("dp", "mp"), None),
            P(("dp", "mp")),
            P("dp", "mp"),
            P(("dp", "mp"), None),
            P(("dp", "mp"), None),
            P("mp", "dp"),
            P(("dp", "mp"), None),
            P("dp", "mp"),
            P(("dp", "mp"), None),
            P(("dp", "mp"), None),
            P(("dp", "mp"), None),
            P(("dp", "mp"), None),
            P(("mp", "dp"), None),
            P("dp", None),
            P(("dp", "mp")),
            P("dp", "mp"),
            P("dp", "mp"),
            P("mp", "dp"),
            P(("dp", "mp"), None),
            P("dp", "mp"),
            P(("dp", "mp"), None),
            P("dp", "mp"),
            P(("mp", "dp"), None),
            P("dp", None),
        ),
        check_vma=False,
    )
```

```python
import functools
from types import SimpleNamespace

import jax
import jax.numpy as jnp
from jax import lax
from jax.experimental import pallas as pl
from jax.experimental.pallas import tpu as pltpu
from jax.sharding import PartitionSpec as P

MESH = pl.DeviceIdType.MESH
MIB = 1 << 20

EPS = 1e-06


def matmul(left, right):
    return jnp.dot(left, right, preferred_element_type=jnp.float32)


def against(left, right):
    return lax.dot_general(
        left, right, (((1,), (1,)), ((), ())), preferred_element_type=jnp.float32
    )


def outer_sum(left, right):
    return lax.dot_general(
        left, right, (((0,), (0,)), ((), ())), preferred_element_type=jnp.float32
    )


def against_exact(left, right):
    return lax.dot_general(
        left,
        right,
        (((1,), (1,)), ((), ())),
        precision=lax.Precision.HIGHEST,
        preferred_element_type=jnp.float32,
    )


def outer_exact(left, right):
    return lax.dot_general(
        left,
        right,
        (((0,), (0,)), ((), ())),
        precision=lax.Precision.HIGHEST,
        preferred_element_type=jnp.float32,
    )


def norm_rows(rows, gain):
    return rows * lax.rsqrt(jnp.mean(rows * rows, axis=-1, keepdims=True) + EPS) * gain


def rotary(entries, places, sign):
    half = entries.shape[-1] // 2
    freq = 10000.0 ** (-jnp.arange(half).astype(jnp.float32) * 2.0 / entries.shape[-1])
    angle = places.astype(jnp.float32)[:, None] * freq[None, :]
    cosine = jnp.cos(angle)[:, None, :]
    sine = sign * jnp.sin(angle)[:, None, :]
    first = entries[..., :half]
    second = entries[..., half:]
    return jnp.concatenate(
        [first * cosine - second * sine, second * cosine + first * sine], axis=-1
    )


class Wires:
    def __init__(self, levels, sends, lands, locals_=None):
        self.sends, self.lands, self.locals = sends, lands, locals_
        self.levels = levels
        self.count = self.local_count = 0
        self.open = []
        dp, mp = lax.axis_index("dp"), lax.axis_index("mp")
        self.dp, self.mp = dp, mp
        self.z, self.y, self.x, self.c = dp // 2, dp % 2, mp // 2, mp % 2

    def take(self, number=1):
        first = self.count
        self.count += number
        assert self.count <= self.sends.shape[0], self.count
        return first

    def at(self, z, y, x, c):
        return (z * 2 + y, x * 2 + c)

    def up(self):
        return self.at(self.z + 1, self.y, self.x, self.c)

    def down(self):
        return self.at(self.z - 1, self.y, self.x, self.c)

    def over_x(self):
        return self.at(self.z, self.y, 1 - self.x, self.c)

    def over_y(self):
        return self.at(self.z, 1 - self.y, self.x, self.c)

    def over_core(self):
        return self.at(self.z, self.y, self.x, 1 - self.c)

    def copy(self, source, target, out, land, device):
        return pltpu.make_async_remote_copy(
            src_ref=source,
            dst_ref=target,
            send_sem=self.sends.at[out],
            recv_sem=self.lands.at[land],
            device_id=device,
            device_id_type=MESH,
        )

    def send(self, source, target, out, land, device, when=True):
        made = self.copy(source, target, out, land, device)
        under(when, made.start)
        self.open.append((when, made.wait_send))

    def landed(self, target, land):
        self.copy(target, target, land, land, self.over_x()).wait_recv()

    def local(self, source, target):
        made = pltpu.make_async_copy(source, target, self.locals.at[self.local_count])
        self.local_count += 1
        assert self.local_count <= self.locals.shape[0], self.local_count
        made.start()
        return made

    def take_local(self, number):
        first = self.local_count
        self.local_count += number
        assert self.local_count <= self.locals.shape[0], self.local_count
        return first

    def finish(self):
        for when, wait in self.open:
            under(when, wait)

    def greet(self, far=False, flat=False):
        barrier = pltpu.get_barrier_semaphore()

        def call(device):
            pl.semaphore_signal(barrier, inc=1, device_id=device, device_id_type=MESH)

        call(self.over_x())
        call(self.over_core())
        if far:
            call(self.at(self.z, self.y, 1 - self.x, 1 - self.c))
            for step in range(1, 2 * self.levels):
                call((lax.rem(self.dp + step, 2 * self.levels), self.mp))
            pl.semaphore_wait(barrier, 2 + 2 * self.levels)
            return
        if flat:
            pl.semaphore_wait(barrier, 2)
            return
        call(self.over_y())
        pl.when(self.z > 0)(lambda: call(self.down()))
        pl.when(self.z < self.levels - 1)(lambda: call(self.up()))
        ends = jnp.where(self.z > 0, 1, 0) + jnp.where(self.z < self.levels - 1, 1, 0)
        pl.semaphore_wait(barrier, 3 + ends)


def under(when, act):
    if when is True:
        act()
    else:
        pl.when(when)(act)


def sides(w, step):
    yield (True, w.z - step, w.z >= step)
    yield (False, w.z + step, w.z < w.levels - step)


def gather_all(w, own, at, parts):
    z, y, x, c = w.z, w.y, w.x, w.c
    n = w.levels
    rise, fall, by_x, by_y, last_x, last_y = (w.take(n) for _ in range(6))
    by_core = w.take(4 * n)

    def core(block, zs, ys, xs):
        place = by_core + zs * 4 + ys * 2 + xs
        return (block, block, place, place, w.over_core())

    here = at(z, y, x, c)
    kept = w.local(own, here)
    w.send(own, here, rise + z, rise + z, w.up(), z < n - 1)
    w.send(own, here, fall + z, fall + z, w.down(), z > 0)
    w.send(own, here, by_x + z, by_x + z, w.over_x())
    w.send(own, here, by_y + z, by_y + z, w.over_y())
    place = by_core + z * 4 + y * 2 + x
    w.send(own, here, place, place, w.over_core())
    yield

    def plane(zs, ok):
        block = at(zs, y, 1 - x, c)
        under(ok, lambda: w.landed(block, by_x + zs))
        for piece in parts(block)[:1]:
            if piece is not None:
                w.send(piece, piece, last_y + zs, last_y + zs, w.over_y(), ok)
        w.send(*core(block, zs, y, 1 - x), ok)
        block = at(zs, 1 - y, x, c)
        under(ok, lambda: w.landed(block, by_y + zs))
        for piece in parts(block)[1:]:
            if piece is not None:
                w.send(piece, piece, last_x + zs, last_x + zs, w.over_x(), ok)
        w.send(*core(block, zs, 1 - y, x), ok)

    plane(z, True)
    yield
    for step in range(1, n):
        for rising, zs, ok in sides(w, step):
            block = at(zs, y, x, c)
            lane = rise if rising else fall
            under(ok, lambda: w.landed(block, lane + zs))
            if rising:
                w.send(block, block, rise + zs, rise + zs, w.up(), jnp.logical_and(ok, z < n - 1))
            else:
                w.send(block, block, fall + zs, fall + zs, w.down(), jnp.logical_and(ok, z > 0))
            w.send(block, block, by_x + zs, by_x + zs, w.over_x(), ok)
            w.send(block, block, by_y + zs, by_y + zs, w.over_y(), ok)
            w.send(*core(block, zs, y, x), ok)
        yield
        for _, zs, ok in sides(w, step):
            plane(zs, ok)
        yield
    for step in range(n):
        for _, zs, ok in sides(w, step) if step else [(True, z, True)]:
            block = at(zs, 1 - y, 1 - x, c)
            for piece, lane in zip(parts(block), (last_y, last_x)):
                if piece is not None:
                    under(ok, lambda: w.landed(piece, lane + zs))
            w.send(*core(block, zs, 1 - y, 1 - x), ok)
        yield
    for zs in range(n):
        for ys in range(2):
            for xs in range(2):
                w.landed(at(zs, ys, xs, 1 - c), by_core + zs * 4 + ys * 2 + xs)
    kept.wait()


def gather_dp(w, own, at):
    z, y, n = w.z, w.y, w.levels
    rise, fall, by_y = (w.take(n) for _ in range(3))
    here = at(z, y)
    kept = w.local(own, here)
    w.send(own, here, rise + z, rise + z, w.up(), z < n - 1)
    w.send(own, here, fall + z, fall + z, w.down(), z > 0)
    w.send(own, here, by_y + z, by_y + z, w.over_y())
    yield
    yield
    for step in range(1, n):
        for rising, zs, ok in sides(w, step):
            block = at(zs, y)
            lane = rise if rising else fall
            under(ok, lambda: w.landed(block, lane + zs))
            if rising:
                w.send(block, block, rise + zs, rise + zs, w.up(), jnp.logical_and(ok, z < n - 1))
            else:
                w.send(block, block, fall + zs, fall + zs, w.down(), jnp.logical_and(ok, z > 0))
            w.send(block, block, by_y + zs, by_y + zs, w.over_y(), ok)
        yield
        yield
    for zs in range(n):
        w.landed(at(zs, 1 - y), by_y + zs)
    kept.wait()


def gather_mp(w, own, at):
    x, c = w.x, w.c
    first, second = w.take(), w.take(2)
    here = at(x, c)
    kept = w.local(own, here)
    w.send(own, here, first, first, w.over_x())
    w.send(own, here, second, second, w.over_core())
    yield
    block = at(1 - x, c)
    w.landed(block, first)
    w.send(block, block, second + 1, second + 1, w.over_core())
    yield
    w.landed(at(x, 1 - c), second)
    w.landed(at(1 - x, 1 - c), second + 1)
    kept.wait()


def exchange_dp(w, source, target):
    count = 2 * w.levels
    first = w.take(count)
    kept = w.local(source(w.dp), target(w.dp))
    for step in range(1, count):
        there = lax.rem(w.dp + step, count)
        w.send(source(there), target(w.dp), first + step, first + step, (there, w.mp))
        yield
    for step in range(1, count):
        w.landed(target(lax.rem(w.dp + count - step, count)), first + step)
    kept.wait()


PACE = 4


def turn(steps, after=(), pace=PACE):
    spare = [one for one in after for _ in range(7)]
    turn_on(steps, spare, pace)
    for one in spare:
        next(one)
    turn_on(after)


def turn_on(steps, spare=(), pace=0):
    steps = list(steps)
    while steps:
        for _ in range(min(pace, len(spare))):
            next(spare.pop(0))
        left = []
        for one in steps:
            try:
                next(one)
                left.append(one)
            except StopIteration:
                pass
        steps = left


CHUNK = 16


def add_up(target, *sources):
    rows = target.shape[0]

    def one(i, unused):
        part = pl.ds(pl.multiple_of(i * CHUNK, CHUNK), CHUNK)
        total = sources[0][part, :].astype(jnp.float32)
        for source in sources[1:]:
            total = total + source[part, :].astype(jnp.float32)
        target[part, :] = total.astype(target.dtype)
        return unused

    lax.fori_loop(0, rows // CHUNK, one, 0)


def chain_z(w, own, below, above, out):
    z, n = w.z, w.levels
    rise, fall = w.take(n), w.take(n)
    for step in range(n - 1, 0, -1):
        for rising, zt, ok in ((True, z + step, z < n - step), (False, z - step, z >= step)):
            lane = rise if rising else fall
            slot = below(zt) if rising else above(zt)
            inner = jnp.logical_and(ok, (z > 0) if rising else (z < n - 1))

            def take_in():
                w.landed(slot, lane + zt)
                add_up(own(zt), own(zt), slot)

            under(inner, take_in)
            w.send(own(zt), slot, lane + zt, lane + zt, w.up() if rising else w.down(), ok)
        yield
    under(z > 0, lambda: w.landed(below(z), rise + z))
    under(z < n - 1, lambda: w.landed(above(z), fall + z))
    under(z == 0, lambda: add_up(out, own(z), above(z)))
    under(z == n - 1, lambda: add_up(out, own(z), below(z)))
    under(
        jnp.logical_and(z > 0, z < n - 1), lambda: add_up(out, own(z), below(z), above(z))
    )


def planes(w):
    z, n = w.z, w.levels
    for k in range(n - 1):
        falling = n - 1 - k
        low_half = jnp.where(falling > z, falling, falling - 1)
        high_half = jnp.where(k < z, k, k + 1)
        yield jnp.where(z < n // 2, low_half, high_half)
    yield z


def scatter_all(w, part, landing, own, core, half_x, half_y, full_x, full_y, below, above, out, make=None):
    z, y, x, c, n = w.z, w.y, w.x, w.c, w.levels
    to_core, to_hx, to_hy, to_fx, to_fy = (w.take(4 * n), w.take(n), w.take(n), w.take(n), w.take(n))
    rise, fall = w.take(n), w.take(n)
    from_part, from_landing = w.take_local(4 * n), w.take_local(4 * n)
    rows = own.shape[1]
    cut = rows // 2 // CHUNK * CHUNK
    first, second = pl.ds(0, cut), pl.ds(cut, rows - cut)
    kinds = ((1 - y, 1 - x), (1 - y, x), (y, 1 - x), (y, x))
    order = list(planes(w))
    kept = {}

    def start(k):
        zs = order[k]
        for kind, (ys, xs) in enumerate(kinds):
            here = k * 4 + kind
            lane = to_core + here
            w.send(part.at[flat(zs, ys, xs, 1 - c)], landing.at[here], lane, lane, w.over_core())
            kept[here] = pltpu.make_async_copy(
                part.at[flat(zs, ys, xs, c)], own.at[here], w.locals.at[from_part + here]
            )
            kept[here].start()

    def join(k):
        loads = []
        for kind in range(4):
            here = k * 4 + kind
            w.landed(landing.at[here], to_core + here)
            load = pltpu.make_async_copy(landing.at[here], core.at[kind], w.locals.at[from_landing + here])
            load.start()
            loads.append(load)
        for kind in range(4):
            here = k * 4 + kind
            kept[here].wait()
            loads[kind].wait()
            add_up(own.at[here], own.at[here], core.at[kind])
            if kind == 0:
                w.send(own.at[here, first], half_x.at[k], to_hx + k, to_hx + k, w.over_x())
                w.send(own.at[here, second], half_y.at[k], to_hy + k, to_hy + k, w.over_y())

    def across(k):
        here = k * 4 + 1
        w.landed(half_x.at[k], to_hx + k)
        add_up(own.at[here, first], own.at[here, first], half_x.at[k])
        w.send(own.at[here], full_y.at[k], to_fy + k, to_fy + k, w.over_y())
        here = k * 4 + 2
        w.landed(half_y.at[k], to_hy + k)
        add_up(own.at[here, second], own.at[here, second], half_y.at[k])
        w.send(own.at[here], full_x.at[k], to_fx + k, to_fx + k, w.over_x())

    def along(k):
        zs, here = order[k], own.at[k * 4 + 3]
        w.landed(full_x.at[k], to_fx + k)
        w.landed(full_y.at[k], to_fy + k)
        if k == n - 1:
            add_up(here, here, full_x.at[k], full_y.at[k])
            return
        rising, falling = zs > z, zs < z
        more_up, more_down = jnp.logical_and(rising, z > 0), jnp.logical_and(falling, z < n - 1)

        def take_below():
            w.landed(below.at[zs], rise + zs)
            add_up(here, here, full_x.at[k], full_y.at[k], below.at[zs])

        def take_above():
            w.landed(above.at[zs], fall + zs)
            add_up(here, here, full_x.at[k], full_y.at[k], above.at[zs])

        under(more_up, take_below)
        under(more_down, take_above)
        under(
            jnp.logical_not(jnp.logical_or(more_up, more_down)),
            lambda: add_up(here, here, full_x.at[k], full_y.at[k]),
        )
        w.send(here, below.at[zs], rise + zs, rise + zs, w.up(), rising)
        w.send(here, above.at[zs], fall + zs, fall + zs, w.down(), falling)

    for k in range(n + 3):
        if k < n:
            if make is not None:
                yield from make(k, order[k])
            start(k)
            yield
        for lag, act in ((1, join), (2, across), (3, along)):
            if 0 <= k - lag < n:
                act(k - lag)
                yield
    here = own.at[4 * n - 1]
    under(z > 0, lambda: w.landed(below.at[z], rise + z))
    under(z < n - 1, lambda: w.landed(above.at[z], fall + z))
    under(z == 0, lambda: add_up(out, here, above.at[z]))
    under(z == n - 1, lambda: add_up(out, here, below.at[z]))
    under(jnp.logical_and(z > 0, z < n - 1), lambda: add_up(out, here, below.at[z], above.at[z]))


def scatter_all_scratch(n, rows, columns):
    cut = rows // 2 // CHUNK * CHUNK
    shapes = [(4 * n, rows), (4, rows), (n, cut), (n, rows - cut)] + [(n, rows)] * 4
    return [pltpu.VMEM(shape + (columns,), jnp.bfloat16) for shape in shapes]


def scatter_dp(w, part, own, over, below, above, out):
    z, y, n = w.z, w.y, w.levels
    by_y, spare = w.take(n), w.take_local(n)
    kept = []
    order = []
    for step in range(n - 1, 0, -1):
        order += [side for side in sides(w, step)]
    order.append((True, z, True))
    for _, zs, ok in order:
        w.send(part.at[zs * 2 + 1 - y], over.at[zs], by_y + zs, by_y + zs, w.over_y(), ok)
        made = pltpu.make_async_copy(part.at[zs * 2 + y], own.at[zs], w.locals.at[spare + zs])
        under(ok, made.start)
        kept.append(made)
    yield
    for made, (_, zs, ok) in zip(kept, order):

        def act():
            made.wait()
            w.landed(over.at[zs], by_y + zs)
            add_up(own.at[zs], own.at[zs], over.at[zs])

        under(ok, act)
    yield
    yield from chain_z(
        w, lambda zt: own.at[zt], lambda zt: below.at[zt], lambda zt: above.at[zt], out
    )


def scatter_mp(w, part, own, first, second, out):
    x, c = w.x, w.c
    core, cross = w.take(2), w.take()
    kept = []
    for i, xs in enumerate((1 - x, x)):
        w.send(part.at[xs * 2 + 1 - c], first.at[i], core + i, core + i, w.over_core())
        kept.append(w.local(part.at[xs * 2 + c], own.at[i]))
    kept[0].wait()
    w.landed(first.at[0], core)
    add_up(own.at[0], own.at[0], first.at[0])
    w.send(own.at[0], second, cross, cross, w.over_x())
    kept[1].wait()
    w.landed(first.at[1], core + 1)
    w.landed(second, cross)
    add_up(out, own.at[1], first.at[1], second)


ANY = pl.BlockSpec(memory_space=pl.ANY)
WHOLE = pl.BlockSpec(memory_space=pltpu.VMEM)


def call(kernel, identity, arrays, outs, scratch, signals, locals_, in_vmem=False, name=None):
    return pl.pallas_call(
        kernel,
        out_shape=[jax.ShapeDtypeStruct(shape, kind) for shape, kind, _ in outs],
        in_specs=[ANY] * len(arrays),
        out_specs=[WHOLE if near else ANY for _, _, near in outs],
        scratch_shapes=list(scratch)
        + [
            pltpu.SemaphoreType.DMA((signals,)),
            pltpu.SemaphoreType.DMA((signals,)),
            pltpu.SemaphoreType.DMA((max(locals_, 1),)),
        ],
        compiler_params=pltpu.CompilerParams(
            collective_id=identity, has_side_effects=True, vmem_limit_bytes=60 * MIB
        ),
        name=name,
    )(*arrays)


def halves(block):
    rows = block.shape[0]
    cut = rows // 2 // CHUNK * CHUNK
    return (block.at[pl.ds(0, cut)], block.at[pl.ds(cut, rows - cut)])


def by_x_last(block):
    return (None, block)


def rows_of(ref, index, rows):
    return ref.at[pl.ds(pl.multiple_of(index * rows, rows), rows)]


def columns_of(ref, index, columns):
    return ref.at[:, pl.ds(pl.multiple_of(index * columns, columns), columns)]


def flat(z, y, x, c):
    return (z * 2 + y) * 4 + x * 2 + c


def begin(levels, tensors):
    names = list(vars(tensors))
    count = 2 * levels
    wide = tensors.query_weight.shape[1]
    unit = tensors.gate_weight.shape[1] // count
    deep = tensors.gate_weight.shape[0] * count
    rows = tensors.layer_input.shape[0]
    packed = tensors.maps.shape
    low = tensors.gate_expand.shape[0] * count
    piece = deep // 4
    shapes = dict(
        layer_input=(4, rows, deep),
        maps=(4 * count * packed[0], packed[1]),
        output_expand=(low, deep),
        down_expand=(low, deep),
        query_weight=(deep, wide),
        output_weight=(wide, deep),
        expands=(low, tensors.expands.shape[1]),
        output_shrink=(tensors.output_shrink.shape[0] * count, low),
        output_grad=(4 * count, rows, deep),
        gate_weight=(deep, unit),
        up_weight=(deep, unit),
        down_weight=(unit, deep),
        gate_expand=(low, unit),
        up_expand=(low, unit),
    )

    def kernel(*refs):
        given = SimpleNamespace(**dict(zip(names, refs)))
        got = SimpleNamespace(**dict(zip(shapes, refs[len(names) :])))
        w = Wires(levels, *refs[len(names) + len(shapes) :])
        w.greet(far=True)

        def expand_at(into):
            def at(z, y, x, c):
                return into.at[
                    pl.ds(pl.multiple_of((z * 2 + y) * (low // count), low // count), low // count),
                    pl.ds(pl.multiple_of((x * 2 + c) * piece, piece), piece),
                ]

            return at

        steps = [
            gather_mp(w, given.layer_input, lambda x, c: got.layer_input.at[x * 2 + c]),
            gather_dp(w, given.query_weight, lambda z, y: rows_of(got.query_weight, z * 2 + y, deep // count)),
            gather_dp(w, given.output_weight, lambda z, y: columns_of(got.output_weight, z * 2 + y, deep // count)),
            gather_all(w, given.maps, lambda z, y, x, c: rows_of(got.maps, flat(z, y, x, c), packed[0]), halves),
            gather_dp(w, given.expands, lambda z, y: rows_of(got.expands, z * 2 + y, low // count)),
            gather_dp(
                w,
                given.output_shrink,
                lambda z, y: rows_of(got.output_shrink, z * 2 + y, given.output_shrink.shape[0]),
            ),
        ]
        for own, into in ((given.output_expand, got.output_expand), (given.down_expand, got.down_expand)):
            steps.append(gather_all(w, columns_of(own, w.mp, piece), expand_at(into), halves))
        steps.append(gather_all(w, given.output_grad, lambda z, y, x, c: got.output_grad.at[flat(z, y, x, c)], halves))
        after = [
            exchange_dp(w, lambda dp: columns_of(given.gate_weight, dp, unit), lambda dp: rows_of(got.gate_weight, dp, deep // count)),
            exchange_dp(w, lambda dp: columns_of(given.up_weight, dp, unit), lambda dp: rows_of(got.up_weight, dp, deep // count)),
            exchange_dp(w, lambda dp: rows_of(given.down_weight, dp, unit), lambda dp: columns_of(got.down_weight, dp, deep // count)),
            exchange_dp(w, lambda dp: columns_of(given.gate_expand, dp, unit), lambda dp: rows_of(got.gate_expand, dp, low // count)),
            exchange_dp(w, lambda dp: columns_of(given.up_expand, dp, unit), lambda dp: rows_of(got.up_expand, dp, low // count)),
        ]
        turn(steps, after)
        w.finish()

    kind = jnp.bfloat16
    given = call(
        kernel,
        0,
        list(vars(tensors).values()),
        [(shape, kind, False) for shape in shapes.values()],
        [],
        64 * levels + 48 * levels * 3,
        32,
        name="begin",
    )
    return SimpleNamespace(**dict(zip(shapes, given)))


def spread(levels, rows):
    here, wide = rows.shape

    def kernel(own, out, *sems):
        w = Wires(levels, *sems)
        w.greet()
        turn([gather_all(w, own, lambda z, y, x, c: out.at[flat(z, y, x, c)], halves)])
        w.finish()

    (out,) = call(
        kernel, 1, [rows], [((8 * levels, here, wide), rows.dtype, False)], [], 40 * levels, 4, name="spread"
    )
    return out


def collect(levels, urgent, other, units):
    _, here, wide = urgent.shape
    names = list(vars(units))
    count = 2 * levels
    deep, unit = units.gate_weight.shape
    low = units.gate_expand.shape[0]
    shapes = dict(
        gate_weight=(deep // count, unit * count),
        up_weight=(deep // count, unit * count),
        down_weight=(unit * count, deep // count),
        gate_expand=(low // count, unit * count),
        up_expand=(low // count, unit * count),
    )
    scratch = scatter_all_scratch(levels, here, wide)
    each = len(scratch)

    def kernel(urgent_ref, other_ref, *refs):
        given = SimpleNamespace(**dict(zip(names, refs)))
        refs = refs[len(names) :]
        got = SimpleNamespace(**dict(zip(shapes, refs)))
        urgent_out, other_out, urgent_land, other_land = refs[len(names) : len(names) + 4]
        buffers = refs[len(names) + 4 :]
        w = Wires(levels, *buffers[-3:])
        w.greet(far=True)

        def later():
            for _ in range(LAG):
                yield
            yield from scatter_all(w, other_ref, other_land, *buffers[each : 2 * each], other_out)

        after = [
            exchange_dp(w, lambda dp: rows_of(given.gate_weight, dp, deep // count), lambda dp: columns_of(got.gate_weight, dp, unit)),
            exchange_dp(w, lambda dp: rows_of(given.up_weight, dp, deep // count), lambda dp: columns_of(got.up_weight, dp, unit)),
            exchange_dp(w, lambda dp: columns_of(given.down_weight, dp, deep // count), lambda dp: rows_of(got.down_weight, dp, unit)),
            exchange_dp(w, lambda dp: rows_of(given.gate_expand, dp, low // count), lambda dp: columns_of(got.gate_expand, dp, unit)),
            exchange_dp(w, lambda dp: rows_of(given.up_expand, dp, low // count), lambda dp: columns_of(got.up_expand, dp, unit)),
        ]
        turn([scatter_all(w, urgent_ref, urgent_land, *buffers[:each], urgent_out), later()], after, BACK)
        w.finish()

    outs = [(shape, jnp.bfloat16, False) for shape in shapes.values()]
    outs += [((here, wide), jnp.float32, True)] * 2 + [((4 * levels, here, wide), jnp.bfloat16, False)] * 2
    made = call(
        kernel,
        2,
        [urgent, other] + list(vars(units).values()),
        outs,
        scratch * 2,
        2 * 10 * levels + 5 * 2 * levels + 4,
        16 * levels + 8,
        name="collect",
    )
    return made[5], made[6], SimpleNamespace(**dict(zip(shapes, made)))


LAG, BACK = 3, 2


def share_mp(levels, rows):
    def kernel(own, out, *sems):
        w = Wires(levels, *sems)
        w.greet(flat=True)
        turn([gather_mp(w, own, lambda x, c: out.at[x * 2 + c])])
        w.finish()

    (out,) = call(kernel, 3, [rows], [((4,) + rows.shape, rows.dtype, False)], [], 16, 4, name="share_mp")
    return out


def sum_mp(levels, part):
    _, here, wide = part.shape

    def kernel(given, out, own, first, second, *sems):
        w = Wires(levels, *sems)
        w.greet(flat=True)
        scatter_mp(w, given, own, first, second, out)
        w.finish()

    (out,) = call(
        kernel,
        4,
        [part],
        [((here, wide), jnp.float32, True)],
        [pltpu.VMEM((2, here, wide), part.dtype)] * 2 + [pltpu.VMEM((here, wide), part.dtype)],
        16,
        4,
        name="sum_mp",
    )
    return out


def end(levels, small, split, share):
    few, wide = small.shape[1:]
    many, flatly = split.shape[1:]
    scratch = scatter_all_scratch(levels, few, wide)
    scratch += [pltpu.VMEM((levels, many, flatly), jnp.bfloat16)] * 4

    def kernel(small_ref, split_ref, small_out, split_out, shared, landing, *buffers):
        w = Wires(levels, *buffers[-3:])
        w.greet(far=True)

        def over_all():
            yield from scatter_all(w, small_ref, landing, *buffers[:8], small_out)
            mine = small_out.at[:, pl.ds(wide - share, share)]
            yield from gather_mp(w, mine, lambda x, c: shared.at[x * 2 + c])

        turn([scatter_dp(w, split_ref, *buffers[8:-3], split_out), over_all()])
        w.finish()

    made = call(
        kernel,
        5,
        [small, split],
        [
            ((few, wide), jnp.float32, True),
            ((many, flatly), jnp.float32, True),
            ((4, few, share), jnp.float32, True),
            ((4 * levels, few, wide), jnp.bfloat16, False),
        ],
        scratch,
        16 * levels,
        9 * levels + 4,
        name="end",
    )
    return made[:3]


def low(rows):
    return rows.astype(jnp.bfloat16)


def unit_rows(rows):
    scale = lax.rsqrt(jnp.mean(rows * rows, axis=-1, keepdims=True) + EPS)
    return rows * scale, scale


def norm_back(grad, normed, scale):
    return scale * (grad - normed * jnp.mean(grad * normed, axis=-1, keepdims=True))


def by_unit(
    levels,
    layer_input,
    output_grad,
    attention_gain,
    query_weight,
    key_weight,
    value_weight,
    output_weight,
    query_shrink,
    query_expand,
    key_shrink,
    key_expand,
    value_shrink,
    value_expand,
    output_shrink,
    output_expand,
    feedforward_gain,
    gate_weight,
    up_weight,
    down_weight,
    gate_shrink,
    gate_expand,
    up_shrink,
    up_expand,
    down_shrink,
    down_expand,
    group_ids,
    positions,
    segments,
):
    count = 2 * levels
    rows = layer_input.shape[0]
    tokens = 4 * rows
    deep = layer_input.shape[1]
    head = key_weight.shape[1]
    heads = query_weight.shape[1] // head
    rank = query_expand.shape[0] * count
    mp = lax.axis_index("mp")
    share = query_shrink.shape[0] // 4

    gains = jnp.stack([attention_gain, feedforward_gain], axis=1)
    gains = jnp.pad(gains, ((0, 0), (0, 126)))
    maps = jnp.concatenate(
        [key_weight, value_weight, query_shrink, key_shrink, value_shrink, gate_shrink, up_shrink, gains],
        axis=1,
    )
    maps = lax.dynamic_slice_in_dim(maps, mp * share, share, 0)
    expands = jnp.concatenate([query_expand, key_expand, value_expand], axis=1)
    got = begin(
        levels,
        SimpleNamespace(
            layer_input=layer_input,
            maps=maps,
            output_expand=output_expand,
            down_expand=down_expand,
            query_weight=query_weight,
            output_weight=output_weight,
            expands=expands,
            output_shrink=output_shrink,
            output_grad=output_grad,
            gate_weight=gate_weight,
            up_weight=up_weight,
            down_weight=down_weight,
            gate_expand=gate_expand,
            up_expand=up_expand,
        ),
    )
    maps = got.maps
    key_w, value_w = maps[:, :head], maps[:, head : 2 * head]
    query_a, key_a, value_a, gate_a, up_a = (
        maps[:, 2 * head + i * rank : 2 * head + (i + 1) * rank] for i in range(5)
    )
    gain_one = maps[:, 2 * head + 5 * rank : 2 * head + 5 * rank + 1].astype(jnp.float32)
    gain_two = maps[:, 2 * head + 5 * rank + 1 : 2 * head + 5 * rank + 2].astype(jnp.float32)
    query_b = got.expands[:, : heads * head]
    key_b = got.expands[:, heads * head : (heads + 1) * head]
    value_b = got.expands[:, (heads + 1) * head :]
    output_a, output_b = got.output_shrink, got.output_expand
    query_full = low(gain_one * (got.query_weight.astype(jnp.float32) + matmul(query_a, query_b)))
    key_full = low(gain_one * (key_w.astype(jnp.float32) + matmul(key_a, key_b)))
    value_full = low(gain_one * (value_w.astype(jnp.float32) + matmul(value_a, value_b)))
    inward = jnp.concatenate([query_full, key_full, value_full], axis=1)
    outward = low(got.output_weight.astype(jnp.float32) + matmul(output_a, output_b))

    allowed = (
        (group_ids[:, None] == group_ids[None, :])
        & (positions[None, :] <= positions[:, None])
        & ((segments[None, :] == 0) | (segments[None, :] == segments[:, None]))
    )
    group_rows = got.layer_input.reshape(tokens, deep).astype(jnp.float32)
    normed = low(unit_rows(group_rows)[0])
    lin = matmul(normed, inward)
    wide = heads * head
    queries = low(rotary(lin[:, :wide].reshape(tokens, heads, head), positions, 1.0) * head ** (-0.5))
    keys = low(rotary(lin[:, None, wide : wide + head], positions, 1.0)[:, 0, :])
    values = low(lin[:, wide + head :])
    scores = jnp.einsum("thd,sd->hts", queries, keys, preferred_element_type=jnp.float32)
    scores = jnp.where(allowed[None], scores, -1e30)
    expo = jnp.exp(scores - jnp.max(scores, axis=-1, keepdims=True))
    probability = expo / jnp.sum(expo, axis=-1, keepdims=True)
    probability_low = low(probability)
    mixed = low(
        jnp.einsum("hts,sd->thd", probability_low, values, preferred_element_type=jnp.float32)
    ).reshape(tokens, wide)
    branch = sum_mp(levels, low(matmul(mixed, outward)).reshape(4, rows, deep))
    own_rows = layer_input.astype(jnp.float32)
    middle = own_rows + branch

    gate_up = low(
        gain_two
        * (
            jnp.concatenate([got.gate_weight, got.up_weight], axis=1).astype(jnp.float32)
            + jnp.concatenate([matmul(gate_a, got.gate_expand), matmul(up_a, got.up_expand)], axis=1)
        )
    )
    unit = got.gate_weight.shape[1]
    down_a, down_b = down_shrink, got.down_expand
    down_full = low(got.down_weight.astype(jnp.float32) + matmul(down_a, down_b))
    normed_middle, scale_middle = unit_rows(middle)
    feed = spread(levels, low(normed_middle)).reshape(4 * count * rows, deep)
    grads = got.output_grad.reshape(4 * count * rows, deep)
    pre = matmul(feed, gate_up)
    hidden_wide, pull = jax.vjp(
        lambda gate, up: jax.nn.gelu(gate, approximate=True) * up, pre[:, :unit], pre[:, unit:]
    )
    hidden = low(hidden_wide)
    grad_pre = low(jnp.concatenate(pull(against(grads, down_full)), axis=1))
    blocks = (4 * count, rows, deep)
    down_grad = outer_sum(hidden, grads)
    gate_up_normed = outer_sum(feed, grad_pre)
    feed_gain = jnp.sum(gate_up_normed * gate_up.astype(jnp.float32), axis=1, keepdims=True) / gain_two
    gate_up_grad = low(gate_up_normed * gain_two)
    down_grad_low = low(down_grad)
    down_shrink_grad = against(down_grad_low, down_b)
    down_b_part = outer_sum(down_a, down_grad_low)
    gate_b_grad = low(outer_sum(gate_a, gate_up_grad[:, :unit]))
    up_b_grad = low(outer_sum(up_a, gate_up_grad[:, unit:]))
    grad_normed, branch, units = collect(
        levels,
        low(against(grad_pre, gate_up)).reshape(blocks),
        low(matmul(hidden, down_full)).reshape(blocks),
        SimpleNamespace(
            gate_weight=gate_up_grad[:, :unit],
            up_weight=gate_up_grad[:, unit:],
            down_weight=down_grad_low,
            gate_expand=gate_b_grad,
            up_expand=up_b_grad,
        ),
    )
    result = low(middle + branch)
    grad_middle = output_grad.astype(jnp.float32) + norm_back(grad_normed, normed_middle, scale_middle)
    gate_a_part = against(gate_up_grad[:, :unit], got.gate_expand)
    up_a_part = against(gate_up_grad[:, unit:], got.up_expand)

    grad_branch = share_mp(levels, low(grad_middle)).reshape(tokens, deep)
    output_grad_w = outer_sum(mixed, grad_branch)
    grad_mixed = low(against(grad_branch, outward)).reshape(tokens, heads, head)
    grad_values = jnp.einsum("hts,thd->sd", probability_low, grad_mixed, preferred_element_type=jnp.float32)
    grad_probability = jnp.einsum("thd,sd->hts", grad_mixed, values, preferred_element_type=jnp.float32)
    grad_scores = low(
        probability * (grad_probability - jnp.sum(probability * grad_probability, axis=-1, keepdims=True))
    )
    grad_queries = jnp.einsum("hts,sd->thd", grad_scores, keys, preferred_element_type=jnp.float32)
    grad_keys = jnp.einsum("hts,thd->sd", grad_scores, queries, preferred_element_type=jnp.float32)
    grad_query = rotary(grad_queries * head ** (-0.5), positions, -1.0).reshape(tokens, wide)
    grad_key = rotary(grad_keys[:, None, :], positions, -1.0)[:, 0, :]
    grad_lin = low(jnp.concatenate([grad_query, grad_key, grad_values], axis=1))
    grad_rows = sum_mp(levels, low(against(grad_lin, inward)).reshape(4, rows, deep))
    normed_own, scale_own = unit_rows(own_rows)
    input_grad = grad_middle + norm_back(grad_rows, normed_own, scale_own)

    lin_normed = outer_sum(normed, grad_lin)
    attention_gain_part = jnp.sum(lin_normed * inward.astype(jnp.float32), axis=1, keepdims=True) / gain_one
    lin_grad = low(lin_normed * gain_one)
    query_part, key_part, value_part = (
        lin_grad[:, :wide],
        lin_grad[:, wide : wide + head],
        lin_grad[:, wide + head :],
    )
    query_b_part = outer_sum(query_a, query_part)
    key_b_part = outer_sum(key_a, key_part)
    value_b_part = outer_sum(value_a, value_part)
    query_a_part = against(query_part, query_b)
    output_low = low(output_grad_w)
    output_a_part = against(output_low, output_b)
    output_b_part = outer_sum(output_a, output_low)

    def by_device(array):
        return low(array).reshape(4 * count, array.shape[0] // (4 * count), array.shape[1])

    def fold(array):
        return by_device(array).reshape(4 * count, share, -1)

    def fold_wide(array):
        cut = low(array).reshape(count, array.shape[0] // count, 4, array.shape[1] // 4)
        return cut.transpose(0, 2, 1, 3).reshape(4 * count, share, -1)

    gain_part = jnp.pad(jnp.concatenate([attention_gain_part, feed_gain], axis=1), ((0, 0), (0, 62)))
    small = jnp.concatenate(
        [
            by_device(key_part),
            by_device(value_part),
            by_device(query_a_part),
            by_device(gate_a_part),
            by_device(up_a_part),
            by_device(gain_part),
            fold(key_b_part),
            fold(value_b_part),
            fold_wide(output_b_part),
            fold_wide(down_b_part),
        ],
        axis=2,
    )
    split = jnp.concatenate(
        [
            low(query_part).reshape(count, -1, wide),
            output_low.reshape(wide, count, deep // count).transpose(1, 0, 2).reshape(count, -1, wide),
            low(query_b_part).reshape(count, -1, wide),
            low(output_a_part).reshape(count, -1, wide),
        ],
        axis=1,
    )
    wide_share = 2 * (rank // count) * (deep // 4) // share
    few, many, shared = end(levels, small, split, wide_share)
    key_own, value_own = few[:, :head], few[:, head : 2 * head]
    query_a_own, gate_a_own, up_a_own = (
        few[:, 2 * head + i * rank : 2 * head + (i + 1) * rank] for i in range(3)
    )
    place = 2 * head + 3 * rank
    key_b_own = few[:, place + 64 : place + 96].reshape(-1, head)
    value_b_own = few[:, place + 96 : place + 128].reshape(-1, head)
    half = wide_share // 2

    def unfold(array):
        return array.reshape(4, rank // count, deep // 4).transpose(1, 0, 2).reshape(-1, deep)

    key_a_own = against(low(key_own), key_b)
    value_a_own = against(low(value_own), value_b)
    first = query_weight.shape[0]
    second = first + output_weight.size // wide
    third = second + query_expand.shape[0]
    wider = jnp.float32
    return (
        result,
        input_grad,
        few[:, place],
        many[:first],
        key_own,
        value_own,
        many[first:second].reshape(output_weight.shape),
        query_a_own,
        many[second:third],
        key_a_own,
        key_b_own,
        value_a_own,
        value_b_own,
        many[third:].reshape(output_shrink.shape),
        unfold(shared[:, :, :half]),
        few[:, place + 1],
        units.gate_weight.astype(wider),
        units.up_weight.astype(wider),
        units.down_weight.astype(wider),
        gate_a_own,
        units.gate_expand.astype(wider),
        up_a_own,
        units.up_expand.astype(wider),
        down_shrink_grad,
        unfold(shared[:, :, half:]),
    )


def body(
    layer_input,
    output_grad,
    attention_gain,
    query_weight,
    key_weight,
    value_weight,
    output_weight,
    query_shrink,
    query_expand,
    key_shrink,
    key_expand,
    value_shrink,
    value_expand,
    output_shrink,
    output_expand,
    feedforward_gain,
    gate_weight,
    up_weight,
    down_weight,
    gate_shrink,
    gate_expand,
    up_shrink,
    up_expand,
    down_shrink,
    down_expand,
    group_ids,
    positions,
    segments,
):
    rows_local = layer_input.shape[0]
    own_start = lax.axis_index("mp") * rows_local
    allowed = (
        (group_ids[:, None] == group_ids[None, :])
        & (positions[None, :] <= positions[:, None])
        & ((segments[None, :] == 0) | (segments[None, :] == segments[:, None]))
    )

    def gather_attention():
        return (
            lax.all_gather(attention_gain, "dp", axis=0, tiled=True),
            lax.all_gather(query_weight, "dp", axis=0, tiled=True),
            lax.all_gather(key_weight, "dp", axis=0, tiled=True),
            lax.all_gather(value_weight, "dp", axis=0, tiled=True),
            lax.all_gather(output_weight, "dp", axis=1, tiled=True),
            lax.all_gather(query_shrink, "dp", axis=0, tiled=True),
            lax.all_gather(query_expand, "dp", axis=0, tiled=True),
            lax.all_gather(key_shrink, "dp", axis=0, tiled=True),
            lax.all_gather(key_expand, "dp", axis=0, tiled=True),
            lax.all_gather(value_shrink, "dp", axis=0, tiled=True),
            lax.all_gather(value_expand, "dp", axis=0, tiled=True),
            lax.all_gather(output_shrink, "dp", axis=0, tiled=True),
            lax.all_gather(output_expand, "dp", axis=0, tiled=True),
        )

    def gather_feed():
        return (
            lax.all_gather(feedforward_gain, "dp", axis=0, tiled=True),
            lax.all_gather(gate_weight, "dp", axis=0, tiled=True),
            lax.all_gather(up_weight, "dp", axis=0, tiled=True),
            lax.all_gather(down_weight, "dp", axis=1, tiled=True),
            lax.all_gather(gate_shrink, "dp", axis=0, tiled=True),
            lax.all_gather(gate_expand, "dp", axis=0, tiled=True),
            lax.all_gather(up_shrink, "dp", axis=0, tiled=True),
            lax.all_gather(up_expand, "dp", axis=0, tiled=True),
            lax.all_gather(down_shrink, "dp", axis=0, tiled=True),
            lax.all_gather(down_expand, "dp", axis=0, tiled=True),
        )

    def gather_rows(rows):
        return lax.all_gather(rows, "mp", axis=0, tiled=True)

    def gather_grads(rows):
        return lax.all_gather(rows, "mp", axis=0, tiled=True)

    def scatter_grads(term):
        return lax.psum_scatter(
            term(jnp.int32(0), lax.axis_size("mp") * rows_local),
            "mp",
            scatter_dimension=0,
            tiled=True,
        )

    def project_out(mixed, weight, shrink, expand):
        reduced = lax.psum(matmul(mixed, shrink), "mp").astype(jnp.bfloat16)

        def term(start, count):
            return matmul(mixed, weight)

        branch = lax.psum_scatter(
            term(jnp.int32(0), lax.axis_size("mp") * rows_local),
            "mp",
            scatter_dimension=0,
            tiled=True,
        )
        own = lax.dynamic_slice_in_dim(reduced, own_start, rows_local, 0)
        return (branch + matmul(own, expand), reduced)

    def masked_scores(queries, keys_rot):
        scores = jnp.einsum("thd,sd->hts", queries, keys_rot, preferred_element_type=jnp.float32)
        return jnp.where(allowed[None], scores, -1e30)

    def attention_forward(rows_in, params):
        (
            gain_one,
            w_query,
            w_key,
            w_value,
            w_output,
            query_a,
            query_b,
            key_a,
            key_b,
            value_a,
            value_b,
            output_a,
            output_b,
        ) = params
        normed = gather_rows(norm_rows(rows_in, gain_one.astype(jnp.float32)).astype(jnp.bfloat16))
        tokens = normed.shape[0]
        head_size = w_key.shape[1]
        heads = w_query.shape[1] // head_size
        query_low = matmul(normed, query_a).astype(jnp.bfloat16)
        key_low = matmul(normed, key_a).astype(jnp.bfloat16)
        value_low = matmul(normed, value_a).astype(jnp.bfloat16)
        query_lin = matmul(normed, w_query) + matmul(query_low, query_b)
        key_lin = matmul(normed, w_key) + matmul(key_low, key_b)
        value_lin = matmul(normed, w_value) + matmul(value_low, value_b)
        queries = (
            rotary(query_lin.reshape(tokens, heads, head_size), positions, 1.0)
            * head_size ** (-0.5)
        ).astype(jnp.bfloat16)
        keys_rot = rotary(key_lin[:, None, :], positions, 1.0)[:, 0, :].astype(jnp.bfloat16)
        values = value_lin.astype(jnp.bfloat16)
        scores = masked_scores(queries, keys_rot)
        highest = jnp.max(scores, axis=-1, keepdims=True)
        expo = jnp.exp(scores - highest)
        totals = jnp.sum(expo, axis=-1, keepdims=True)
        probability = expo / totals
        logsum = highest + jnp.log(totals)
        mixed = jnp.einsum(
            "hts,sd->thd",
            probability.astype(jnp.bfloat16),
            values,
            preferred_element_type=jnp.float32,
        )
        mixed = mixed.reshape(tokens, heads * head_size).astype(jnp.bfloat16)
        branch, reduced = project_out(mixed, w_output, output_a, output_b)
        saved = (
            normed,
            query_low,
            key_low,
            value_low,
            queries,
            keys_rot,
            values,
            logsum,
            mixed,
            reduced,
        )
        return (rows_in + branch, saved)

    def feed_forward(middle, params):
        gain_two, w_gate, w_up, w_down, gate_a, gate_b, up_a, up_b, down_a, down_b = params
        normed = gather_rows(norm_rows(middle, gain_two.astype(jnp.float32)).astype(jnp.bfloat16))
        gate_low = matmul(normed, gate_a).astype(jnp.bfloat16)
        up_low = matmul(normed, up_a).astype(jnp.bfloat16)
        gate_pre = matmul(normed, w_gate) + matmul(gate_low, gate_b)
        up_pre = matmul(normed, w_up) + matmul(up_low, up_b)
        hidden = (jax.nn.gelu(gate_pre, approximate=True) * up_pre).astype(jnp.bfloat16)
        branch, reduced = project_out(hidden, w_down, down_a, down_b)
        return (middle + branch, (normed, gate_low, up_low, gate_pre, up_pre, hidden, reduced))

    rows_in = layer_input.astype(jnp.float32)
    attention_params = gather_attention()
    middle, attention_saved = attention_forward(rows_in, attention_params)
    feed_params = gather_feed()
    result, feed_saved = feed_forward(middle, feed_params)
    feed_params = gather_feed()
    feed_saved = feed_forward(middle, feed_params)[1]
    gain_two, w_gate, w_up, w_down, gate_a, gate_b, up_a, up_b, down_a, down_b = feed_params
    normed_feed, gate_low, up_low, gate_pre, up_pre, hidden, reduced_feed = feed_saved
    grad_branch_feed = gather_grads(output_grad)
    down_weight_grad = outer_sum(hidden, grad_branch_feed)
    down_expand_grad = outer_sum(reduced_feed, grad_branch_feed)
    grad_reduced_feed = against(grad_branch_feed, down_b).astype(jnp.bfloat16)
    down_shrink_grad = outer_sum(hidden, grad_reduced_feed)
    grad_hidden = against(grad_branch_feed, w_down) + against(grad_reduced_feed, down_a)
    unused, gelu_pull = jax.vjp(
        lambda gated, upper: jax.nn.gelu(gated, approximate=True) * upper, gate_pre, up_pre
    )
    grad_gate, grad_up = gelu_pull(grad_hidden)
    grad_gate = grad_gate.astype(jnp.bfloat16)
    grad_up = grad_up.astype(jnp.bfloat16)
    gate_expand_grad = outer_sum(gate_low, grad_gate)
    up_expand_grad = outer_sum(up_low, grad_up)
    grad_gate_low = against(grad_gate, gate_b)
    grad_up_low = against(grad_up, up_b)
    feed_wide = normed_feed.astype(jnp.float32)
    gate_shrink_grad = outer_exact(feed_wide, grad_gate_low)
    up_shrink_grad = outer_exact(feed_wide, grad_up_low)
    gate_a_wide = gate_a.astype(jnp.float32)
    up_a_wide = up_a.astype(jnp.float32)

    def feed_term(start, count):

        def pick(rows):
            return rows

        total = against(pick(grad_gate), w_gate) + against(pick(grad_up), w_up)
        return (
            total
            + against_exact(pick(grad_gate_low), gate_a_wide)
            + against_exact(pick(grad_up_low), up_a_wide)
        )

    grad_normed_feed = scatter_grads(feed_term)
    unused, norm_pull = jax.vjp(norm_rows, middle, gain_two.astype(jnp.float32))
    grad_middle_part, feed_gain_grad = norm_pull(grad_normed_feed)
    grad_middle = output_grad.astype(jnp.float32) + grad_middle_part
    gate_weight_grad = outer_sum(normed_feed, grad_gate)
    up_weight_grad = outer_sum(normed_feed, grad_up)
    feed_split = (
        lax.psum_scatter(
            gate_weight_grad.astype(jnp.bfloat16), "dp", scatter_dimension=0, tiled=True
        ).astype(jnp.float32),
        lax.psum_scatter(
            up_weight_grad.astype(jnp.bfloat16), "dp", scatter_dimension=0, tiled=True
        ).astype(jnp.float32),
        lax.psum_scatter(
            down_weight_grad.astype(jnp.bfloat16), "dp", scatter_dimension=1, tiled=True
        ).astype(jnp.float32),
        lax.psum_scatter(
            gate_expand_grad.astype(jnp.bfloat16), "dp", scatter_dimension=0, tiled=True
        ).astype(jnp.float32),
        lax.psum_scatter(
            up_expand_grad.astype(jnp.bfloat16), "dp", scatter_dimension=0, tiled=True
        ).astype(jnp.float32),
        lax.psum_scatter(
            down_shrink_grad.astype(jnp.bfloat16), "dp", scatter_dimension=0, tiled=True
        ).astype(jnp.float32),
        lax.psum_scatter(
            down_expand_grad.astype(jnp.bfloat16), "dp", scatter_dimension=0, tiled=True
        ).astype(jnp.float32),
    )
    gate_weight_own, up_weight_own = (feed_split[0], feed_split[1])
    down_weight_own, gate_expand_own, up_expand_own, down_shrink_own, down_expand_own = (
        feed_split[2],
        feed_split[3],
        feed_split[4],
        feed_split[5],
        feed_split[6],
    )
    feed_shared = (
        lax.psum_scatter(feed_gain_grad, ("dp", "mp"), scatter_dimension=0, tiled=True),
        lax.psum_scatter(gate_shrink_grad, ("dp", "mp"), scatter_dimension=0, tiled=True),
        lax.psum_scatter(up_shrink_grad, ("dp", "mp"), scatter_dimension=0, tiled=True),
    )
    attention_params = gather_attention()
    attention_saved = attention_forward(rows_in, attention_params)[1]
    (
        gain_one,
        w_query,
        w_key,
        w_value,
        w_output,
        query_a,
        query_b,
        key_a,
        key_b,
        value_a,
        value_b,
        output_a,
        output_b,
    ) = attention_params
    normed, query_low, key_low, value_low, queries, keys_rot, values, logsum, mixed, reduced = (
        attention_saved
    )
    tokens = normed.shape[0]
    head_size = w_key.shape[1]
    heads = w_query.shape[1] // head_size
    grad_branch = gather_grads(grad_middle.astype(jnp.bfloat16))
    output_weight_grad = outer_sum(mixed, grad_branch)
    output_expand_grad = outer_sum(reduced, grad_branch)
    grad_reduced = against(grad_branch, output_b).astype(jnp.bfloat16)
    output_shrink_grad = outer_sum(mixed, grad_reduced)
    grad_mixed = (against(grad_branch, w_output) + against(grad_reduced, output_a)).astype(
        jnp.bfloat16
    )
    grad_mixed = grad_mixed.reshape(tokens, heads, head_size)
    probability = jnp.exp(masked_scores(queries, keys_rot) - logsum)
    grad_values = jnp.einsum(
        "hts,thd->sd",
        probability.astype(jnp.bfloat16),
        grad_mixed,
        preferred_element_type=jnp.float32,
    )
    grad_probability = jnp.einsum(
        "thd,sd->hts", grad_mixed, values, preferred_element_type=jnp.float32
    )
    grad_scores = probability * (
        grad_probability - jnp.sum(probability * grad_probability, axis=-1, keepdims=True)
    )
    grad_scores = grad_scores.astype(jnp.bfloat16)
    grad_queries_rot = jnp.einsum(
        "hts,sd->thd", grad_scores, keys_rot, preferred_element_type=jnp.float32
    )
    grad_keys_rot = jnp.einsum(
        "hts,thd->sd", grad_scores, queries, preferred_element_type=jnp.float32
    )
    grad_query = (
        rotary(grad_queries_rot * head_size ** (-0.5), positions, -1.0)
        .reshape(tokens, heads * head_size)
        .astype(jnp.bfloat16)
    )
    grad_key = rotary(grad_keys_rot[:, None, :], positions, -1.0)[:, 0, :]
    normed_wide = normed.astype(jnp.float32)
    query_weight_grad = outer_sum(normed, grad_query)
    query_expand_grad = outer_sum(query_low, grad_query)
    grad_query_low = against(grad_query, query_b)
    query_shrink_grad = outer_exact(normed_wide, grad_query_low)
    key_weight_grad = outer_exact(normed_wide, grad_key)
    key_expand_grad = outer_exact(key_low.astype(jnp.float32), grad_key)
    grad_key_low = against_exact(grad_key, key_b.astype(jnp.float32))
    key_shrink_grad = outer_exact(normed_wide, grad_key_low)
    value_weight_grad = outer_exact(normed_wide, grad_values)
    value_expand_grad = outer_exact(value_low.astype(jnp.float32), grad_values)
    grad_value_low = against_exact(grad_values, value_b.astype(jnp.float32))
    value_shrink_grad = outer_exact(normed_wide, grad_value_low)
    query_a_wide = query_a.astype(jnp.float32)
    key_wide = w_key.astype(jnp.float32)
    key_a_wide = key_a.astype(jnp.float32)
    value_wide = w_value.astype(jnp.float32)
    value_a_wide = value_a.astype(jnp.float32)

    def attention_term(start, count):

        def pick(rows):
            return rows

        total = against(pick(grad_query), w_query) + against_exact(
            pick(grad_query_low), query_a_wide
        )
        total = (
            total
            + against_exact(pick(grad_key), key_wide)
            + against_exact(pick(grad_key_low), key_a_wide)
        )
        return (
            total
            + against_exact(pick(grad_values), value_wide)
            + against_exact(pick(grad_value_low), value_a_wide)
        )

    grad_normed = scatter_grads(attention_term)
    unused, norm_pull_one = jax.vjp(norm_rows, rows_in, gain_one.astype(jnp.float32))
    grad_input_part, attention_gain_grad = norm_pull_one(grad_normed)
    input_grad = grad_middle + grad_input_part
    attention_split = (
        lax.psum_scatter(
            query_weight_grad.astype(jnp.bfloat16), "dp", scatter_dimension=0, tiled=True
        ).astype(jnp.float32),
        lax.psum_scatter(
            output_weight_grad.astype(jnp.bfloat16), "dp", scatter_dimension=1, tiled=True
        ).astype(jnp.float32),
        lax.psum_scatter(
            query_expand_grad.astype(jnp.bfloat16), "dp", scatter_dimension=0, tiled=True
        ).astype(jnp.float32),
        lax.psum_scatter(
            output_shrink_grad.astype(jnp.bfloat16), "dp", scatter_dimension=0, tiled=True
        ).astype(jnp.float32),
        lax.psum_scatter(
            output_expand_grad.astype(jnp.bfloat16), "dp", scatter_dimension=0, tiled=True
        ).astype(jnp.float32),
    )
    attention_shared = (
        lax.psum_scatter(attention_gain_grad, ("dp", "mp"), scatter_dimension=0, tiled=True),
        lax.psum_scatter(key_weight_grad, ("dp", "mp"), scatter_dimension=0, tiled=True),
        lax.psum_scatter(value_weight_grad, ("dp", "mp"), scatter_dimension=0, tiled=True),
        lax.psum_scatter(query_shrink_grad, ("dp", "mp"), scatter_dimension=0, tiled=True),
        lax.psum_scatter(key_shrink_grad, ("dp", "mp"), scatter_dimension=0, tiled=True),
        lax.psum_scatter(key_expand_grad, ("dp", "mp"), scatter_dimension=0, tiled=True),
        lax.psum_scatter(value_shrink_grad, ("dp", "mp"), scatter_dimension=0, tiled=True),
        lax.psum_scatter(value_expand_grad, ("dp", "mp"), scatter_dimension=0, tiled=True),
    )
    return (
        result.astype(jnp.bfloat16),
        input_grad,
        attention_shared[0],
        attention_split[0],
        attention_shared[1],
        attention_shared[2],
        attention_split[1],
        attention_shared[3],
        attention_split[2],
        attention_shared[4],
        attention_shared[5],
        attention_shared[6],
        attention_shared[7],
        attention_split[3],
        attention_split[4],
        feed_shared[0],
        gate_weight_own,
        up_weight_own,
        down_weight_own,
        feed_shared[1],
        gate_expand_own,
        feed_shared[2],
        up_expand_own,
        down_shrink_own,
        down_expand_own,
    )


def solution(mesh):
    levels = mesh.shape["dp"] // 2
    few = mesh.shape["mp"] == 4 and mesh.shape["dp"] % 2 == 0 and levels <= 4
    step = functools.partial(by_unit, levels) if few else body
    placed = (
        P(("dp", "mp"), None),
        P(("dp", "mp"), None),
        P("dp"),
        P("dp", "mp"),
        P("dp", None),
        P("dp", None),
        P("mp", "dp"),
        P("dp", None),
        P("dp", "mp"),
        P("dp", None),
        P("dp", None),
        P("dp", None),
        P("dp", None),
        P(("mp", "dp"), None),
        P("dp", None),
        P("dp"),
        P("dp", "mp"),
        P("dp", "mp"),
        P("mp", "dp"),
        P("dp", None),
        P("dp", "mp"),
        P("dp", None),
        P("dp", "mp"),
        P(("mp", "dp"), None),
        P("dp", None),
        P("dp"),
        P("dp"),
        P("dp"),
    )
    return jax.shard_map(
        step,
        mesh=mesh,
        in_specs=placed,
        out_specs=(
            P(("dp", "mp"), None),
            P(("dp", "mp"), None),
            P(("dp", "mp")),
            P("dp", "mp"),
            P(("dp", "mp"), None),
            P(("dp", "mp"), None),
            P("mp", "dp"),
            P(("dp", "mp"), None),
            P("dp", "mp"),
            P(("dp", "mp"), None),
            P(("dp", "mp"), None),
            P(("dp", "mp"), None),
            P(("dp", "mp"), None),
            P(("mp", "dp"), None),
            P("dp", None),
            P(("dp", "mp")),
            P("dp", "mp"),
            P("dp", "mp"),
            P("mp", "dp"),
            P(("dp", "mp"), None),
            P("dp", "mp"),
            P(("dp", "mp"), None),
            P("dp", "mp"),
            P(("mp", "dp"), None),
            P("dp", None),
        ),
        check_vma=False,
    )
```

```python
import functools
import math
from types import SimpleNamespace

import jax
import jax.numpy as jnp
from jax import lax
from jax.experimental import pallas as pl
from jax.experimental.pallas import tpu as pltpu
from jax.sharding import PartitionSpec as P

MESH = pl.DeviceIdType.MESH
MIB = 1 << 20

EPS = 1e-06


def matmul(left, right):
    return jnp.dot(left, right, preferred_element_type=jnp.float32)


def against(left, right):
    return lax.dot_general(
        left, right, (((1,), (1,)), ((), ())), preferred_element_type=jnp.float32
    )


def outer_sum(left, right):
    return lax.dot_general(
        left, right, (((0,), (0,)), ((), ())), preferred_element_type=jnp.float32
    )


def against_exact(left, right):
    return lax.dot_general(
        left,
        right,
        (((1,), (1,)), ((), ())),
        precision=lax.Precision.HIGHEST,
        preferred_element_type=jnp.float32,
    )


def outer_exact(left, right):
    return lax.dot_general(
        left,
        right,
        (((0,), (0,)), ((), ())),
        precision=lax.Precision.HIGHEST,
        preferred_element_type=jnp.float32,
    )


def norm_rows(rows, gain):
    return rows * lax.rsqrt(jnp.mean(rows * rows, axis=-1, keepdims=True) + EPS) * gain


def rotary(entries, places, sign):
    half = entries.shape[-1] // 2
    freq = 10000.0 ** (-jnp.arange(half).astype(jnp.float32) * 2.0 / entries.shape[-1])
    angle = places.astype(jnp.float32)[:, None] * freq[None, :]
    cosine = jnp.cos(angle)[:, None, :]
    sine = sign * jnp.sin(angle)[:, None, :]
    first = entries[..., :half]
    second = entries[..., half:]
    return jnp.concatenate(
        [first * cosine - second * sine, second * cosine + first * sine], axis=-1
    )


class Wires:
    def __init__(self, levels, sends, lands, locals_=None):
        self.sends, self.lands, self.locals = sends, lands, locals_
        self.levels = levels
        self.count = self.local_count = 0
        self.open = []
        dp, mp = lax.axis_index("dp"), lax.axis_index("mp")
        self.dp, self.mp = dp, mp
        self.z, self.y, self.x, self.c = dp // 2, dp % 2, mp // 2, mp % 2

    def take(self, number=1):
        first = self.count
        self.count += number
        assert self.count <= self.sends.shape[0], self.count
        return first

    def at(self, z, y, x, c):
        return (z * 2 + y, x * 2 + c)

    def up(self):
        return self.at(self.z + 1, self.y, self.x, self.c)

    def down(self):
        return self.at(self.z - 1, self.y, self.x, self.c)

    def over_x(self):
        return self.at(self.z, self.y, 1 - self.x, self.c)

    def over_y(self):
        return self.at(self.z, 1 - self.y, self.x, self.c)

    def over_core(self):
        return self.at(self.z, self.y, self.x, 1 - self.c)

    def copy(self, source, target, out, land, device):
        return pltpu.make_async_remote_copy(
            src_ref=source,
            dst_ref=target,
            send_sem=self.sends.at[out],
            recv_sem=self.lands.at[land],
            device_id=device,
            device_id_type=MESH,
        )

    def send(self, source, target, out, land, device, when=True):
        made = self.copy(source, target, out, land, device)
        under(when, made.start)
        self.open.append((when, made.wait_send))

    def landed(self, target, land):
        self.copy(target, target, land, land, self.over_x()).wait_recv()

    def local(self, source, target):
        made = pltpu.make_async_copy(source, target, self.locals.at[self.local_count])
        self.local_count += 1
        assert self.local_count <= self.locals.shape[0], self.local_count
        made.start()
        return made

    def take_local(self, number):
        first = self.local_count
        self.local_count += number
        assert self.local_count <= self.locals.shape[0], self.local_count
        return first

    def finish(self):
        for when, wait in self.open:
            under(when, wait)

    def greet(self, far=False, flat=False):
        barrier = pltpu.get_barrier_semaphore()

        def call(device):
            pl.semaphore_signal(barrier, inc=1, device_id=device, device_id_type=MESH)

        call(self.over_x())
        call(self.over_core())
        if far:
            call(self.at(self.z, self.y, 1 - self.x, 1 - self.c))
            for step in range(1, 2 * self.levels):
                call((lax.rem(self.dp + step, 2 * self.levels), self.mp))
            pl.semaphore_wait(barrier, 2 + 2 * self.levels)
            return
        if flat:
            pl.semaphore_wait(barrier, 2)
            return
        call(self.over_y())
        pl.when(self.z > 0)(lambda: call(self.down()))
        pl.when(self.z < self.levels - 1)(lambda: call(self.up()))
        ends = jnp.where(self.z > 0, 1, 0) + jnp.where(self.z < self.levels - 1, 1, 0)
        pl.semaphore_wait(barrier, 3 + ends)


def under(when, act):
    if when is True:
        act()
    else:
        pl.when(when)(act)


def sides(w, step):
    yield (True, w.z - step, w.z >= step)
    yield (False, w.z + step, w.z < w.levels - step)


def gather_all(w, own, at, parts):
    z, y, x, c = w.z, w.y, w.x, w.c
    n = w.levels
    rise, fall, by_x, by_y, last_x, last_y = (w.take(n) for _ in range(6))
    by_core = w.take(4 * n)

    def core(block, zs, ys, xs):
        place = by_core + zs * 4 + ys * 2 + xs
        return (block, block, place, place, w.over_core())

    here = at(z, y, x, c)
    kept = w.local(own, here)
    w.send(own, here, rise + z, rise + z, w.up(), z < n - 1)
    w.send(own, here, fall + z, fall + z, w.down(), z > 0)
    w.send(own, here, by_x + z, by_x + z, w.over_x())
    w.send(own, here, by_y + z, by_y + z, w.over_y())
    place = by_core + z * 4 + y * 2 + x
    w.send(own, here, place, place, w.over_core())
    yield

    def plane(zs, ok):
        block = at(zs, y, 1 - x, c)
        under(ok, lambda: w.landed(block, by_x + zs))
        for piece in parts(block)[:1]:
            if piece is not None:
                w.send(piece, piece, last_y + zs, last_y + zs, w.over_y(), ok)
        w.send(*core(block, zs, y, 1 - x), ok)
        block = at(zs, 1 - y, x, c)
        under(ok, lambda: w.landed(block, by_y + zs))
        for piece in parts(block)[1:]:
            if piece is not None:
                w.send(piece, piece, last_x + zs, last_x + zs, w.over_x(), ok)
        w.send(*core(block, zs, 1 - y, x), ok)

    plane(z, True)
    yield
    for step in range(1, n):
        for rising, zs, ok in sides(w, step):
            block = at(zs, y, x, c)
            lane = rise if rising else fall
            under(ok, lambda: w.landed(block, lane + zs))
            if rising:
                w.send(block, block, rise + zs, rise + zs, w.up(), jnp.logical_and(ok, z < n - 1))
            else:
                w.send(block, block, fall + zs, fall + zs, w.down(), jnp.logical_and(ok, z > 0))
            w.send(block, block, by_x + zs, by_x + zs, w.over_x(), ok)
            w.send(block, block, by_y + zs, by_y + zs, w.over_y(), ok)
            w.send(*core(block, zs, y, x), ok)
        yield
        for _, zs, ok in sides(w, step):
            plane(zs, ok)
        yield
    for step in range(n):
        for _, zs, ok in sides(w, step) if step else [(True, z, True)]:
            block = at(zs, 1 - y, 1 - x, c)
            for piece, lane in zip(parts(block), (last_y, last_x)):
                if piece is not None:
                    under(ok, lambda: w.landed(piece, lane + zs))
            w.send(*core(block, zs, 1 - y, 1 - x), ok)
        yield
    for zs in range(n):
        for ys in range(2):
            for xs in range(2):
                w.landed(at(zs, ys, xs, 1 - c), by_core + zs * 4 + ys * 2 + xs)
    kept.wait()


def gather_dp(w, own, at):
    z, y, n = w.z, w.y, w.levels
    rise, fall, by_y = (w.take(n) for _ in range(3))
    here = at(z, y)
    kept = w.local(own, here)
    w.send(own, here, rise + z, rise + z, w.up(), z < n - 1)
    w.send(own, here, fall + z, fall + z, w.down(), z > 0)
    w.send(own, here, by_y + z, by_y + z, w.over_y())
    yield
    yield
    for step in range(1, n):
        for rising, zs, ok in sides(w, step):
            block = at(zs, y)
            lane = rise if rising else fall
            under(ok, lambda: w.landed(block, lane + zs))
            if rising:
                w.send(block, block, rise + zs, rise + zs, w.up(), jnp.logical_and(ok, z < n - 1))
            else:
                w.send(block, block, fall + zs, fall + zs, w.down(), jnp.logical_and(ok, z > 0))
            w.send(block, block, by_y + zs, by_y + zs, w.over_y(), ok)
        yield
        yield
    for zs in range(n):
        w.landed(at(zs, 1 - y), by_y + zs)
    kept.wait()


def gather_mp(w, own, at):
    x, c = w.x, w.c
    first, second = w.take(), w.take(2)
    here = at(x, c)
    kept = w.local(own, here)
    w.send(own, here, first, first, w.over_x())
    w.send(own, here, second, second, w.over_core())
    yield
    block = at(1 - x, c)
    w.landed(block, first)
    w.send(block, block, second + 1, second + 1, w.over_core())
    yield
    w.landed(at(x, 1 - c), second)
    w.landed(at(1 - x, 1 - c), second + 1)
    kept.wait()


def exchange_dp(w, source, target):
    count = 2 * w.levels
    first = w.take(count)
    kept = w.local(source(w.dp), target(w.dp))
    for step in range(1, count):
        there = lax.rem(w.dp + step, count)
        w.send(source(there), target(w.dp), first + step, first + step, (there, w.mp))
        yield
    for step in range(1, count):
        w.landed(target(lax.rem(w.dp + count - step, count)), first + step)
    kept.wait()


PACE = 4


def turn(steps, after=(), pace=PACE):
    spare = [one for one in after for _ in range(7)]
    turn_on(steps, spare, pace)
    for one in spare:
        next(one)
    turn_on(after)


def turn_on(steps, spare=(), pace=0):
    steps = list(steps)
    while steps:
        for _ in range(min(pace, len(spare))):
            next(spare.pop(0))
        left = []
        for one in steps:
            try:
                next(one)
                left.append(one)
            except StopIteration:
                pass
        steps = left


CHUNK = 16


def add_up(target, *sources):
    rows = target.shape[0]

    def one(i, unused):
        part = pl.ds(pl.multiple_of(i * CHUNK, CHUNK), CHUNK)
        total = sources[0][part, :].astype(jnp.float32)
        for source in sources[1:]:
            total = total + source[part, :].astype(jnp.float32)
        target[part, :] = total.astype(target.dtype)
        return unused

    lax.fori_loop(0, rows // CHUNK, one, 0)


def chain_z(w, own, below, above, out):
    z, n = w.z, w.levels
    rise, fall = w.take(n), w.take(n)
    for step in range(n - 1, 0, -1):
        for rising, zt, ok in ((True, z + step, z < n - step), (False, z - step, z >= step)):
            lane = rise if rising else fall
            slot = below(zt) if rising else above(zt)
            inner = jnp.logical_and(ok, (z > 0) if rising else (z < n - 1))

            def take_in():
                w.landed(slot, lane + zt)
                add_up(own(zt), own(zt), slot)

            under(inner, take_in)
            w.send(own(zt), slot, lane + zt, lane + zt, w.up() if rising else w.down(), ok)
        yield
    under(z > 0, lambda: w.landed(below(z), rise + z))
    under(z < n - 1, lambda: w.landed(above(z), fall + z))
    under(z == 0, lambda: add_up(out, own(z), above(z)))
    under(z == n - 1, lambda: add_up(out, own(z), below(z)))
    under(
        jnp.logical_and(z > 0, z < n - 1), lambda: add_up(out, own(z), below(z), above(z))
    )


def planes(w):
    z, n = w.z, w.levels
    for k in range(n - 1):
        falling = n - 1 - k
        low_half = jnp.where(falling > z, falling, falling - 1)
        high_half = jnp.where(k < z, k, k + 1)
        yield jnp.where(z < n // 2, low_half, high_half)
    yield z


def scatter_all(w, part, landing, own, core, half_x, half_y, full_x, full_y, below, above, out, make=None):
    z, y, x, c, n = w.z, w.y, w.x, w.c, w.levels
    to_core, to_hx, to_hy, to_fx, to_fy = (w.take(4 * n), w.take(n), w.take(n), w.take(n), w.take(n))
    rise, fall = w.take(n), w.take(n)
    from_part, from_landing = w.take_local(4 * n), w.take_local(4 * n)
    rows = own.shape[1]
    cut = rows // 2 // CHUNK * CHUNK
    first, second = pl.ds(0, cut), pl.ds(cut, rows - cut)
    kinds = ((1 - y, 1 - x), (1 - y, x), (y, 1 - x), (y, x))
    order = list(planes(w))
    kept = {}

    def start(k):
        zs = order[k]
        for kind, (ys, xs) in enumerate(kinds):
            here = k * 4 + kind
            lane = to_core + here
            w.send(part.at[flat(zs, ys, xs, 1 - c)], landing.at[here], lane, lane, w.over_core())
            kept[here] = pltpu.make_async_copy(
                part.at[flat(zs, ys, xs, c)], own.at[here], w.locals.at[from_part + here]
            )
            kept[here].start()

    def join(k):
        loads = []
        for kind in range(4):
            here = k * 4 + kind
            w.landed(landing.at[here], to_core + here)
            load = pltpu.make_async_copy(landing.at[here], core.at[kind], w.locals.at[from_landing + here])
            load.start()
            loads.append(load)
        for kind in range(4):
            here = k * 4 + kind
            kept[here].wait()
            loads[kind].wait()
            add_up(own.at[here], own.at[here], core.at[kind])
            if kind == 0:
                w.send(own.at[here, first], half_x.at[k], to_hx + k, to_hx + k, w.over_x())
                w.send(own.at[here, second], half_y.at[k], to_hy + k, to_hy + k, w.over_y())

    def across(k):
        here = k * 4 + 1
        w.landed(half_x.at[k], to_hx + k)
        add_up(own.at[here, first], own.at[here, first], half_x.at[k])
        w.send(own.at[here], full_y.at[k], to_fy + k, to_fy + k, w.over_y())
        here = k * 4 + 2
        w.landed(half_y.at[k], to_hy + k)
        add_up(own.at[here, second], own.at[here, second], half_y.at[k])
        w.send(own.at[here], full_x.at[k], to_fx + k, to_fx + k, w.over_x())

    def along(k):
        zs, here = order[k], own.at[k * 4 + 3]
        w.landed(full_x.at[k], to_fx + k)
        w.landed(full_y.at[k], to_fy + k)
        if k == n - 1:
            add_up(here, here, full_x.at[k], full_y.at[k])
            return
        rising, falling = zs > z, zs < z
        more_up, more_down = jnp.logical_and(rising, z > 0), jnp.logical_and(falling, z < n - 1)

        def take_below():
            w.landed(below.at[zs - 1], rise + zs)
            add_up(here, here, full_x.at[k], full_y.at[k], below.at[zs - 1])

        def take_above():
            w.landed(above.at[zs], fall + zs)
            add_up(here, here, full_x.at[k], full_y.at[k], above.at[zs])

        under(more_up, take_below)
        under(more_down, take_above)
        under(
            jnp.logical_not(jnp.logical_or(more_up, more_down)),
            lambda: add_up(here, here, full_x.at[k], full_y.at[k]),
        )
        w.send(here, below.at[zs - 1], rise + zs, rise + zs, w.up(), rising)
        w.send(here, above.at[zs], fall + zs, fall + zs, w.down(), falling)

    for k in range(n + 3):
        if make is not None:
            yield from make(k)
        if k < n:
            start(k)
            yield
        for lag, act in ((1, join), (2, across), (3, along)):
            if 0 <= k - lag < n:
                act(k - lag)
                yield
    here = own.at[4 * n - 1]
    under(z > 0, lambda: w.landed(below.at[z - 1], rise + z))
    under(z < n - 1, lambda: w.landed(above.at[z], fall + z))
    under(z == 0, lambda: add_up(out, here, above.at[z]))
    under(z == n - 1, lambda: add_up(out, here, below.at[z - 1]))
    under(jnp.logical_and(z > 0, z < n - 1), lambda: add_up(out, here, below.at[z - 1], above.at[z]))


def scatter_all_scratch(n, rows, columns):
    cut = rows // 2 // CHUNK * CHUNK
    shapes = [(4 * n, rows), (4, rows), (n, cut), (n, rows - cut)] + [(n, rows)] * 2 + [(n - 1, rows)] * 2
    return [pltpu.VMEM(shape + (columns,), jnp.bfloat16) for shape in shapes]


def scatter_dp(w, part, own, over, below, above, out):
    z, y, n = w.z, w.y, w.levels
    by_y, spare = w.take(n), w.take_local(n)
    kept = []
    order = []
    for step in range(n - 1, 0, -1):
        order += [side for side in sides(w, step)]
    order.append((True, z, True))
    for _, zs, ok in order:
        w.send(part.at[zs * 2 + 1 - y], over.at[zs], by_y + zs, by_y + zs, w.over_y(), ok)
        made = pltpu.make_async_copy(part.at[zs * 2 + y], own.at[zs], w.locals.at[spare + zs])
        under(ok, made.start)
        kept.append(made)
    yield
    for made, (_, zs, ok) in zip(kept, order):

        def act():
            made.wait()
            w.landed(over.at[zs], by_y + zs)
            add_up(own.at[zs], own.at[zs], over.at[zs])

        under(ok, act)
    yield
    yield from chain_z(
        w, lambda zt: own.at[zt], lambda zt: below.at[zt], lambda zt: above.at[zt], out
    )


def scatter_mp(w, part, own, first, second, out):
    x, c = w.x, w.c
    core, cross = w.take(2), w.take()
    kept = []
    for i, xs in enumerate((1 - x, x)):
        w.send(part.at[xs * 2 + 1 - c], first.at[i], core + i, core + i, w.over_core())
        kept.append(w.local(part.at[xs * 2 + c], own.at[i]))
    kept[0].wait()
    w.landed(first.at[0], core)
    add_up(own.at[0], own.at[0], first.at[0])
    w.send(own.at[0], second, cross, cross, w.over_x())
    kept[1].wait()
    w.landed(first.at[1], core + 1)
    w.landed(second, cross)
    add_up(out, own.at[1], first.at[1], second)


VMEM = 62 * MIB
ANY = pl.BlockSpec(memory_space=pl.ANY)
WHOLE = pl.BlockSpec(memory_space=pltpu.VMEM)


def call(kernel, identity, arrays, outs, scratch, signals, locals_, in_vmem=False, name=None):
    return pl.pallas_call(
        kernel,
        out_shape=[jax.ShapeDtypeStruct(shape, kind) for shape, kind, _ in outs],
        in_specs=[ANY] * len(arrays),
        out_specs=[WHOLE if near else ANY for _, _, near in outs],
        scratch_shapes=list(scratch)
        + [
            pltpu.SemaphoreType.DMA((signals,)),
            pltpu.SemaphoreType.DMA((signals,)),
            pltpu.SemaphoreType.DMA((max(locals_, 1),)),
        ],
        compiler_params=pltpu.CompilerParams(
            collective_id=identity, has_side_effects=True, vmem_limit_bytes=VMEM
        ),
        name=name,
    )(*arrays)


def halves(block):
    rows = block.shape[0]
    cut = rows // 2 // CHUNK * CHUNK
    return (block.at[pl.ds(0, cut)], block.at[pl.ds(cut, rows - cut)])


def by_x_last(block):
    return (None, block)


def rows_of(ref, index, rows):
    return ref.at[pl.ds(pl.multiple_of(index * rows, rows), rows)]


def columns_of(ref, index, columns):
    return ref.at[:, pl.ds(pl.multiple_of(index * columns, columns), columns)]


def flat(z, y, x, c):
    return (z * 2 + y) * 4 + x * 2 + c


def begin(levels, tensors):
    names = list(vars(tensors))
    count = 2 * levels
    wide = tensors.query_weight.shape[1]
    unit = tensors.gate_weight.shape[1] // count
    deep = tensors.gate_weight.shape[0] * count
    rows = tensors.layer_input.shape[0]
    packed = tensors.maps.shape
    low = tensors.gate_expand.shape[0] * count
    piece = deep // 4
    shapes = dict(
        layer_input=(4, rows, deep),
        maps=(4 * count * packed[0], packed[1]),
        output_expand=(low, deep),
        down_expand=(low, deep),
        query_weight=(deep, wide),
        output_weight=(wide, deep),
        expands=(low, tensors.expands.shape[1]),
        output_shrink=(tensors.output_shrink.shape[0] * count, low),
        output_grad=(4 * count, rows, deep),
        gate_weight=(deep, unit),
        up_weight=(deep, unit),
        down_weight=(unit, deep),
        gate_expand=(low, unit),
        up_expand=(low, unit),
    )

    def kernel(*refs):
        given = SimpleNamespace(**dict(zip(names, refs)))
        got = SimpleNamespace(**dict(zip(shapes, refs[len(names) :])))
        w = Wires(levels, *refs[len(names) + len(shapes) :])
        w.greet(far=True)

        def expand_at(into):
            def at(z, y, x, c):
                return into.at[
                    pl.ds(pl.multiple_of((z * 2 + y) * (low // count), low // count), low // count),
                    pl.ds(pl.multiple_of((x * 2 + c) * piece, piece), piece),
                ]

            return at

        steps = [
            gather_mp(w, given.layer_input, lambda x, c: got.layer_input.at[x * 2 + c]),
            gather_dp(w, given.query_weight, lambda z, y: rows_of(got.query_weight, z * 2 + y, deep // count)),
            gather_dp(w, given.output_weight, lambda z, y: columns_of(got.output_weight, z * 2 + y, deep // count)),
            gather_all(w, given.maps, lambda z, y, x, c: rows_of(got.maps, flat(z, y, x, c), packed[0]), halves),
            gather_dp(w, given.expands, lambda z, y: rows_of(got.expands, z * 2 + y, low // count)),
            gather_dp(
                w,
                given.output_shrink,
                lambda z, y: rows_of(got.output_shrink, z * 2 + y, given.output_shrink.shape[0]),
            ),
        ]
        for own, into in ((given.output_expand, got.output_expand), (given.down_expand, got.down_expand)):
            steps.append(gather_all(w, columns_of(own, w.mp, piece), expand_at(into), halves))
        steps.append(gather_all(w, given.output_grad, lambda z, y, x, c: got.output_grad.at[flat(z, y, x, c)], halves))
        after = [
            exchange_dp(w, lambda dp: columns_of(given.gate_weight, dp, unit), lambda dp: rows_of(got.gate_weight, dp, deep // count)),
            exchange_dp(w, lambda dp: columns_of(given.up_weight, dp, unit), lambda dp: rows_of(got.up_weight, dp, deep // count)),
            exchange_dp(w, lambda dp: rows_of(given.down_weight, dp, unit), lambda dp: columns_of(got.down_weight, dp, deep // count)),
            exchange_dp(w, lambda dp: columns_of(given.gate_expand, dp, unit), lambda dp: rows_of(got.gate_expand, dp, low // count)),
            exchange_dp(w, lambda dp: columns_of(given.up_expand, dp, unit), lambda dp: rows_of(got.up_expand, dp, low // count)),
        ]
        turn(steps, after)
        w.finish()

    kind = jnp.bfloat16
    given = call(
        kernel,
        0,
        list(vars(tensors).values()),
        [(shape, kind, False) for shape in shapes.values()],
        [],
        64 * levels + 48 * levels * 3,
        32,
        name="begin",
    )
    return SimpleNamespace(**dict(zip(shapes, given)))


def spread(levels, rows):
    here, wide = rows.shape

    def kernel(own, out, *sems):
        w = Wires(levels, *sems)
        w.greet()
        turn([gather_all(w, own, lambda z, y, x, c: out.at[flat(z, y, x, c)], halves)])
        w.finish()

    (out,) = call(
        kernel, 1, [rows], [((8 * levels, here, wide), rows.dtype, False)], [], 40 * levels, 4, name="spread"
    )
    return out


def gelu_pair(gate):
    inner = GELU * (gate + 0.044715 * gate * gate * gate)
    bend = jnp.tanh(inner)
    slope = GELU * (1.0 + 3.0 * 0.044715 * gate * gate)
    return 0.5 * gate * (1.0 + bend), 0.5 * (1.0 + bend) + 0.5 * gate * (1.0 - bend * bend) * slope


GELU = (2.0 / math.pi) ** 0.5
TALL = 256


def feed(levels, rows, tokens, grads, gate_up, down):
    deep, both = gate_up.shape
    unit = both // 2
    total = tokens.shape[0]
    level = total // levels
    count = 2 * levels
    strip = deep // count
    half = total // 2
    steps = level // TALL
    kind = jnp.bfloat16
    scratch = scatter_all_scratch(levels, rows, deep)
    each = len(scratch)

    def kernel(tokens_ref, grads_ref, gate_up_hbm, down_hbm, *refs):
        grad_out, branch_out, pair_hbm, single_hbm, gate_own, up_own, down_own = refs[:7]
        hidden_hbm, pre_hbm, grad_part, branch_part, grad_land, branch_land = refs[7:13]
        buffers = refs[13:]
        one, two = buffers[:each], buffers[each : 2 * each - 1]
        two = two[:1] + (one[1],) + two[1:]
        gate_up_ref, down_ref, arena, hidden_stage, pre_stage, columns, down_stage, loads, stores = buffers[
            2 * each - 1 : -3
        ]

        def space(number, slot):
            return arena.at[pl.ds(pl.multiple_of((2 * number + slot) * TALL, TALL), TALL)]

        w = Wires(levels, *buffers[-3:])
        weights = [w.local(gate_up_hbm, gate_up_ref), w.local(down_hbm, down_ref)]
        order = list(planes(w))

        def load(k, j, slot):
            start = pl.ds(pl.multiple_of(order[k] * level + j * TALL, TALL), TALL)
            return (
                pltpu.make_async_copy(tokens_ref.at[start], space(0, slot), loads.at[0, slot]),
                pltpu.make_async_copy(grads_ref.at[start], space(1, slot), loads.at[1, slot]),
            )

        def store(k, j, slot):
            start = pl.multiple_of(order[k] * level + j * TALL, TALL)
            block = order[k] * (level // rows) + j * (TALL // rows)
            made = [
                pltpu.make_async_copy(hidden_stage.at[slot], hidden_hbm.at[pl.ds(start, TALL)], stores.at[0, slot]),
                pltpu.make_async_copy(pre_stage.at[slot], pre_hbm.at[pl.ds(start, TALL)], stores.at[1, slot]),
            ]
            for i in range(TALL // rows):
                piece = pl.ds(i * rows, rows)
                made += [
                    pltpu.make_async_copy(space(2, slot).at[piece], grad_part.at[block + i], stores.at[2 + 2 * i, slot]),
                    pltpu.make_async_copy(space(3, slot).at[piece], branch_part.at[block + i], stores.at[3 + 2 * i, slot]),
                ]
            return made

        for copy in load(0, 0, 0):
            copy.start()
        w.greet(far=True)
        for copy in weights:
            copy.wait()

        lanes = w.take(3 * count)

        def there(i):
            return lax.rem(w.dp + 1 + i, count)

        def strip_of(ref, i):
            return columns_of(ref, there(i), strip)

        def strip_load(ref, i):
            slot = lax.rem(i, 2)
            return pltpu.make_async_copy(strip_of(ref, i), columns.at[slot], loads.at[0, slot])

        def pair_store(i):
            slot = lax.rem(i, 2)
            return pltpu.make_async_copy(pre_stage.at[slot], rows_of(pair_hbm, there(i), strip), stores.at[0, slot])

        def single_store(i):
            slot = lax.rem(i, 2)
            return pltpu.make_async_copy(down_stage.at[slot], strip_of(single_hbm, i), stores.at[1, slot])

        def pair_pieces(i):
            both_rows = rows_of(pair_hbm, there(i), strip)
            yield both_rows.at[:, pl.ds(0, unit)], columns_of(gate_own, w.dp, unit), lanes + i
            yield both_rows.at[:, pl.ds(unit, unit)], columns_of(up_own, w.dp, unit), lanes + count + i

        def single_pieces(i):
            yield strip_of(single_hbm, i), rows_of(down_own, w.dp, unit), lanes + 2 * count + i

        def give(pieces, i):
            for source, target, lane in pieces(i):
                w.copy(source, target, lane, lane, (there(i), w.mp)).start()

        def keep(pieces):
            for source, target, _ in pieces(count - 1):
                w.local(source, target).wait()

        def product(left, right, left_wide, right_wide):
            return sum(
                lax.dot_general(
                    left[pl.ds(0, half), pl.ds(i * left_wide[0], left_wide[1])] if left_wide[0] else left[pl.ds(i * half, half), :],
                    right[pl.ds(0, half), pl.ds(i * right_wide[0], right_wide[1])] if right_wide[0] else right[pl.ds(i * half, half), :],
                    (((0,), (0,)), ((), ())),
                    preferred_element_type=jnp.float32,
                )
                for i in range(2)
            )

        def pair_strip(i, carry):
            slot = lax.rem(i, 2)
            strip_load(tokens_ref, i).wait()

            @pl.when(i < count - 1)
            def _():
                strip_load(tokens_ref, i + 1).start()

            @pl.when(i == count - 1)
            def _():
                strip_load(grads_ref, count - 1 - i).start()

            pre_stage[slot] = product(columns.at[slot], arena, (0, 0), (both, both)).astype(kind)
            pair_store(i).start()

            @pl.when(i > 0)
            def _():
                pair_store(i - 1).wait()
                give(pair_pieces, i - 1)

            return carry

        def single_strip(i, carry):
            slot = lax.rem(i, 2)
            strip_load(grads_ref, i).wait()

            @pl.when(i < count - 1)
            def _():
                strip_load(grads_ref, i + 1).start()

            down_stage[slot] = product(gate_up_ref, columns.at[slot], (unit, unit), (0, 0)).astype(kind)
            single_store(i).start()

            @pl.when(i > 0)
            def _():
                single_store(i - 1).wait()
                give(single_pieces, i - 1)

            return carry

        def gradients(k):
            if k == levels:
                held = []
                for i in range(2):
                    piece = pl.ds(i * half, half)
                    held.append(w.local(pre_hbm.at[piece], arena.at[:, pl.ds(i * both, both)]))
                    held.append(w.local(hidden_hbm.at[piece], gate_up_ref.at[:, pl.ds(i * unit, unit)]))
                strip_load(tokens_ref, 0).start()
                for copy in held:
                    copy.wait()
                lax.fori_loop(0, count // 2, pair_strip, 0)
            if k == levels + 1:
                lax.fori_loop(count // 2, count, pair_strip, 0)
                pair_store(count - 1).wait()
                keep(pair_pieces)
            if k == levels + 2:
                lax.fori_loop(0, count, single_strip, 0)
                single_store(count - 1).wait()
                keep(single_pieces)

        def make(k):
            if k >= levels:
                gradients(k)
                yield
                return

            def chunk(j, carry):
                slot = lax.rem(j, 2)
                for copy in load(k, j, slot):
                    copy.wait()

                @pl.when(j < steps - 1)
                def _():
                    for copy in load(k, j + 1, 1 - slot):
                        copy.start()

                if k < levels - 1:

                    @pl.when(j == steps - 1)
                    def _():
                        for copy in load(k + 1, 0, 0):
                            copy.start()

                @pl.when(j >= 2)
                def _():
                    for copy in store(k, j - 2, slot):
                        copy.wait()

                pre = jnp.dot(space(0, slot)[...], gate_up_ref[...], preferred_element_type=jnp.float32)
                back = against(space(1, slot)[...], down_ref[...])
                gate, up = pre[:, :unit], pre[:, unit:]
                bent, slope = gelu_pair(gate)
                hidden = (bent * up).astype(kind)
                grad_pre = jnp.concatenate([back * up * slope, back * bent], axis=1).astype(kind)
                hidden_stage[slot] = hidden
                pre_stage[slot] = grad_pre
                space(2, slot)[...] = against(grad_pre, gate_up_ref[...]).astype(kind)
                space(3, slot)[...] = jnp.dot(hidden, down_ref[...], preferred_element_type=jnp.float32).astype(kind)
                for copy in store(k, j, slot):
                    copy.start()
                return carry

            lax.fori_loop(0, steps, chunk, 0)
            for j in range(max(steps - 2, 0), steps):
                for copy in store(k, j, j % 2):
                    copy.wait()
            yield

        def idle(k):
            yield

        turn(
            [
                scatter_all(w, grad_part, grad_land, *one, grad_out, make=make),
                scatter_all(w, branch_part, branch_land, *two, branch_out, make=idle),
            ]
        )
        for i in range(count - 1):
            source = lax.rem(w.dp + count - 1 - i, count)
            for sent, (_, _, lane) in zip(
                (columns_of(gate_own, source, unit), columns_of(up_own, source, unit), rows_of(down_own, source, unit)),
                (*pair_pieces(i), *single_pieces(i)),
            ):
                w.landed(sent, lane)
                w.copy(sent, sent, lane, lane, w.over_x()).wait_send()
        w.finish()

    assert total == 2 * deep and 2 * both == deep and 8 * TALL == deep and strip == TALL
    tall = [(deep, deep), (2, TALL, unit), (2, TALL, both), (2, total, strip), (2, unit, strip)]
    outs = [((rows, deep), jnp.float32, True)] * 2
    outs += [((deep, both), kind, False), ((unit, deep), kind, False)]
    outs += [((strip, unit * count), kind, False)] * 2 + [((unit * count, strip), kind, False)]
    outs += [((total, unit), kind, False), ((total, both), kind, False)]
    outs += [((total // rows, rows, deep), kind, False)] * 2 + [((4 * levels, rows, deep), kind, False)] * 2
    made = call(
        kernel,
        2,
        [tokens, grads, gate_up, down],
        outs,
        scratch
        + scratch[:1]
        + scratch[2:]
        + [pltpu.VMEM(gate_up.shape, kind), pltpu.VMEM(down.shape, kind)]
        + [pltpu.VMEM(shape, kind) for shape in tall]
        + [pltpu.SemaphoreType.DMA((2, 2)), pltpu.SemaphoreType.DMA((2 + 2 * (TALL // rows), 2))],
        2 * 10 * levels + 6 * levels + 4,
        16 * levels + 12,
        name="feed",
    )
    return made[:7]


def share_mp(levels, rows):
    def kernel(own, out, *sems):
        w = Wires(levels, *sems)
        w.greet(flat=True)
        turn([gather_mp(w, own, lambda x, c: out.at[x * 2 + c])])
        w.finish()

    (out,) = call(kernel, 3, [rows], [((4,) + rows.shape, rows.dtype, False)], [], 16, 4, name="share_mp")
    return out


def sum_mp(levels, part):
    _, here, wide = part.shape

    def kernel(given, out, own, first, second, *sems):
        w = Wires(levels, *sems)
        w.greet(flat=True)
        scatter_mp(w, given, own, first, second, out)
        w.finish()

    (out,) = call(
        kernel,
        4,
        [part],
        [((here, wide), jnp.float32, True)],
        [pltpu.VMEM((2, here, wide), part.dtype)] * 2 + [pltpu.VMEM((here, wide), part.dtype)],
        16,
        4,
        name="sum_mp",
    )
    return out


BACK = 4


def end(levels, small, split, units, share):
    names = list(vars(units))
    count = 2 * levels
    low, unit = units.gate_expand.shape
    shapes = dict(
        gate_expand=(low // count, unit * count),
        up_expand=(low // count, unit * count),
    )
    few, wide = small.shape[1:]
    many, flatly = split.shape[1:]
    scratch = scatter_all_scratch(levels, few, wide)
    scratch += [pltpu.VMEM((levels, many, flatly), jnp.bfloat16)] * 4
    first = len(names) + 2

    def kernel(*refs):
        small_ref, split_ref = refs[:2]
        given = SimpleNamespace(**dict(zip(names, refs[2:])))
        got = SimpleNamespace(**dict(zip(shapes, refs[first:])))
        after = first + len(shapes)
        small_out, split_out, shared, landing = refs[after : after + 4]
        buffers = refs[after + 4 : -3]
        w = Wires(levels, *refs[-3:])
        w.greet(far=True)

        def over_all():
            yield from scatter_all(w, small_ref, landing, *buffers[:8], small_out)
            mine = small_out.at[:, pl.ds(wide - share, share)]
            yield from gather_mp(w, mine, lambda x, c: shared.at[x * 2 + c])

        steps = [
            scatter_dp(w, split_ref, *buffers[8:], split_out),
            over_all(),
        ]
        after = [
            exchange_dp(w, lambda dp: rows_of(given.gate_expand, dp, low // count), lambda dp: columns_of(got.gate_expand, dp, unit)),
            exchange_dp(w, lambda dp: rows_of(given.up_expand, dp, low // count), lambda dp: columns_of(got.up_expand, dp, unit)),
        ]
        turn(steps, after, BACK)
        w.finish()

    outs = [(shape, jnp.bfloat16, False) for shape in shapes.values()]
    outs += [((few, wide), jnp.float32, True), ((many, flatly), jnp.float32, True), ((4, few, share), jnp.float32, True), ((4 * levels, few, wide), jnp.bfloat16, False)]
    made = call(
        kernel,
        5,
        [small, split] + list(vars(units).values()),
        outs,
        scratch,
        32 * levels,
        9 * levels + 16,
        name="end",
    )
    return SimpleNamespace(**dict(zip(shapes, made))), made[-4], made[-3], made[-2]


def low(rows):
    return rows.astype(jnp.bfloat16)


def unit_rows(rows):
    scale = lax.rsqrt(jnp.mean(rows * rows, axis=-1, keepdims=True) + EPS)
    return rows * scale, scale


def norm_back(grad, normed, scale):
    return scale * (grad - normed * jnp.mean(grad * normed, axis=-1, keepdims=True))


def by_unit(
    levels,
    layer_input,
    output_grad,
    attention_gain,
    query_weight,
    key_weight,
    value_weight,
    output_weight,
    query_shrink,
    query_expand,
    key_shrink,
    key_expand,
    value_shrink,
    value_expand,
    output_shrink,
    output_expand,
    feedforward_gain,
    gate_weight,
    up_weight,
    down_weight,
    gate_shrink,
    gate_expand,
    up_shrink,
    up_expand,
    down_shrink,
    down_expand,
    group_ids,
    positions,
    segments,
):
    count = 2 * levels
    rows = layer_input.shape[0]
    tokens = 4 * rows
    deep = layer_input.shape[1]
    head = key_weight.shape[1]
    heads = query_weight.shape[1] // head
    rank = query_expand.shape[0] * count
    mp = lax.axis_index("mp")
    share = query_shrink.shape[0] // 4

    gains = jnp.stack([attention_gain, feedforward_gain], axis=1)
    gains = jnp.pad(gains, ((0, 0), (0, 126)))
    maps = jnp.concatenate(
        [key_weight, value_weight, query_shrink, key_shrink, value_shrink, gate_shrink, up_shrink, gains],
        axis=1,
    )
    maps = lax.dynamic_slice_in_dim(maps, mp * share, share, 0)
    expands = jnp.concatenate([query_expand, key_expand, value_expand], axis=1)
    got = begin(
        levels,
        SimpleNamespace(
            layer_input=layer_input,
            maps=maps,
            output_expand=output_expand,
            down_expand=down_expand,
            query_weight=query_weight,
            output_weight=output_weight,
            expands=expands,
            output_shrink=output_shrink,
            output_grad=output_grad,
            gate_weight=gate_weight,
            up_weight=up_weight,
            down_weight=down_weight,
            gate_expand=gate_expand,
            up_expand=up_expand,
        ),
    )
    maps = got.maps
    key_w, value_w = maps[:, :head], maps[:, head : 2 * head]
    query_a, key_a, value_a, gate_a, up_a = (
        maps[:, 2 * head + i * rank : 2 * head + (i + 1) * rank] for i in range(5)
    )
    gain_one = maps[:, 2 * head + 5 * rank : 2 * head + 5 * rank + 1].astype(jnp.float32)
    gain_two = maps[:, 2 * head + 5 * rank + 1 : 2 * head + 5 * rank + 2].astype(jnp.float32)
    query_b = got.expands[:, : heads * head]
    key_b = got.expands[:, heads * head : (heads + 1) * head]
    value_b = got.expands[:, (heads + 1) * head :]
    output_a, output_b = got.output_shrink, got.output_expand
    query_full = low(gain_one * (got.query_weight.astype(jnp.float32) + matmul(query_a, query_b)))
    key_full = low(gain_one * (key_w.astype(jnp.float32) + matmul(key_a, key_b)))
    value_full = low(gain_one * (value_w.astype(jnp.float32) + matmul(value_a, value_b)))
    inward = jnp.concatenate([query_full, key_full, value_full], axis=1)
    outward = low(got.output_weight.astype(jnp.float32) + matmul(output_a, output_b))

    allowed = (
        (group_ids[:, None] == group_ids[None, :])
        & (positions[None, :] <= positions[:, None])
        & ((segments[None, :] == 0) | (segments[None, :] == segments[:, None]))
    )
    group_rows = got.layer_input.reshape(tokens, deep).astype(jnp.float32)
    normed = low(unit_rows(group_rows)[0])
    lin = matmul(normed, inward)
    wide = heads * head
    queries = low(rotary(lin[:, :wide].reshape(tokens, heads, head), positions, 1.0) * head ** (-0.5))
    keys = low(rotary(lin[:, None, wide : wide + head], positions, 1.0)[:, 0, :])
    values = low(lin[:, wide + head :])
    scores = jnp.einsum("thd,sd->hts", queries, keys, preferred_element_type=jnp.float32)
    scores = jnp.where(allowed[None], scores, -1e30)
    expo = jnp.exp(scores - jnp.max(scores, axis=-1, keepdims=True))
    probability = expo / jnp.sum(expo, axis=-1, keepdims=True)
    probability_low = low(probability)
    mixed = low(
        jnp.einsum("hts,sd->thd", probability_low, values, preferred_element_type=jnp.float32)
    ).reshape(tokens, wide)
    branch = sum_mp(levels, low(matmul(mixed, outward)).reshape(4, rows, deep))
    own_rows = layer_input.astype(jnp.float32)
    middle = own_rows + branch

    gate_up = low(
        gain_two
        * (
            jnp.concatenate([got.gate_weight, got.up_weight], axis=1).astype(jnp.float32)
            + jnp.concatenate([matmul(gate_a, got.gate_expand), matmul(up_a, got.up_expand)], axis=1)
        )
    )
    unit = got.gate_weight.shape[1]
    down_a, down_b = down_shrink, got.down_expand
    down_full = low(got.down_weight.astype(jnp.float32) + matmul(down_a, down_b))
    normed_middle, scale_middle = unit_rows(middle)
    normed_all = spread(levels, low(normed_middle)).reshape(4 * count * rows, deep)
    grads = got.output_grad.reshape(4 * count * rows, deep)
    grad_normed, branch, pair_grad, down_grad_low, gate_own, up_own, down_own = feed(levels, rows, normed_all, grads, gate_up, down_full)
    result = low(middle + branch)
    grad_middle = output_grad.astype(jnp.float32) + norm_back(grad_normed, normed_middle, scale_middle)

    feed_gain = (
        jnp.sum(pair_grad.astype(jnp.float32) * gate_up.astype(jnp.float32), axis=1, keepdims=True) / gain_two
    )
    down_shrink_grad = against(down_grad_low, down_b)
    down_b_part = outer_sum(down_a, down_grad_low)
    gate_b_grad = low(outer_sum(low(gain_two * gate_a.astype(jnp.float32)), pair_grad[:, :unit]))
    up_b_grad = low(outer_sum(low(gain_two * up_a.astype(jnp.float32)), pair_grad[:, unit:]))
    gate_a_part = gain_two * against(pair_grad[:, :unit], got.gate_expand)
    up_a_part = gain_two * against(pair_grad[:, unit:], got.up_expand)

    grad_branch = share_mp(levels, low(grad_middle)).reshape(tokens, deep)
    output_grad_w = outer_sum(mixed, grad_branch)
    grad_mixed = low(against(grad_branch, outward)).reshape(tokens, heads, head)
    grad_values = jnp.einsum("hts,thd->sd", probability_low, grad_mixed, preferred_element_type=jnp.float32)
    grad_probability = jnp.einsum("thd,sd->hts", grad_mixed, values, preferred_element_type=jnp.float32)
    grad_scores = low(
        probability * (grad_probability - jnp.sum(probability * grad_probability, axis=-1, keepdims=True))
    )
    grad_queries = jnp.einsum("hts,sd->thd", grad_scores, keys, preferred_element_type=jnp.float32)
    grad_keys = jnp.einsum("hts,thd->sd", grad_scores, queries, preferred_element_type=jnp.float32)
    grad_query = rotary(grad_queries * head ** (-0.5), positions, -1.0).reshape(tokens, wide)
    grad_key = rotary(grad_keys[:, None, :], positions, -1.0)[:, 0, :]
    grad_lin = low(jnp.concatenate([grad_query, grad_key, grad_values], axis=1))
    grad_rows = sum_mp(levels, low(against(grad_lin, inward)).reshape(4, rows, deep))
    normed_own, scale_own = unit_rows(own_rows)
    input_grad = grad_middle + norm_back(grad_rows, normed_own, scale_own)

    lin_normed = outer_sum(normed, grad_lin)
    attention_gain_part = jnp.sum(lin_normed * inward.astype(jnp.float32), axis=1, keepdims=True) / gain_one
    lin_grad = low(lin_normed * gain_one)
    query_part, key_part, value_part = (
        lin_grad[:, :wide],
        lin_grad[:, wide : wide + head],
        lin_grad[:, wide + head :],
    )
    query_b_part = outer_sum(query_a, query_part)
    key_b_part = outer_sum(key_a, key_part)
    value_b_part = outer_sum(value_a, value_part)
    query_a_part = against(query_part, query_b)
    output_low = low(output_grad_w)
    output_a_part = against(output_low, output_b)
    output_b_part = outer_sum(output_a, output_low)

    def by_device(array):
        return low(array).reshape(4 * count, array.shape[0] // (4 * count), array.shape[1])

    def fold(array):
        return by_device(array).reshape(4 * count, share, -1)

    def fold_wide(array):
        cut = low(array).reshape(count, array.shape[0] // count, 4, array.shape[1] // 4)
        return cut.transpose(0, 2, 1, 3).reshape(4 * count, share, -1)

    gain_part = jnp.pad(jnp.concatenate([attention_gain_part, feed_gain], axis=1), ((0, 0), (0, 62)))
    small = jnp.concatenate(
        [
            by_device(key_part),
            by_device(value_part),
            by_device(query_a_part),
            by_device(gate_a_part),
            by_device(up_a_part),
            by_device(gain_part),
            fold(key_b_part),
            fold(value_b_part),
            fold_wide(output_b_part),
            fold_wide(down_b_part),
        ],
        axis=2,
    )
    split = jnp.concatenate(
        [
            low(query_part).reshape(count, -1, wide),
            output_low.reshape(wide, count, deep // count).transpose(1, 0, 2).reshape(count, -1, wide),
            low(query_b_part).reshape(count, -1, wide),
            low(output_a_part).reshape(count, -1, wide),
        ],
        axis=1,
    )
    wide_share = 2 * (rank // count) * (deep // 4) // share
    units, few, many, shared = end(
        levels,
        small,
        split,
        SimpleNamespace(
            gate_expand=gate_b_grad,
            up_expand=up_b_grad,
        ),
        wide_share,
    )
    key_own, value_own = few[:, :head], few[:, head : 2 * head]
    query_a_own, gate_a_own, up_a_own = (
        few[:, 2 * head + i * rank : 2 * head + (i + 1) * rank] for i in range(3)
    )
    place = 2 * head + 3 * rank
    key_b_own = few[:, place + 64 : place + 96].reshape(-1, head)
    value_b_own = few[:, place + 96 : place + 128].reshape(-1, head)
    half = wide_share // 2

    def unfold(array):
        return array.reshape(4, rank // count, deep // 4).transpose(1, 0, 2).reshape(-1, deep)

    key_a_own = against(low(key_own), key_b)
    value_a_own = against(low(value_own), value_b)
    first = query_weight.shape[0]
    second = first + output_weight.size // wide
    third = second + query_expand.shape[0]
    wider = jnp.float32
    own_gain = feedforward_gain.astype(wider)[:, None]
    return (
        result,
        input_grad,
        few[:, place],
        many[:first],
        key_own,
        value_own,
        many[first:second].reshape(output_weight.shape),
        query_a_own,
        many[second:third],
        key_a_own,
        key_b_own,
        value_a_own,
        value_b_own,
        many[third:].reshape(output_shrink.shape),
        unfold(shared[:, :, :half]),
        few[:, place + 1],
        own_gain * gate_own.astype(wider),
        own_gain * up_own.astype(wider),
        down_own.astype(wider),
        gate_a_own,
        units.gate_expand.astype(wider),
        up_a_own,
        units.up_expand.astype(wider),
        down_shrink_grad,
        unfold(shared[:, :, half:]),
    )


def body(
    layer_input,
    output_grad,
    attention_gain,
    query_weight,
    key_weight,
    value_weight,
    output_weight,
    query_shrink,
    query_expand,
    key_shrink,
    key_expand,
    value_shrink,
    value_expand,
    output_shrink,
    output_expand,
    feedforward_gain,
    gate_weight,
    up_weight,
    down_weight,
    gate_shrink,
    gate_expand,
    up_shrink,
    up_expand,
    down_shrink,
    down_expand,
    group_ids,
    positions,
    segments,
):
    rows_local = layer_input.shape[0]
    own_start = lax.axis_index("mp") * rows_local
    allowed = (
        (group_ids[:, None] == group_ids[None, :])
        & (positions[None, :] <= positions[:, None])
        & ((segments[None, :] == 0) | (segments[None, :] == segments[:, None]))
    )

    def gather_attention():
        return (
            lax.all_gather(attention_gain, "dp", axis=0, tiled=True),
            lax.all_gather(query_weight, "dp", axis=0, tiled=True),
            lax.all_gather(key_weight, "dp", axis=0, tiled=True),
            lax.all_gather(value_weight, "dp", axis=0, tiled=True),
            lax.all_gather(output_weight, "dp", axis=1, tiled=True),
            lax.all_gather(query_shrink, "dp", axis=0, tiled=True),
            lax.all_gather(query_expand, "dp", axis=0, tiled=True),
            lax.all_gather(key_shrink, "dp", axis=0, tiled=True),
            lax.all_gather(key_expand, "dp", axis=0, tiled=True),
            lax.all_gather(value_shrink, "dp", axis=0, tiled=True),
            lax.all_gather(value_expand, "dp", axis=0, tiled=True),
            lax.all_gather(output_shrink, "dp", axis=0, tiled=True),
            lax.all_gather(output_expand, "dp", axis=0, tiled=True),
        )

    def gather_feed():
        return (
            lax.all_gather(feedforward_gain, "dp", axis=0, tiled=True),
            lax.all_gather(gate_weight, "dp", axis=0, tiled=True),
            lax.all_gather(up_weight, "dp", axis=0, tiled=True),
            lax.all_gather(down_weight, "dp", axis=1, tiled=True),
            lax.all_gather(gate_shrink, "dp", axis=0, tiled=True),
            lax.all_gather(gate_expand, "dp", axis=0, tiled=True),
            lax.all_gather(up_shrink, "dp", axis=0, tiled=True),
            lax.all_gather(up_expand, "dp", axis=0, tiled=True),
            lax.all_gather(down_shrink, "dp", axis=0, tiled=True),
            lax.all_gather(down_expand, "dp", axis=0, tiled=True),
        )

    def gather_rows(rows):
        return lax.all_gather(rows, "mp", axis=0, tiled=True)

    def gather_grads(rows):
        return lax.all_gather(rows, "mp", axis=0, tiled=True)

    def scatter_grads(term):
        return lax.psum_scatter(
            term(jnp.int32(0), lax.axis_size("mp") * rows_local),
            "mp",
            scatter_dimension=0,
            tiled=True,
        )

    def project_out(mixed, weight, shrink, expand):
        reduced = lax.psum(matmul(mixed, shrink), "mp").astype(jnp.bfloat16)

        def term(start, count):
            return matmul(mixed, weight)

        branch = lax.psum_scatter(
            term(jnp.int32(0), lax.axis_size("mp") * rows_local),
            "mp",
            scatter_dimension=0,
            tiled=True,
        )
        own = lax.dynamic_slice_in_dim(reduced, own_start, rows_local, 0)
        return (branch + matmul(own, expand), reduced)

    def masked_scores(queries, keys_rot):
        scores = jnp.einsum("thd,sd->hts", queries, keys_rot, preferred_element_type=jnp.float32)
        return jnp.where(allowed[None], scores, -1e30)

    def attention_forward(rows_in, params):
        (
            gain_one,
            w_query,
            w_key,
            w_value,
            w_output,
            query_a,
            query_b,
            key_a,
            key_b,
            value_a,
            value_b,
            output_a,
            output_b,
        ) = params
        normed = gather_rows(norm_rows(rows_in, gain_one.astype(jnp.float32)).astype(jnp.bfloat16))
        tokens = normed.shape[0]
        head_size = w_key.shape[1]
        heads = w_query.shape[1] // head_size
        query_low = matmul(normed, query_a).astype(jnp.bfloat16)
        key_low = matmul(normed, key_a).astype(jnp.bfloat16)
        value_low = matmul(normed, value_a).astype(jnp.bfloat16)
        query_lin = matmul(normed, w_query) + matmul(query_low, query_b)
        key_lin = matmul(normed, w_key) + matmul(key_low, key_b)
        value_lin = matmul(normed, w_value) + matmul(value_low, value_b)
        queries = (
            rotary(query_lin.reshape(tokens, heads, head_size), positions, 1.0)
            * head_size ** (-0.5)
        ).astype(jnp.bfloat16)
        keys_rot = rotary(key_lin[:, None, :], positions, 1.0)[:, 0, :].astype(jnp.bfloat16)
        values = value_lin.astype(jnp.bfloat16)
        scores = masked_scores(queries, keys_rot)
        highest = jnp.max(scores, axis=-1, keepdims=True)
        expo = jnp.exp(scores - highest)
        totals = jnp.sum(expo, axis=-1, keepdims=True)
        probability = expo / totals
        logsum = highest + jnp.log(totals)
        mixed = jnp.einsum(
            "hts,sd->thd",
            probability.astype(jnp.bfloat16),
            values,
            preferred_element_type=jnp.float32,
        )
        mixed = mixed.reshape(tokens, heads * head_size).astype(jnp.bfloat16)
        branch, reduced = project_out(mixed, w_output, output_a, output_b)
        saved = (
            normed,
            query_low,
            key_low,
            value_low,
            queries,
            keys_rot,
            values,
            logsum,
            mixed,
            reduced,
        )
        return (rows_in + branch, saved)

    def feed_forward(middle, params):
        gain_two, w_gate, w_up, w_down, gate_a, gate_b, up_a, up_b, down_a, down_b = params
        normed = gather_rows(norm_rows(middle, gain_two.astype(jnp.float32)).astype(jnp.bfloat16))
        gate_low = matmul(normed, gate_a).astype(jnp.bfloat16)
        up_low = matmul(normed, up_a).astype(jnp.bfloat16)
        gate_pre = matmul(normed, w_gate) + matmul(gate_low, gate_b)
        up_pre = matmul(normed, w_up) + matmul(up_low, up_b)
        hidden = (jax.nn.gelu(gate_pre, approximate=True) * up_pre).astype(jnp.bfloat16)
        branch, reduced = project_out(hidden, w_down, down_a, down_b)
        return (middle + branch, (normed, gate_low, up_low, gate_pre, up_pre, hidden, reduced))

    rows_in = layer_input.astype(jnp.float32)
    attention_params = gather_attention()
    middle, attention_saved = attention_forward(rows_in, attention_params)
    feed_params = gather_feed()
    result, feed_saved = feed_forward(middle, feed_params)
    feed_params = gather_feed()
    feed_saved = feed_forward(middle, feed_params)[1]
    gain_two, w_gate, w_up, w_down, gate_a, gate_b, up_a, up_b, down_a, down_b = feed_params
    normed_feed, gate_low, up_low, gate_pre, up_pre, hidden, reduced_feed = feed_saved
    grad_branch_feed = gather_grads(output_grad)
    down_weight_grad = outer_sum(hidden, grad_branch_feed)
    down_expand_grad = outer_sum(reduced_feed, grad_branch_feed)
    grad_reduced_feed = against(grad_branch_feed, down_b).astype(jnp.bfloat16)
    down_shrink_grad = outer_sum(hidden, grad_reduced_feed)
    grad_hidden = against(grad_branch_feed, w_down) + against(grad_reduced_feed, down_a)
    unused, gelu_pull = jax.vjp(
        lambda gated, upper: jax.nn.gelu(gated, approximate=True) * upper, gate_pre, up_pre
    )
    grad_gate, grad_up = gelu_pull(grad_hidden)
    grad_gate = grad_gate.astype(jnp.bfloat16)
    grad_up = grad_up.astype(jnp.bfloat16)
    gate_expand_grad = outer_sum(gate_low, grad_gate)
    up_expand_grad = outer_sum(up_low, grad_up)
    grad_gate_low = against(grad_gate, gate_b)
    grad_up_low = against(grad_up, up_b)
    feed_wide = normed_feed.astype(jnp.float32)
    gate_shrink_grad = outer_exact(feed_wide, grad_gate_low)
    up_shrink_grad = outer_exact(feed_wide, grad_up_low)
    gate_a_wide = gate_a.astype(jnp.float32)
    up_a_wide = up_a.astype(jnp.float32)

    def feed_term(start, count):

        def pick(rows):
            return rows

        total = against(pick(grad_gate), w_gate) + against(pick(grad_up), w_up)
        return (
            total
            + against_exact(pick(grad_gate_low), gate_a_wide)
            + against_exact(pick(grad_up_low), up_a_wide)
        )

    grad_normed_feed = scatter_grads(feed_term)
    unused, norm_pull = jax.vjp(norm_rows, middle, gain_two.astype(jnp.float32))
    grad_middle_part, feed_gain_grad = norm_pull(grad_normed_feed)
    grad_middle = output_grad.astype(jnp.float32) + grad_middle_part
    gate_weight_grad = outer_sum(normed_feed, grad_gate)
    up_weight_grad = outer_sum(normed_feed, grad_up)
    feed_split = (
        lax.psum_scatter(
            gate_weight_grad.astype(jnp.bfloat16), "dp", scatter_dimension=0, tiled=True
        ).astype(jnp.float32),
        lax.psum_scatter(
            up_weight_grad.astype(jnp.bfloat16), "dp", scatter_dimension=0, tiled=True
        ).astype(jnp.float32),
        lax.psum_scatter(
            down_weight_grad.astype(jnp.bfloat16), "dp", scatter_dimension=1, tiled=True
        ).astype(jnp.float32),
        lax.psum_scatter(
            gate_expand_grad.astype(jnp.bfloat16), "dp", scatter_dimension=0, tiled=True
        ).astype(jnp.float32),
        lax.psum_scatter(
            up_expand_grad.astype(jnp.bfloat16), "dp", scatter_dimension=0, tiled=True
        ).astype(jnp.float32),
        lax.psum_scatter(
            down_shrink_grad.astype(jnp.bfloat16), "dp", scatter_dimension=0, tiled=True
        ).astype(jnp.float32),
        lax.psum_scatter(
            down_expand_grad.astype(jnp.bfloat16), "dp", scatter_dimension=0, tiled=True
        ).astype(jnp.float32),
    )
    gate_weight_own, up_weight_own = (feed_split[0], feed_split[1])
    down_weight_own, gate_expand_own, up_expand_own, down_shrink_own, down_expand_own = (
        feed_split[2],
        feed_split[3],
        feed_split[4],
        feed_split[5],
        feed_split[6],
    )
    feed_shared = (
        lax.psum_scatter(feed_gain_grad, ("dp", "mp"), scatter_dimension=0, tiled=True),
        lax.psum_scatter(gate_shrink_grad, ("dp", "mp"), scatter_dimension=0, tiled=True),
        lax.psum_scatter(up_shrink_grad, ("dp", "mp"), scatter_dimension=0, tiled=True),
    )
    attention_params = gather_attention()
    attention_saved = attention_forward(rows_in, attention_params)[1]
    (
        gain_one,
        w_query,
        w_key,
        w_value,
        w_output,
        query_a,
        query_b,
        key_a,
        key_b,
        value_a,
        value_b,
        output_a,
        output_b,
    ) = attention_params
    normed, query_low, key_low, value_low, queries, keys_rot, values, logsum, mixed, reduced = (
        attention_saved
    )
    tokens = normed.shape[0]
    head_size = w_key.shape[1]
    heads = w_query.shape[1] // head_size
    grad_branch = gather_grads(grad_middle.astype(jnp.bfloat16))
    output_weight_grad = outer_sum(mixed, grad_branch)
    output_expand_grad = outer_sum(reduced, grad_branch)
    grad_reduced = against(grad_branch, output_b).astype(jnp.bfloat16)
    output_shrink_grad = outer_sum(mixed, grad_reduced)
    grad_mixed = (against(grad_branch, w_output) + against(grad_reduced, output_a)).astype(
        jnp.bfloat16
    )
    grad_mixed = grad_mixed.reshape(tokens, heads, head_size)
    probability = jnp.exp(masked_scores(queries, keys_rot) - logsum)
    grad_values = jnp.einsum(
        "hts,thd->sd",
        probability.astype(jnp.bfloat16),
        grad_mixed,
        preferred_element_type=jnp.float32,
    )
    grad_probability = jnp.einsum(
        "thd,sd->hts", grad_mixed, values, preferred_element_type=jnp.float32
    )
    grad_scores = probability * (
        grad_probability - jnp.sum(probability * grad_probability, axis=-1, keepdims=True)
    )
    grad_scores = grad_scores.astype(jnp.bfloat16)
    grad_queries_rot = jnp.einsum(
        "hts,sd->thd", grad_scores, keys_rot, preferred_element_type=jnp.float32
    )
    grad_keys_rot = jnp.einsum(
        "hts,thd->sd", grad_scores, queries, preferred_element_type=jnp.float32
    )
    grad_query = (
        rotary(grad_queries_rot * head_size ** (-0.5), positions, -1.0)
        .reshape(tokens, heads * head_size)
        .astype(jnp.bfloat16)
    )
    grad_key = rotary(grad_keys_rot[:, None, :], positions, -1.0)[:, 0, :]
    normed_wide = normed.astype(jnp.float32)
    query_weight_grad = outer_sum(normed, grad_query)
    query_expand_grad = outer_sum(query_low, grad_query)
    grad_query_low = against(grad_query, query_b)
    query_shrink_grad = outer_exact(normed_wide, grad_query_low)
    key_weight_grad = outer_exact(normed_wide, grad_key)
    key_expand_grad = outer_exact(key_low.astype(jnp.float32), grad_key)
    grad_key_low = against_exact(grad_key, key_b.astype(jnp.float32))
    key_shrink_grad = outer_exact(normed_wide, grad_key_low)
    value_weight_grad = outer_exact(normed_wide, grad_values)
    value_expand_grad = outer_exact(value_low.astype(jnp.float32), grad_values)
    grad_value_low = against_exact(grad_values, value_b.astype(jnp.float32))
    value_shrink_grad = outer_exact(normed_wide, grad_value_low)
    query_a_wide = query_a.astype(jnp.float32)
    key_wide = w_key.astype(jnp.float32)
    key_a_wide = key_a.astype(jnp.float32)
    value_wide = w_value.astype(jnp.float32)
    value_a_wide = value_a.astype(jnp.float32)

    def attention_term(start, count):

        def pick(rows):
            return rows

        total = against(pick(grad_query), w_query) + against_exact(
            pick(grad_query_low), query_a_wide
        )
        total = (
            total
            + against_exact(pick(grad_key), key_wide)
            + against_exact(pick(grad_key_low), key_a_wide)
        )
        return (
            total
            + against_exact(pick(grad_values), value_wide)
            + against_exact(pick(grad_value_low), value_a_wide)
        )

    grad_normed = scatter_grads(attention_term)
    unused, norm_pull_one = jax.vjp(norm_rows, rows_in, gain_one.astype(jnp.float32))
    grad_input_part, attention_gain_grad = norm_pull_one(grad_normed)
    input_grad = grad_middle + grad_input_part
    attention_split = (
        lax.psum_scatter(
            query_weight_grad.astype(jnp.bfloat16), "dp", scatter_dimension=0, tiled=True
        ).astype(jnp.float32),
        lax.psum_scatter(
            output_weight_grad.astype(jnp.bfloat16), "dp", scatter_dimension=1, tiled=True
        ).astype(jnp.float32),
        lax.psum_scatter(
            query_expand_grad.astype(jnp.bfloat16), "dp", scatter_dimension=0, tiled=True
        ).astype(jnp.float32),
        lax.psum_scatter(
            output_shrink_grad.astype(jnp.bfloat16), "dp", scatter_dimension=0, tiled=True
        ).astype(jnp.float32),
        lax.psum_scatter(
            output_expand_grad.astype(jnp.bfloat16), "dp", scatter_dimension=0, tiled=True
        ).astype(jnp.float32),
    )
    attention_shared = (
        lax.psum_scatter(attention_gain_grad, ("dp", "mp"), scatter_dimension=0, tiled=True),
        lax.psum_scatter(key_weight_grad, ("dp", "mp"), scatter_dimension=0, tiled=True),
        lax.psum_scatter(value_weight_grad, ("dp", "mp"), scatter_dimension=0, tiled=True),
        lax.psum_scatter(query_shrink_grad, ("dp", "mp"), scatter_dimension=0, tiled=True),
        lax.psum_scatter(key_shrink_grad, ("dp", "mp"), scatter_dimension=0, tiled=True),
        lax.psum_scatter(key_expand_grad, ("dp", "mp"), scatter_dimension=0, tiled=True),
        lax.psum_scatter(value_shrink_grad, ("dp", "mp"), scatter_dimension=0, tiled=True),
        lax.psum_scatter(value_expand_grad, ("dp", "mp"), scatter_dimension=0, tiled=True),
    )
    return (
        result.astype(jnp.bfloat16),
        input_grad,
        attention_shared[0],
        attention_split[0],
        attention_shared[1],
        attention_shared[2],
        attention_split[1],
        attention_shared[3],
        attention_split[2],
        attention_shared[4],
        attention_shared[5],
        attention_shared[6],
        attention_shared[7],
        attention_split[3],
        attention_split[4],
        feed_shared[0],
        gate_weight_own,
        up_weight_own,
        down_weight_own,
        feed_shared[1],
        gate_expand_own,
        feed_shared[2],
        up_expand_own,
        down_shrink_own,
        down_expand_own,
    )


def solution(mesh):
    levels = mesh.shape["dp"] // 2
    few = mesh.shape["mp"] == 4 and mesh.shape["dp"] % 2 == 0 and levels <= 4
    step = functools.partial(by_unit, levels) if few else body
    placed = (
        P(("dp", "mp"), None),
        P(("dp", "mp"), None),
        P("dp"),
        P("dp", "mp"),
        P("dp", None),
        P("dp", None),
        P("mp", "dp"),
        P("dp", None),
        P("dp", "mp"),
        P("dp", None),
        P("dp", None),
        P("dp", None),
        P("dp", None),
        P(("mp", "dp"), None),
        P("dp", None),
        P("dp"),
        P("dp", "mp"),
        P("dp", "mp"),
        P("mp", "dp"),
        P("dp", None),
        P("dp", "mp"),
        P("dp", None),
        P("dp", "mp"),
        P(("mp", "dp"), None),
        P("dp", None),
        P("dp"),
        P("dp"),
        P("dp"),
    )
    return jax.shard_map(
        step,
        mesh=mesh,
        in_specs=placed,
        out_specs=(
            P(("dp", "mp"), None),
            P(("dp", "mp"), None),
            P(("dp", "mp")),
            P("dp", "mp"),
            P(("dp", "mp"), None),
            P(("dp", "mp"), None),
            P("mp", "dp"),
            P(("dp", "mp"), None),
            P("dp", "mp"),
            P(("dp", "mp"), None),
            P(("dp", "mp"), None),
            P(("dp", "mp"), None),
            P(("dp", "mp"), None),
            P(("mp", "dp"), None),
            P("dp", None),
            P(("dp", "mp")),
            P("dp", "mp"),
            P("dp", "mp"),
            P("mp", "dp"),
            P(("dp", "mp"), None),
            P("dp", "mp"),
            P(("dp", "mp"), None),
            P("dp", "mp"),
            P(("mp", "dp"), None),
            P("dp", None),
        ),
        check_vma=False,
    )
```

```python
import functools
import math
from types import SimpleNamespace

import jax
import jax.numpy as jnp
from jax import lax
from jax.experimental import pallas as pl
from jax.experimental.pallas import tpu as pltpu
from jax.sharding import PartitionSpec as P

MESH = pl.DeviceIdType.MESH
MIB = 1 << 20

EPS = 1e-06


def matmul(left, right):
    return jnp.dot(left, right, preferred_element_type=jnp.float32)


def against(left, right):
    return lax.dot_general(
        left, right, (((1,), (1,)), ((), ())), preferred_element_type=jnp.float32
    )


def outer_sum(left, right):
    return lax.dot_general(
        left, right, (((0,), (0,)), ((), ())), preferred_element_type=jnp.float32
    )


def against_exact(left, right):
    return lax.dot_general(
        left,
        right,
        (((1,), (1,)), ((), ())),
        precision=lax.Precision.HIGHEST,
        preferred_element_type=jnp.float32,
    )


def outer_exact(left, right):
    return lax.dot_general(
        left,
        right,
        (((0,), (0,)), ((), ())),
        precision=lax.Precision.HIGHEST,
        preferred_element_type=jnp.float32,
    )


def norm_rows(rows, gain):
    return rows * lax.rsqrt(jnp.mean(rows * rows, axis=-1, keepdims=True) + EPS) * gain


def rotary(entries, places, sign):
    half = entries.shape[-1] // 2
    freq = 10000.0 ** (-jnp.arange(half).astype(jnp.float32) * 2.0 / entries.shape[-1])
    angle = places.astype(jnp.float32)[:, None] * freq[None, :]
    cosine = jnp.cos(angle)[:, None, :]
    sine = sign * jnp.sin(angle)[:, None, :]
    first = entries[..., :half]
    second = entries[..., half:]
    return jnp.concatenate(
        [first * cosine - second * sine, second * cosine + first * sine], axis=-1
    )


class Wires:
    def __init__(self, levels, sends, lands, locals_=None):
        self.sends, self.lands, self.locals = sends, lands, locals_
        self.levels = levels
        self.count = self.local_count = 0
        self.open = []
        dp, mp = lax.axis_index("dp"), lax.axis_index("mp")
        self.dp, self.mp = dp, mp
        self.z, self.y, self.x, self.c = dp // 2, dp % 2, mp // 2, mp % 2

    def take(self, number=1):
        first = self.count
        self.count += number
        assert self.count <= self.sends.shape[0], self.count
        return first

    def at(self, z, y, x, c):
        return (z * 2 + y, x * 2 + c)

    def up(self):
        return self.at(self.z + 1, self.y, self.x, self.c)

    def down(self):
        return self.at(self.z - 1, self.y, self.x, self.c)

    def over_x(self):
        return self.at(self.z, self.y, 1 - self.x, self.c)

    def over_y(self):
        return self.at(self.z, 1 - self.y, self.x, self.c)

    def over_core(self):
        return self.at(self.z, self.y, self.x, 1 - self.c)

    def copy(self, source, target, out, land, device):
        return pltpu.make_async_remote_copy(
            src_ref=source,
            dst_ref=target,
            send_sem=self.sends.at[out],
            recv_sem=self.lands.at[land],
            device_id=device,
            device_id_type=MESH,
        )

    def send(self, source, target, out, land, device, when=True):
        made = self.copy(source, target, out, land, device)
        under(when, made.start)
        self.open.append((when, made.wait_send))

    def landed(self, target, land):
        self.copy(target, target, land, land, self.over_x()).wait_recv()

    def local(self, source, target):
        made = pltpu.make_async_copy(source, target, self.locals.at[self.local_count])
        self.local_count += 1
        assert self.local_count <= self.locals.shape[0], self.local_count
        made.start()
        return made

    def take_local(self, number):
        first = self.local_count
        self.local_count += number
        assert self.local_count <= self.locals.shape[0], self.local_count
        return first

    def finish(self):
        for when, wait in self.open:
            under(when, wait)

    def greet(self, far=False, flat=False):
        barrier = pltpu.get_barrier_semaphore()

        def call(device):
            pl.semaphore_signal(barrier, inc=1, device_id=device, device_id_type=MESH)

        call(self.over_x())
        call(self.over_core())
        if far:
            call(self.at(self.z, self.y, 1 - self.x, 1 - self.c))
            for step in range(1, 2 * self.levels):
                call((lax.rem(self.dp + step, 2 * self.levels), self.mp))
            pl.semaphore_wait(barrier, 2 + 2 * self.levels)
            return
        if flat:
            pl.semaphore_wait(barrier, 2)
            return
        call(self.over_y())
        pl.when(self.z > 0)(lambda: call(self.down()))
        pl.when(self.z < self.levels - 1)(lambda: call(self.up()))
        ends = jnp.where(self.z > 0, 1, 0) + jnp.where(self.z < self.levels - 1, 1, 0)
        pl.semaphore_wait(barrier, 3 + ends)


def under(when, act):
    if when is True:
        act()
    else:
        pl.when(when)(act)


def sides(w, step):
    yield (True, w.z - step, w.z >= step)
    yield (False, w.z + step, w.z < w.levels - step)


def gather_all(w, own, at, parts):
    z, y, x, c = w.z, w.y, w.x, w.c
    n = w.levels
    rise, fall, by_x, by_y, last_x, last_y = (w.take(n) for _ in range(6))
    by_core = w.take(4 * n)

    def core(block, zs, ys, xs):
        place = by_core + zs * 4 + ys * 2 + xs
        return (block, block, place, place, w.over_core())

    here = at(z, y, x, c)
    kept = w.local(own, here)
    w.send(own, here, rise + z, rise + z, w.up(), z < n - 1)
    w.send(own, here, fall + z, fall + z, w.down(), z > 0)
    w.send(own, here, by_x + z, by_x + z, w.over_x())
    w.send(own, here, by_y + z, by_y + z, w.over_y())
    place = by_core + z * 4 + y * 2 + x
    w.send(own, here, place, place, w.over_core())
    yield

    def plane(zs, ok):
        block = at(zs, y, 1 - x, c)
        under(ok, lambda: w.landed(block, by_x + zs))
        for piece in parts(block)[:1]:
            if piece is not None:
                w.send(piece, piece, last_y + zs, last_y + zs, w.over_y(), ok)
        w.send(*core(block, zs, y, 1 - x), ok)
        block = at(zs, 1 - y, x, c)
        under(ok, lambda: w.landed(block, by_y + zs))
        for piece in parts(block)[1:]:
            if piece is not None:
                w.send(piece, piece, last_x + zs, last_x + zs, w.over_x(), ok)
        w.send(*core(block, zs, 1 - y, x), ok)

    plane(z, True)
    yield
    for step in range(1, n):
        for rising, zs, ok in sides(w, step):
            block = at(zs, y, x, c)
            lane = rise if rising else fall
            under(ok, lambda: w.landed(block, lane + zs))
            if rising:
                w.send(block, block, rise + zs, rise + zs, w.up(), jnp.logical_and(ok, z < n - 1))
            else:
                w.send(block, block, fall + zs, fall + zs, w.down(), jnp.logical_and(ok, z > 0))
            w.send(block, block, by_x + zs, by_x + zs, w.over_x(), ok)
            w.send(block, block, by_y + zs, by_y + zs, w.over_y(), ok)
            w.send(*core(block, zs, y, x), ok)
        yield
        for _, zs, ok in sides(w, step):
            plane(zs, ok)
        yield
    for step in range(n):
        for _, zs, ok in sides(w, step) if step else [(True, z, True)]:
            block = at(zs, 1 - y, 1 - x, c)
            for piece, lane in zip(parts(block), (last_y, last_x)):
                if piece is not None:
                    under(ok, lambda: w.landed(piece, lane + zs))
            w.send(*core(block, zs, 1 - y, 1 - x), ok)
        yield
    for zs in range(n):
        for ys in range(2):
            for xs in range(2):
                w.landed(at(zs, ys, xs, 1 - c), by_core + zs * 4 + ys * 2 + xs)
    kept.wait()


def gather_dp(w, own, at):
    z, y, n = w.z, w.y, w.levels
    rise, fall, by_y = (w.take(n) for _ in range(3))
    here = at(z, y)
    kept = w.local(own, here)
    w.send(own, here, rise + z, rise + z, w.up(), z < n - 1)
    w.send(own, here, fall + z, fall + z, w.down(), z > 0)
    w.send(own, here, by_y + z, by_y + z, w.over_y())
    yield
    yield
    for step in range(1, n):
        for rising, zs, ok in sides(w, step):
            block = at(zs, y)
            lane = rise if rising else fall
            under(ok, lambda: w.landed(block, lane + zs))
            if rising:
                w.send(block, block, rise + zs, rise + zs, w.up(), jnp.logical_and(ok, z < n - 1))
            else:
                w.send(block, block, fall + zs, fall + zs, w.down(), jnp.logical_and(ok, z > 0))
            w.send(block, block, by_y + zs, by_y + zs, w.over_y(), ok)
        yield
        yield
    for zs in range(n):
        w.landed(at(zs, 1 - y), by_y + zs)
    kept.wait()


def gather_mp(w, own, at):
    x, c = w.x, w.c
    first, second = w.take(), w.take(2)
    here = at(x, c)
    kept = w.local(own, here)
    w.send(own, here, first, first, w.over_x())
    w.send(own, here, second, second, w.over_core())
    yield
    block = at(1 - x, c)
    w.landed(block, first)
    w.send(block, block, second + 1, second + 1, w.over_core())
    yield
    w.landed(at(x, 1 - c), second)
    w.landed(at(1 - x, 1 - c), second + 1)
    kept.wait()


def exchange_dp(w, source, target):
    count = 2 * w.levels
    first = w.take(count)
    kept = w.local(source(w.dp), target(w.dp))
    for step in range(1, count):
        there = lax.rem(w.dp + step, count)
        w.send(source(there), target(w.dp), first + step, first + step, (there, w.mp))
        yield
    for step in range(1, count):
        w.landed(target(lax.rem(w.dp + count - step, count)), first + step)
    kept.wait()


PACE = 4


def turn(steps, after=(), pace=PACE):
    spare = [one for one in after for _ in range(7)]
    turn_on(steps, spare, pace)
    for one in spare:
        next(one)
    turn_on(after)


def turn_on(steps, spare=(), pace=0):
    steps = list(steps)
    while steps:
        for _ in range(min(pace, len(spare))):
            next(spare.pop(0))
        left = []
        for one in steps:
            try:
                next(one)
                left.append(one)
            except StopIteration:
                pass
        steps = left


CHUNK = 16


def add_up(target, *sources):
    rows = target.shape[0]

    def one(i, unused):
        part = pl.ds(pl.multiple_of(i * CHUNK, CHUNK), CHUNK)
        total = sources[0][part, :].astype(jnp.float32)
        for source in sources[1:]:
            total = total + source[part, :].astype(jnp.float32)
        target[part, :] = total.astype(target.dtype)
        return unused

    lax.fori_loop(0, rows // CHUNK, one, 0)


def planes(w):
    z, n = w.z, w.levels
    for k in range(n - 1):
        falling = n - 1 - k
        low_half = jnp.where(falling > z, falling, falling - 1)
        high_half = jnp.where(k < z, k, k + 1)
        yield jnp.where(z < n // 2, low_half, high_half)
    yield z


def scatter_all(w, part, landing, own, core, half_x, half_y, full_x, full_y, below, above, out, make=None):
    z, y, x, c, n = w.z, w.y, w.x, w.c, w.levels
    to_core, to_hx, to_hy, to_fx, to_fy = (w.take(4 * n), w.take(n), w.take(n), w.take(n), w.take(n))
    rise, fall = w.take(n), w.take(n)
    from_part, from_landing = w.take_local(4 * n), w.take_local(4 * n)
    rows = own.shape[1]
    cut = rows // 2 // CHUNK * CHUNK
    first, second = pl.ds(0, cut), pl.ds(cut, rows - cut)
    kinds = ((1 - y, 1 - x), (1 - y, x), (y, 1 - x), (y, x))
    order = list(planes(w))
    kept = {}

    def start(k):
        zs = order[k]
        for kind, (ys, xs) in enumerate(kinds):
            here = k * 4 + kind
            lane = to_core + here
            for source, into in part(zs, ys, xs, 1 - c):
                w.copy(source, into(landing.at[here]), lane, lane, w.over_core()).start()
            w.open.append((True, w.copy(landing.at[here], landing.at[here], lane, lane, w.over_core()).wait_send))
            for source, into in part(zs, ys, xs, c):
                pltpu.make_async_copy(source, into(own.at[here]), w.locals.at[from_part + here]).start()
            kept[here] = pltpu.make_async_copy(landing.at[here], own.at[here], w.locals.at[from_part + here])

    def join(k):
        loads = []
        for kind in range(4):
            here = k * 4 + kind
            w.landed(landing.at[here], to_core + here)
            load = pltpu.make_async_copy(landing.at[here], core.at[kind], w.locals.at[from_landing + here])
            load.start()
            loads.append(load)
        for kind in range(4):
            here = k * 4 + kind
            kept[here].wait()
            loads[kind].wait()
            add_up(own.at[here], own.at[here], core.at[kind])
            if kind == 0:
                w.send(own.at[here, first], half_x.at[k], to_hx + k, to_hx + k, w.over_x())
                w.send(own.at[here, second], half_y.at[k], to_hy + k, to_hy + k, w.over_y())

    def across(k):
        here = k * 4 + 1
        w.landed(half_x.at[k], to_hx + k)
        add_up(own.at[here, first], own.at[here, first], half_x.at[k])
        w.send(own.at[here], full_y.at[k], to_fy + k, to_fy + k, w.over_y())
        here = k * 4 + 2
        w.landed(half_y.at[k], to_hy + k)
        add_up(own.at[here, second], own.at[here, second], half_y.at[k])
        w.send(own.at[here], full_x.at[k], to_fx + k, to_fx + k, w.over_x())

    def along(k):
        zs, here = order[k], own.at[k * 4 + 3]
        w.landed(full_x.at[k], to_fx + k)
        w.landed(full_y.at[k], to_fy + k)
        if k == n - 1:
            add_up(here, here, full_x.at[k], full_y.at[k])
            return
        pass_on(w, zs, here, (full_x.at[k], full_y.at[k]), below, above, rise, fall)

    for k in range(n + 3):
        if make is not None:
            yield from make(k)
        if k < n:
            start(k)
            yield
        for lag, act in ((1, join), (2, across), (3, along)):
            if 0 <= k - lag < n:
                act(k - lag)
                yield
    last_sum(w, own.at[4 * n - 1], (), below, above, rise, fall, out)


def pass_on(w, zs, here, sources, below, above, rise, fall):
    z, n = w.z, w.levels
    rising, falling = zs > z, zs < z
    more_up, more_down = jnp.logical_and(rising, z > 0), jnp.logical_and(falling, z < n - 1)

    def take_below():
        w.landed(below.at[zs - 1], rise + zs)
        add_up(here, here, *sources, below.at[zs - 1])

    def take_above():
        w.landed(above.at[zs], fall + zs)
        add_up(here, here, *sources, above.at[zs])

    under(more_up, take_below)
    under(more_down, take_above)
    under(
        jnp.logical_not(jnp.logical_or(more_up, more_down)), lambda: add_up(here, here, *sources)
    )
    w.send(here, below.at[zs - 1], rise + zs, rise + zs, w.up(), rising)
    w.send(here, above.at[zs], fall + zs, fall + zs, w.down(), falling)


def last_sum(w, here, sources, below, above, rise, fall, out):
    z, n = w.z, w.levels
    under(z > 0, lambda: w.landed(below.at[z - 1], rise + z))
    under(z < n - 1, lambda: w.landed(above.at[z], fall + z))
    under(z == 0, lambda: add_up(out, here, *sources, above.at[z]))
    under(z == n - 1, lambda: add_up(out, here, *sources, below.at[z - 1]))
    under(
        jnp.logical_and(z > 0, z < n - 1),
        lambda: add_up(out, here, *sources, below.at[z - 1], above.at[z]),
    )


def scatter_all_scratch(n, rows, columns):
    cut = rows // 2 // CHUNK * CHUNK
    shapes = [(4 * n, rows), (4, rows), (n, cut), (n, rows - cut)] + [(n, rows)] * 2 + [(n - 1, rows)] * 2
    return [pltpu.VMEM(shape + (columns,), jnp.bfloat16) for shape in shapes]


def scatter_dp(w, part, own, over, below, above, out):
    y, n = w.y, w.levels
    by_y, rise, fall, spare = w.take(n), w.take(n), w.take(n), w.take_local(n)
    order = list(planes(w))
    for k, zs in enumerate(order):
        for source, into in part(zs, 1 - y):
            w.copy(source, into(over.at[k]), by_y + k, by_y + k, w.over_y()).start()
        w.open.append((True, w.copy(over.at[k], over.at[k], by_y + k, by_y + k, w.over_y()).wait_send))
        for source, into in part(zs, y):
            pltpu.make_async_copy(source, into(own.at[k]), w.locals.at[spare + k]).start()
        yield
    for k, zs in enumerate(order):
        pltpu.make_async_copy(over.at[k], own.at[k], w.locals.at[spare + k]).wait()
        w.landed(over.at[k], by_y + k)
        if k < n - 1:
            pass_on(w, zs, own.at[k], (over.at[k],), below, above, rise, fall)
            yield
    last_sum(w, own.at[n - 1], (over.at[n - 1],), below, above, rise, fall, out)


def scatter_mp(w, part, own, first, second, out):
    x, c = w.x, w.c
    core, cross = w.take(2), w.take()
    kept = []
    for i, xs in enumerate((1 - x, x)):
        w.send(part.at[xs * 2 + 1 - c], first.at[i], core + i, core + i, w.over_core())
        kept.append(w.local(part.at[xs * 2 + c], own.at[i]))
    kept[0].wait()
    w.landed(first.at[0], core)
    add_up(own.at[0], own.at[0], first.at[0])
    w.send(own.at[0], second, cross, cross, w.over_x())
    kept[1].wait()
    w.landed(first.at[1], core + 1)
    w.landed(second, cross)
    add_up(out, own.at[1], first.at[1], second)


VMEM = 62 * MIB
ANY = pl.BlockSpec(memory_space=pl.ANY)
WHOLE = pl.BlockSpec(memory_space=pltpu.VMEM)


def call(kernel, identity, arrays, outs, scratch, signals, locals_, in_vmem=False, name=None):
    return pl.pallas_call(
        kernel,
        out_shape=[jax.ShapeDtypeStruct(shape, kind) for shape, kind, _ in outs],
        in_specs=[ANY] * len(arrays),
        out_specs=[WHOLE if near else ANY for _, _, near in outs],
        scratch_shapes=list(scratch)
        + [
            pltpu.SemaphoreType.DMA((signals,)),
            pltpu.SemaphoreType.DMA((signals,)),
            pltpu.SemaphoreType.DMA((max(locals_, 1),)),
        ],
        compiler_params=pltpu.CompilerParams(
            collective_id=identity, has_side_effects=True, vmem_limit_bytes=VMEM
        ),
        name=name,
    )(*arrays)


def halves(block):
    rows = block.shape[0]
    cut = rows // 2 // CHUNK * CHUNK
    return (block.at[pl.ds(0, cut)], block.at[pl.ds(cut, rows - cut)])


def by_x_last(block):
    return (None, block)


def rows_of(ref, index, rows):
    return ref.at[pl.ds(pl.multiple_of(index * rows, rows), rows)]


def columns_of(ref, index, columns):
    return ref.at[:, pl.ds(pl.multiple_of(index * columns, columns), columns)]


def flat(z, y, x, c):
    return (z * 2 + y) * 4 + x * 2 + c


def one_block(array):
    return lambda z, y, x, c: [(array.at[flat(z, y, x, c)], lambda ref: ref)]


def corner(first, rows, column, columns):
    return lambda ref: ref.at[pl.ds(first, rows), pl.ds(column, columns)]


def begin(levels, tensors):
    names = list(vars(tensors))
    count = 2 * levels
    wide = tensors.query_weight.shape[1]
    unit = tensors.gate_weight.shape[1] // count
    deep = tensors.gate_weight.shape[0] * count
    rows = tensors.layer_input.shape[0]
    packed = tensors.maps.shape
    low = tensors.gate_expand.shape[0] * count
    piece = deep // 4
    shapes = dict(
        layer_input=(4, rows, deep),
        maps=(4 * count * packed[0], packed[1]),
        output_expand=(low, deep),
        down_expand=(low, deep),
        query_weight=(deep, wide),
        output_weight=(wide, deep),
        expands=(low, tensors.expands.shape[1]),
        output_shrink=(tensors.output_shrink.shape[0] * count, low),
        output_grad=(4 * count, rows, deep),
        gate_weight=(deep, unit),
        up_weight=(deep, unit),
        down_weight=(unit, deep),
        gate_expand=(low, unit),
        up_expand=(low, unit),
    )

    def kernel(*refs):
        given = SimpleNamespace(**dict(zip(names, refs)))
        got = SimpleNamespace(**dict(zip(shapes, refs[len(names) :])))
        w = Wires(levels, *refs[len(names) + len(shapes) :])
        w.greet(far=True)

        def expand_at(into):
            def at(z, y, x, c):
                return into.at[
                    pl.ds(pl.multiple_of((z * 2 + y) * (low // count), low // count), low // count),
                    pl.ds(pl.multiple_of((x * 2 + c) * piece, piece), piece),
                ]

            return at

        steps = [
            gather_mp(w, given.layer_input, lambda x, c: got.layer_input.at[x * 2 + c]),
            gather_dp(w, given.query_weight, lambda z, y: rows_of(got.query_weight, z * 2 + y, deep // count)),
            gather_dp(w, given.output_weight, lambda z, y: columns_of(got.output_weight, z * 2 + y, deep // count)),
            gather_all(w, given.maps, lambda z, y, x, c: rows_of(got.maps, flat(z, y, x, c), packed[0]), halves),
            gather_dp(w, given.expands, lambda z, y: rows_of(got.expands, z * 2 + y, low // count)),
            gather_dp(
                w,
                given.output_shrink,
                lambda z, y: rows_of(got.output_shrink, z * 2 + y, given.output_shrink.shape[0]),
            ),
        ]
        for own, into in ((given.output_expand, got.output_expand), (given.down_expand, got.down_expand)):
            steps.append(gather_all(w, columns_of(own, w.mp, piece), expand_at(into), halves))
        steps.append(gather_all(w, given.output_grad, lambda z, y, x, c: got.output_grad.at[flat(z, y, x, c)], halves))
        after = [
            exchange_dp(w, lambda dp: columns_of(given.gate_weight, dp, unit), lambda dp: rows_of(got.gate_weight, dp, deep // count)),
            exchange_dp(w, lambda dp: columns_of(given.up_weight, dp, unit), lambda dp: rows_of(got.up_weight, dp, deep // count)),
            exchange_dp(w, lambda dp: rows_of(given.down_weight, dp, unit), lambda dp: columns_of(got.down_weight, dp, deep // count)),
            exchange_dp(w, lambda dp: columns_of(given.gate_expand, dp, unit), lambda dp: rows_of(got.gate_expand, dp, low // count)),
            exchange_dp(w, lambda dp: columns_of(given.up_expand, dp, unit), lambda dp: rows_of(got.up_expand, dp, low // count)),
        ]
        turn(steps, after)
        w.finish()

    kind = jnp.bfloat16
    given = call(
        kernel,
        0,
        list(vars(tensors).values()),
        [(shape, kind, False) for shape in shapes.values()],
        [],
        64 * levels + 48 * levels * 3,
        32,
        name="begin",
    )
    return SimpleNamespace(**dict(zip(shapes, given)))


def spread(levels, rows):
    here, wide = rows.shape

    def kernel(own, out, *sems):
        w = Wires(levels, *sems)
        w.greet()
        turn([gather_all(w, own, lambda z, y, x, c: out.at[flat(z, y, x, c)], halves)])
        w.finish()

    (out,) = call(
        kernel, 1, [rows], [((8 * levels, here, wide), rows.dtype, False)], [], 40 * levels, 4, name="spread"
    )
    return out


def gelu_pair(gate):
    inner = GELU * (gate + 0.044715 * gate * gate * gate)
    bend = jnp.tanh(inner)
    slope = GELU * (1.0 + 3.0 * 0.044715 * gate * gate)
    return 0.5 * gate * (1.0 + bend), 0.5 * (1.0 + bend) + 0.5 * gate * (1.0 - bend * bend) * slope


GELU = (2.0 / math.pi) ** 0.5
TALL = 256


def feed(levels, rows, tokens, grads, gate_up, down):
    deep, both = gate_up.shape
    unit = both // 2
    total = tokens.shape[0]
    level = total // levels
    count = 2 * levels
    strip = deep // count
    half = total // 2
    steps = level // TALL
    kind = jnp.bfloat16
    scratch = scatter_all_scratch(levels, rows, deep)
    each = len(scratch)

    def kernel(tokens_ref, grads_ref, gate_up_hbm, down_hbm, *refs):
        grad_out, branch_out, pair_hbm, single_hbm, gate_own, up_own = refs[:6]
        hidden_hbm, pre_hbm, grad_part, branch_part, grad_land, branch_land = refs[6:12]
        buffers = refs[12:]
        one, two = buffers[:each], buffers[each : 2 * each - 1]
        two = two[:1] + (one[1],) + two[1:]
        gate_up_ref, down_ref, arena, hidden_stage, pre_stage, columns, down_stage, loads, stores = buffers[
            2 * each - 1 : -3
        ]

        def space(number, slot):
            return arena.at[pl.ds(pl.multiple_of((2 * number + slot) * TALL, TALL), TALL)]

        w = Wires(levels, *buffers[-3:])
        weights = [w.local(gate_up_hbm, gate_up_ref), w.local(down_hbm, down_ref)]
        order = list(planes(w))

        def load(k, j, slot):
            start = pl.ds(pl.multiple_of(order[k] * level + j * TALL, TALL), TALL)
            return (
                pltpu.make_async_copy(tokens_ref.at[start], space(0, slot), loads.at[0, slot]),
                pltpu.make_async_copy(grads_ref.at[start], space(1, slot), loads.at[1, slot]),
            )

        def store(k, j, slot):
            start = pl.multiple_of(order[k] * level + j * TALL, TALL)
            block = order[k] * (level // rows) + j * (TALL // rows)
            made = [
                pltpu.make_async_copy(hidden_stage.at[slot], hidden_hbm.at[pl.ds(start, TALL)], stores.at[0, slot]),
                pltpu.make_async_copy(pre_stage.at[slot], pre_hbm.at[pl.ds(start, TALL)], stores.at[1, slot]),
            ]
            for i in range(TALL // rows):
                piece = pl.ds(i * rows, rows)
                made += [
                    pltpu.make_async_copy(space(2, slot).at[piece], grad_part.at[block + i], stores.at[2 + 2 * i, slot]),
                    pltpu.make_async_copy(space(3, slot).at[piece], branch_part.at[block + i], stores.at[3 + 2 * i, slot]),
                ]
            return made

        for copy in load(0, 0, 0):
            copy.start()
        w.greet(far=True)
        for copy in weights:
            copy.wait()

        lanes = w.take(2 * count)

        def there(i):
            return lax.rem(w.dp + 1 + i, count)

        def strip_of(ref, i):
            return columns_of(ref, there(i), strip)

        def strip_load(ref, i):
            slot = lax.rem(i, 2)
            return pltpu.make_async_copy(strip_of(ref, i), columns.at[slot], loads.at[0, slot])

        def pair_store(i):
            slot = lax.rem(i, 2)
            return pltpu.make_async_copy(pre_stage.at[slot], rows_of(pair_hbm, there(i), strip), stores.at[0, slot])

        def single_store(i):
            slot = lax.rem(i, 2)
            return pltpu.make_async_copy(down_stage.at[slot], strip_of(single_hbm, i), stores.at[1, slot])

        def pair_pieces(i):
            both_rows = rows_of(pair_hbm, there(i), strip)
            yield both_rows.at[:, pl.ds(0, unit)], columns_of(gate_own, w.dp, unit), lanes + i
            yield both_rows.at[:, pl.ds(unit, unit)], columns_of(up_own, w.dp, unit), lanes + count + i

        def give(pieces, i):
            for source, target, lane in pieces(i):
                w.copy(source, target, lane, lane, (there(i), w.mp)).start()

        def keep(pieces):
            for source, target, _ in pieces(count - 1):
                w.local(source, target).wait()

        def product(left, right, left_wide, right_wide):
            return sum(
                lax.dot_general(
                    left[pl.ds(0, half), pl.ds(i * left_wide[0], left_wide[1])] if left_wide[0] else left[pl.ds(i * half, half), :],
                    right[pl.ds(0, half), pl.ds(i * right_wide[0], right_wide[1])] if right_wide[0] else right[pl.ds(i * half, half), :],
                    (((0,), (0,)), ((), ())),
                    preferred_element_type=jnp.float32,
                )
                for i in range(2)
            )

        def pair_strip(i, carry):
            slot = lax.rem(i, 2)
            strip_load(tokens_ref, i).wait()

            @pl.when(i < count - 1)
            def _():
                strip_load(tokens_ref, i + 1).start()

            @pl.when(i == count - 1)
            def _():
                strip_load(grads_ref, count - 1 - i).start()

            pre_stage[slot] = product(columns.at[slot], arena, (0, 0), (both, both)).astype(kind)
            pair_store(i).start()

            @pl.when(i > 0)
            def _():
                pair_store(i - 1).wait()
                give(pair_pieces, i - 1)

            return carry

        def single_strip(i, carry):
            slot = lax.rem(i, 2)
            strip_load(grads_ref, i).wait()

            @pl.when(i < count - 1)
            def _():
                strip_load(grads_ref, i + 1).start()

            down_stage[slot] = product(gate_up_ref, columns.at[slot], (unit, unit), (0, 0)).astype(kind)
            single_store(i).start()

            @pl.when(i > 0)
            def _():
                single_store(i - 1).wait()

            return carry

        def gradients(k):
            if k == levels:
                held = []
                for i in range(2):
                    piece = pl.ds(i * half, half)
                    held.append(w.local(pre_hbm.at[piece], arena.at[:, pl.ds(i * both, both)]))
                    held.append(w.local(hidden_hbm.at[piece], gate_up_ref.at[:, pl.ds(i * unit, unit)]))
                strip_load(tokens_ref, 0).start()
                for copy in held:
                    copy.wait()
                lax.fori_loop(0, count // 2, pair_strip, 0)
            if k == levels + 1:
                lax.fori_loop(count // 2, count, pair_strip, 0)
                pair_store(count - 1).wait()
                keep(pair_pieces)
            if k == levels + 2:
                lax.fori_loop(0, count, single_strip, 0)
                single_store(count - 1).wait()

        def make(k):
            if k >= levels:
                gradients(k)
                yield
                return

            def chunk(j, carry):
                slot = lax.rem(j, 2)
                for copy in load(k, j, slot):
                    copy.wait()

                @pl.when(j < steps - 1)
                def _():
                    for copy in load(k, j + 1, 1 - slot):
                        copy.start()

                if k < levels - 1:

                    @pl.when(j == steps - 1)
                    def _():
                        for copy in load(k + 1, 0, 0):
                            copy.start()

                @pl.when(j >= 2)
                def _():
                    for copy in store(k, j - 2, slot):
                        copy.wait()

                pre = jnp.dot(space(0, slot)[...], gate_up_ref[...], preferred_element_type=jnp.float32)
                back = against(space(1, slot)[...], down_ref[...])
                gate, up = pre[:, :unit], pre[:, unit:]
                bent, slope = gelu_pair(gate)
                hidden = (bent * up).astype(kind)
                grad_pre = jnp.concatenate([back * up * slope, back * bent], axis=1).astype(kind)
                hidden_stage[slot] = hidden
                pre_stage[slot] = grad_pre
                space(2, slot)[...] = against(grad_pre, gate_up_ref[...]).astype(kind)
                space(3, slot)[...] = jnp.dot(hidden, down_ref[...], preferred_element_type=jnp.float32).astype(kind)
                for copy in store(k, j, slot):
                    copy.start()
                return carry

            lax.fori_loop(0, steps, chunk, 0)
            for j in range(max(steps - 2, 0), steps):
                for copy in store(k, j, j % 2):
                    copy.wait()
            yield

        def idle(k):
            yield

        turn(
            [
                scatter_all(w, one_block(grad_part), grad_land, *one, grad_out, make=make),
                scatter_all(w, one_block(branch_part), branch_land, *two, branch_out, make=idle),
            ]
        )
        for i in range(count - 1):
            source = lax.rem(w.dp + count - 1 - i, count)
            for sent, (_, _, lane) in zip(
                (columns_of(gate_own, source, unit), columns_of(up_own, source, unit)),
                pair_pieces(i),
            ):
                w.landed(sent, lane)
                w.copy(sent, sent, lane, lane, w.over_x()).wait_send()
        w.finish()

    assert total == 2 * deep and 2 * both == deep and 8 * TALL == deep and strip == TALL
    tall = [(deep, deep), (2, TALL, unit), (2, TALL, both), (2, total, strip), (2, unit, strip)]
    outs = [((rows, deep), jnp.float32, True)] * 2
    outs += [((deep, both), kind, False), ((unit, deep), kind, False)]
    outs += [((strip, unit * count), kind, False)] * 2
    outs += [((total, unit), kind, False), ((total, both), kind, False)]
    outs += [((total // rows, rows, deep), kind, False)] * 2 + [((4 * levels, rows, deep), kind, False)] * 2
    made = call(
        kernel,
        2,
        [tokens, grads, gate_up, down],
        outs,
        scratch
        + scratch[:1]
        + scratch[2:]
        + [pltpu.VMEM(gate_up.shape, kind), pltpu.VMEM(down.shape, kind)]
        + [pltpu.VMEM(shape, kind) for shape in tall]
        + [pltpu.SemaphoreType.DMA((2, 2)), pltpu.SemaphoreType.DMA((2 + 2 * (TALL // rows), 2))],
        2 * 10 * levels + 6 * levels + 4,
        16 * levels + 12,
        name="feed",
    )
    return made[:6]


def share_mp(levels, rows):
    def kernel(own, out, *sems):
        w = Wires(levels, *sems)
        w.greet(flat=True)
        turn([gather_mp(w, own, lambda x, c: out.at[x * 2 + c])])
        w.finish()

    (out,) = call(kernel, 3, [rows], [((4,) + rows.shape, rows.dtype, False)], [], 16, 4, name="share_mp")
    return out


def sum_mp(levels, part):
    _, here, wide = part.shape

    def kernel(given, out, own, first, second, *sems):
        w = Wires(levels, *sems)
        w.greet(flat=True)
        scatter_mp(w, given, own, first, second, out)
        w.finish()

    (out,) = call(
        kernel,
        4,
        [part],
        [((here, wide), jnp.float32, True)],
        [pltpu.VMEM((2, here, wide), part.dtype)] * 2 + [pltpu.VMEM((here, wide), part.dtype)],
        16,
        4,
        name="sum_mp",
    )
    return out


BACK = 2


def end(levels, rank, small, wides, query, output, units):
    count = 2 * levels
    deep, narrow = small.shape
    few, piece = deep // (4 * count), deep // 4
    wide = narrow + piece
    high = rank // count
    strip = deep // count
    unit = units.down_weight.shape[0]
    names = list(vars(units))
    shapes = dict(
        down_weight=(unit * count, strip),
        gate_expand=(high, unit * count),
        up_expand=(high, unit * count),
    )
    heads = query[0].shape[1]
    query_shape = (strip + high, heads)
    output_shape = (heads + heads // count, strip)
    scratch = scatter_all_scratch(levels, few, wide)
    each = len(scratch)
    scratch += [pltpu.VMEM((levels,) + query_shape, jnp.bfloat16)] * 4
    scratch += [pltpu.VMEM((levels,) + output_shape, jnp.bfloat16)] * 4

    def kernel(*refs):
        small_ref, wide_one, wide_two, query_w, query_b, output_w, output_a = refs[:7]
        given = SimpleNamespace(**dict(zip(names, refs[7:])))
        refs = refs[7 + len(names) :]
        got = SimpleNamespace(**dict(zip(shapes, refs)))
        small_out, query_out, output_out, shared, landing = refs[len(names) : len(names) + 5]
        buffers = refs[len(names) + 5 :]
        w = Wires(levels, *buffers[-3:])
        w.greet(far=True)

        def blocks(z, y, x, c):
            place = (pl.ds(pl.multiple_of((z * 2 + y) * high, high), high), pl.ds(pl.multiple_of((x * 2 + c) * piece, piece), piece))
            yield rows_of(small_ref, flat(z, y, x, c), few), corner(0, few, 0, narrow)
            yield wide_one.at[place], corner(0, high, narrow, piece)
            yield wide_two.at[place], corner(high, high, narrow, piece)

        def query_blocks(z, y):
            yield rows_of(query_w, z * 2 + y, strip), corner(0, strip, 0, heads)
            yield rows_of(query_b, z * 2 + y, high), corner(strip, high, 0, heads)

        def output_blocks(z, y):
            yield columns_of(output_w, z * 2 + y, strip), corner(0, heads, 0, strip)
            yield rows_of(output_a, z * 2 + y, heads // count), corner(heads, heads // count, 0, strip)

        def over_all():
            yield from scatter_all(w, blocks, landing, *buffers[:each], small_out)
            mine = small_out.at[:, pl.ds(narrow, piece)]
            yield from gather_mp(w, mine, lambda x, c: shared.at[x * 2 + c])

        after = [
            exchange_dp(w, lambda dp: columns_of(given.down_weight, dp, strip), lambda dp: rows_of(got.down_weight, dp, unit)),
            exchange_dp(w, lambda dp: rows_of(given.gate_expand, dp, high), lambda dp: columns_of(got.gate_expand, dp, unit)),
            exchange_dp(w, lambda dp: rows_of(given.up_expand, dp, high), lambda dp: columns_of(got.up_expand, dp, unit)),
        ]
        steps = [
            over_all(),
            scatter_dp(w, query_blocks, *buffers[each : each + 4], query_out),
            scatter_dp(w, output_blocks, *buffers[each + 4 : each + 8], output_out),
        ]
        turn(steps, after, BACK)
        w.finish()

    outs = [(shape, jnp.bfloat16, False) for shape in shapes.values()]
    outs += [((few, wide), jnp.float32, True), (query_shape, jnp.float32, True), (output_shape, jnp.float32, True)]
    outs += [((4, few, piece), jnp.float32, True), ((4 * levels, few, wide), jnp.bfloat16, False)]
    made = call(
        kernel,
        5,
        [small, *wides, *query, *output, *vars(units).values()],
        outs,
        scratch,
        32 * levels,
        10 * levels + 16,
        name="end",
    )
    return SimpleNamespace(**dict(zip(shapes, made))), *made[3:7]


def low(rows):
    return rows.astype(jnp.bfloat16)


def unit_rows(rows):
    scale = lax.rsqrt(jnp.mean(rows * rows, axis=-1, keepdims=True) + EPS)
    return rows * scale, scale


def norm_back(grad, normed, scale):
    return scale * (grad - normed * jnp.mean(grad * normed, axis=-1, keepdims=True))


def ones_in(rows, column):
    columns = jnp.arange(128)[None, :]
    return jnp.broadcast_to((columns >= column) & (columns < column + 32), (rows, 128)).astype(jnp.bfloat16)


def by_unit(
    levels,
    layer_input,
    output_grad,
    attention_gain,
    query_weight,
    key_weight,
    value_weight,
    output_weight,
    query_shrink,
    query_expand,
    key_shrink,
    key_expand,
    value_shrink,
    value_expand,
    output_shrink,
    output_expand,
    feedforward_gain,
    gate_weight,
    up_weight,
    down_weight,
    gate_shrink,
    gate_expand,
    up_shrink,
    up_expand,
    down_shrink,
    down_expand,
    group_ids,
    positions,
    segments,
):
    count = 2 * levels
    rows = layer_input.shape[0]
    tokens = 4 * rows
    deep = layer_input.shape[1]
    head = key_weight.shape[1]
    heads = query_weight.shape[1] // head
    rank = query_expand.shape[0] * count
    mp = lax.axis_index("mp")
    share = query_shrink.shape[0] // 4

    gains = jnp.stack([attention_gain, feedforward_gain], axis=1)
    gains = jnp.pad(gains, ((0, 0), (0, 126)))
    maps = jnp.concatenate(
        [key_weight, value_weight, query_shrink, key_shrink, value_shrink, gate_shrink, up_shrink, gains],
        axis=1,
    )
    maps = lax.dynamic_slice_in_dim(maps, mp * share, share, 0)
    expands = jnp.concatenate([query_expand, key_expand, value_expand], axis=1)
    got = begin(
        levels,
        SimpleNamespace(
            layer_input=layer_input,
            maps=maps,
            output_expand=output_expand,
            down_expand=down_expand,
            query_weight=query_weight,
            output_weight=output_weight,
            expands=expands,
            output_shrink=output_shrink,
            output_grad=output_grad,
            gate_weight=gate_weight,
            up_weight=up_weight,
            down_weight=down_weight,
            gate_expand=gate_expand,
            up_expand=up_expand,
        ),
    )
    maps = got.maps
    key_w, value_w = maps[:, :head], maps[:, head : 2 * head]
    query_a, key_a, value_a, gate_a, up_a = (
        maps[:, 2 * head + i * rank : 2 * head + (i + 1) * rank] for i in range(5)
    )
    gain_one = maps[:, 2 * head + 5 * rank : 2 * head + 5 * rank + 1].astype(jnp.float32)
    gain_two = maps[:, 2 * head + 5 * rank + 1 : 2 * head + 5 * rank + 2].astype(jnp.float32)
    query_b = got.expands[:, : heads * head]
    key_b = got.expands[:, heads * head : (heads + 1) * head]
    value_b = got.expands[:, (heads + 1) * head :]
    output_a, output_b = got.output_shrink, got.output_expand
    query_full = low(gain_one * (got.query_weight.astype(jnp.float32) + matmul(query_a, query_b)))
    key_full = low(gain_one * (key_w.astype(jnp.float32) + matmul(key_a, key_b)))
    value_full = low(gain_one * (value_w.astype(jnp.float32) + matmul(value_a, value_b)))
    inward = jnp.concatenate([query_full, key_full, value_full], axis=1)
    outward = low(got.output_weight.astype(jnp.float32) + matmul(output_a, output_b))

    allowed = (
        (group_ids[:, None] == group_ids[None, :])
        & (positions[None, :] <= positions[:, None])
        & ((segments[None, :] == 0) | (segments[None, :] == segments[:, None]))
    )
    group_rows = got.layer_input.reshape(tokens, deep).astype(jnp.float32)
    normed = low(unit_rows(group_rows)[0])
    lin = matmul(normed, inward)
    wide = heads * head
    queries = low(rotary(lin[:, :wide].reshape(tokens, heads, head), positions, 1.0) * head ** (-0.5))
    keys = low(rotary(lin[:, None, wide : wide + head], positions, 1.0)[:, 0, :])
    values = low(lin[:, wide + head :])
    scores = jnp.einsum("thd,sd->hts", queries, keys, preferred_element_type=jnp.float32)
    scores = jnp.where(allowed[None], scores, -1e30)
    expo = jnp.exp(scores - jnp.max(scores, axis=-1, keepdims=True))
    probability = expo / jnp.sum(expo, axis=-1, keepdims=True)
    probability_low = low(probability)
    mixed = low(
        jnp.einsum("hts,sd->thd", probability_low, values, preferred_element_type=jnp.float32)
    ).reshape(tokens, wide)
    branch = sum_mp(levels, low(matmul(mixed, outward)).reshape(4, rows, deep))
    own_rows = layer_input.astype(jnp.float32)
    middle = own_rows + branch

    gate_up = low(
        gain_two
        * (
            jnp.concatenate([got.gate_weight, got.up_weight], axis=1).astype(jnp.float32)
            + jnp.concatenate([matmul(gate_a, got.gate_expand), matmul(up_a, got.up_expand)], axis=1)
        )
    )
    unit = got.gate_weight.shape[1]
    down_a, down_b = down_shrink, got.down_expand
    down_full = low(got.down_weight.astype(jnp.float32) + matmul(down_a, down_b))
    normed_middle, scale_middle = unit_rows(middle)
    normed_all = spread(levels, low(normed_middle)).reshape(4 * count * rows, deep)
    grads = got.output_grad.reshape(4 * count * rows, deep)
    grad_normed, branch, pair_grad, down_grad_low, gate_own, up_own = feed(levels, rows, normed_all, grads, gate_up, down_full)
    result = low(middle + branch)
    grad_middle = output_grad.astype(jnp.float32) + norm_back(grad_normed, normed_middle, scale_middle)

    down_shrink_grad = against(down_grad_low, down_b)
    gate_b_grad = low(outer_sum(low(gain_two * gate_a.astype(jnp.float32)), pair_grad[:, :unit]))
    up_b_grad = low(outer_sum(low(gain_two * up_a.astype(jnp.float32)), pair_grad[:, unit:]))
    gate_a_part = gain_two * against(pair_grad[:, :unit], got.gate_expand)
    up_a_part = gain_two * against(pair_grad[:, unit:], got.up_expand)

    grad_branch = share_mp(levels, low(grad_middle)).reshape(tokens, deep)
    output_grad_w = outer_sum(mixed, grad_branch)
    grad_mixed = low(against(grad_branch, outward)).reshape(tokens, heads, head)
    grad_values = jnp.einsum("hts,thd->sd", probability_low, grad_mixed, preferred_element_type=jnp.float32)
    grad_probability = jnp.einsum("thd,sd->hts", grad_mixed, values, preferred_element_type=jnp.float32)
    grad_scores = low(
        probability * (grad_probability - jnp.sum(probability * grad_probability, axis=-1, keepdims=True))
    )
    grad_queries = jnp.einsum("hts,sd->thd", grad_scores, keys, preferred_element_type=jnp.float32)
    grad_keys = jnp.einsum("hts,thd->sd", grad_scores, queries, preferred_element_type=jnp.float32)
    grad_query = rotary(grad_queries * head ** (-0.5), positions, -1.0).reshape(tokens, wide)
    grad_key = rotary(grad_keys[:, None, :], positions, -1.0)[:, 0, :]
    grad_lin = low(jnp.concatenate([grad_query, grad_key, grad_values], axis=1))
    grad_rows = sum_mp(levels, low(against(grad_lin, inward)).reshape(4, rows, deep))
    normed_own, scale_own = unit_rows(own_rows)
    input_grad = grad_middle + norm_back(grad_rows, normed_own, scale_own)

    lin_normed = outer_sum(normed, grad_lin)
    lin_grad = low(lin_normed * gain_one)
    query_part, key_part, value_part = (
        lin_grad[:, :wide],
        lin_grad[:, wide : wide + head],
        lin_grad[:, wide + head :],
    )
    output_low = low(output_grad_w)
    gain_parts = matmul(low(lin_normed) * inward, ones_in(inward.shape[1], 0)) + matmul(
        pair_grad * gate_up, ones_in(2 * unit, 32)
    )

    def fold(array):
        return low(array).reshape(4 * count, array.shape[0] // (4 * count), head).reshape(deep, -1)

    folded = jnp.concatenate(
        [fold(outer_sum(key_a, key_part)), fold(outer_sum(value_a, value_part))], axis=1
    )
    small = jnp.concatenate(
        [
            lin_grad[:, wide:],
            low(against(query_part, query_b)),
            low(gate_a_part),
            low(up_a_part),
            low(gain_parts[:, :64]),
            folded,
        ],
        axis=1,
    )
    units, few, query_sum, output_sum, shared = end(
        levels,
        rank,
        small,
        (low(outer_sum(output_a, output_low)), low(outer_sum(down_a, down_grad_low))),
        (query_part, low(outer_sum(query_a, query_part))),
        (output_low, low(against(output_low, output_b))),
        SimpleNamespace(down_weight=down_grad_low, gate_expand=gate_b_grad, up_expand=up_b_grad),
    )
    key_own, value_own = few[:, :head], few[:, head : 2 * head]
    query_a_own, gate_a_own, up_a_own = (
        few[:, 2 * head + i * rank : 2 * head + (i + 1) * rank] for i in range(3)
    )
    place = 2 * head + 3 * rank
    key_b_own = few[:, place + 64 : place + 96].reshape(-1, head)
    value_b_own = few[:, place + 96 : place + 128].reshape(-1, head)
    high = rank // count

    def unfold(array):
        return jnp.concatenate([array[i] for i in range(4)], axis=1)

    def own_part(gain):
        return lax.dynamic_slice_in_dim(gain.astype(jnp.float32), mp * share, share, 0)

    key_a_own = against(low(key_own), key_b)
    value_a_own = against(low(value_own), value_b)
    wider = jnp.float32
    own_gain = feedforward_gain.astype(wider)[:, None]
    return (
        result,
        input_grad,
        few[:, place] / own_part(attention_gain),
        query_sum[: deep // count],
        key_own,
        value_own,
        output_sum[:wide],
        query_a_own,
        query_sum[deep // count :],
        key_a_own,
        key_b_own,
        value_a_own,
        value_b_own,
        output_sum[wide:],
        unfold(shared[:, :high]),
        few[:, place + 32] / own_part(feedforward_gain),
        own_gain * gate_own.astype(wider),
        own_gain * up_own.astype(wider),
        units.down_weight.astype(wider),
        gate_a_own,
        units.gate_expand.astype(wider),
        up_a_own,
        units.up_expand.astype(wider),
        down_shrink_grad,
        unfold(shared[:, high:]),
    )


def body(
    layer_input,
    output_grad,
    attention_gain,
    query_weight,
    key_weight,
    value_weight,
    output_weight,
    query_shrink,
    query_expand,
    key_shrink,
    key_expand,
    value_shrink,
    value_expand,
    output_shrink,
    output_expand,
    feedforward_gain,
    gate_weight,
    up_weight,
    down_weight,
    gate_shrink,
    gate_expand,
    up_shrink,
    up_expand,
    down_shrink,
    down_expand,
    group_ids,
    positions,
    segments,
):
    rows_local = layer_input.shape[0]
    own_start = lax.axis_index("mp") * rows_local
    allowed = (
        (group_ids[:, None] == group_ids[None, :])
        & (positions[None, :] <= positions[:, None])
        & ((segments[None, :] == 0) | (segments[None, :] == segments[:, None]))
    )

    def gather_attention():
        return (
            lax.all_gather(attention_gain, "dp", axis=0, tiled=True),
            lax.all_gather(query_weight, "dp", axis=0, tiled=True),
            lax.all_gather(key_weight, "dp", axis=0, tiled=True),
            lax.all_gather(value_weight, "dp", axis=0, tiled=True),
            lax.all_gather(output_weight, "dp", axis=1, tiled=True),
            lax.all_gather(query_shrink, "dp", axis=0, tiled=True),
            lax.all_gather(query_expand, "dp", axis=0, tiled=True),
            lax.all_gather(key_shrink, "dp", axis=0, tiled=True),
            lax.all_gather(key_expand, "dp", axis=0, tiled=True),
            lax.all_gather(value_shrink, "dp", axis=0, tiled=True),
            lax.all_gather(value_expand, "dp", axis=0, tiled=True),
            lax.all_gather(output_shrink, "dp", axis=0, tiled=True),
            lax.all_gather(output_expand, "dp", axis=0, tiled=True),
        )

    def gather_feed():
        return (
            lax.all_gather(feedforward_gain, "dp", axis=0, tiled=True),
            lax.all_gather(gate_weight, "dp", axis=0, tiled=True),
            lax.all_gather(up_weight, "dp", axis=0, tiled=True),
            lax.all_gather(down_weight, "dp", axis=1, tiled=True),
            lax.all_gather(gate_shrink, "dp", axis=0, tiled=True),
            lax.all_gather(gate_expand, "dp", axis=0, tiled=True),
            lax.all_gather(up_shrink, "dp", axis=0, tiled=True),
            lax.all_gather(up_expand, "dp", axis=0, tiled=True),
            lax.all_gather(down_shrink, "dp", axis=0, tiled=True),
            lax.all_gather(down_expand, "dp", axis=0, tiled=True),
        )

    def gather_rows(rows):
        return lax.all_gather(rows, "mp", axis=0, tiled=True)

    def gather_grads(rows):
        return lax.all_gather(rows, "mp", axis=0, tiled=True)

    def scatter_grads(term):
        return lax.psum_scatter(
            term(jnp.int32(0), lax.axis_size("mp") * rows_local),
            "mp",
            scatter_dimension=0,
            tiled=True,
        )

    def project_out(mixed, weight, shrink, expand):
        reduced = lax.psum(matmul(mixed, shrink), "mp").astype(jnp.bfloat16)

        def term(start, count):
            return matmul(mixed, weight)

        branch = lax.psum_scatter(
            term(jnp.int32(0), lax.axis_size("mp") * rows_local),
            "mp",
            scatter_dimension=0,
            tiled=True,
        )
        own = lax.dynamic_slice_in_dim(reduced, own_start, rows_local, 0)
        return (branch + matmul(own, expand), reduced)

    def masked_scores(queries, keys_rot):
        scores = jnp.einsum("thd,sd->hts", queries, keys_rot, preferred_element_type=jnp.float32)
        return jnp.where(allowed[None], scores, -1e30)

    def attention_forward(rows_in, params):
        (
            gain_one,
            w_query,
            w_key,
            w_value,
            w_output,
            query_a,
            query_b,
            key_a,
            key_b,
            value_a,
            value_b,
            output_a,
            output_b,
        ) = params
        normed = gather_rows(norm_rows(rows_in, gain_one.astype(jnp.float32)).astype(jnp.bfloat16))
        tokens = normed.shape[0]
        head_size = w_key.shape[1]
        heads = w_query.shape[1] // head_size
        query_low = matmul(normed, query_a).astype(jnp.bfloat16)
        key_low = matmul(normed, key_a).astype(jnp.bfloat16)
        value_low = matmul(normed, value_a).astype(jnp.bfloat16)
        query_lin = matmul(normed, w_query) + matmul(query_low, query_b)
        key_lin = matmul(normed, w_key) + matmul(key_low, key_b)
        value_lin = matmul(normed, w_value) + matmul(value_low, value_b)
        queries = (
            rotary(query_lin.reshape(tokens, heads, head_size), positions, 1.0)
            * head_size ** (-0.5)
        ).astype(jnp.bfloat16)
        keys_rot = rotary(key_lin[:, None, :], positions, 1.0)[:, 0, :].astype(jnp.bfloat16)
        values = value_lin.astype(jnp.bfloat16)
        scores = masked_scores(queries, keys_rot)
        highest = jnp.max(scores, axis=-1, keepdims=True)
        expo = jnp.exp(scores - highest)
        totals = jnp.sum(expo, axis=-1, keepdims=True)
        probability = expo / totals
        logsum = highest + jnp.log(totals)
        mixed = jnp.einsum(
            "hts,sd->thd",
            probability.astype(jnp.bfloat16),
            values,
            preferred_element_type=jnp.float32,
        )
        mixed = mixed.reshape(tokens, heads * head_size).astype(jnp.bfloat16)
        branch, reduced = project_out(mixed, w_output, output_a, output_b)
        saved = (
            normed,
            query_low,
            key_low,
            value_low,
            queries,
            keys_rot,
            values,
            logsum,
            mixed,
            reduced,
        )
        return (rows_in + branch, saved)

    def feed_forward(middle, params):
        gain_two, w_gate, w_up, w_down, gate_a, gate_b, up_a, up_b, down_a, down_b = params
        normed = gather_rows(norm_rows(middle, gain_two.astype(jnp.float32)).astype(jnp.bfloat16))
        gate_low = matmul(normed, gate_a).astype(jnp.bfloat16)
        up_low = matmul(normed, up_a).astype(jnp.bfloat16)
        gate_pre = matmul(normed, w_gate) + matmul(gate_low, gate_b)
        up_pre = matmul(normed, w_up) + matmul(up_low, up_b)
        hidden = (jax.nn.gelu(gate_pre, approximate=True) * up_pre).astype(jnp.bfloat16)
        branch, reduced = project_out(hidden, w_down, down_a, down_b)
        return (middle + branch, (normed, gate_low, up_low, gate_pre, up_pre, hidden, reduced))

    rows_in = layer_input.astype(jnp.float32)
    attention_params = gather_attention()
    middle, attention_saved = attention_forward(rows_in, attention_params)
    feed_params = gather_feed()
    result, feed_saved = feed_forward(middle, feed_params)
    feed_params = gather_feed()
    feed_saved = feed_forward(middle, feed_params)[1]
    gain_two, w_gate, w_up, w_down, gate_a, gate_b, up_a, up_b, down_a, down_b = feed_params
    normed_feed, gate_low, up_low, gate_pre, up_pre, hidden, reduced_feed = feed_saved
    grad_branch_feed = gather_grads(output_grad)
    down_weight_grad = outer_sum(hidden, grad_branch_feed)
    down_expand_grad = outer_sum(reduced_feed, grad_branch_feed)
    grad_reduced_feed = against(grad_branch_feed, down_b).astype(jnp.bfloat16)
    down_shrink_grad = outer_sum(hidden, grad_reduced_feed)
    grad_hidden = against(grad_branch_feed, w_down) + against(grad_reduced_feed, down_a)
    unused, gelu_pull = jax.vjp(
        lambda gated, upper: jax.nn.gelu(gated, approximate=True) * upper, gate_pre, up_pre
    )
    grad_gate, grad_up = gelu_pull(grad_hidden)
    grad_gate = grad_gate.astype(jnp.bfloat16)
    grad_up = grad_up.astype(jnp.bfloat16)
    gate_expand_grad = outer_sum(gate_low, grad_gate)
    up_expand_grad = outer_sum(up_low, grad_up)
    grad_gate_low = against(grad_gate, gate_b)
    grad_up_low = against(grad_up, up_b)
    feed_wide = normed_feed.astype(jnp.float32)
    gate_shrink_grad = outer_exact(feed_wide, grad_gate_low)
    up_shrink_grad = outer_exact(feed_wide, grad_up_low)
    gate_a_wide = gate_a.astype(jnp.float32)
    up_a_wide = up_a.astype(jnp.float32)

    def feed_term(start, count):

        def pick(rows):
            return rows

        total = against(pick(grad_gate), w_gate) + against(pick(grad_up), w_up)
        return (
            total
            + against_exact(pick(grad_gate_low), gate_a_wide)
            + against_exact(pick(grad_up_low), up_a_wide)
        )

    grad_normed_feed = scatter_grads(feed_term)
    unused, norm_pull = jax.vjp(norm_rows, middle, gain_two.astype(jnp.float32))
    grad_middle_part, feed_gain_grad = norm_pull(grad_normed_feed)
    grad_middle = output_grad.astype(jnp.float32) + grad_middle_part
    gate_weight_grad = outer_sum(normed_feed, grad_gate)
    up_weight_grad = outer_sum(normed_feed, grad_up)
    feed_split = (
        lax.psum_scatter(
            gate_weight_grad.astype(jnp.bfloat16), "dp", scatter_dimension=0, tiled=True
        ).astype(jnp.float32),
        lax.psum_scatter(
            up_weight_grad.astype(jnp.bfloat16), "dp", scatter_dimension=0, tiled=True
        ).astype(jnp.float32),
        lax.psum_scatter(
            down_weight_grad.astype(jnp.bfloat16), "dp", scatter_dimension=1, tiled=True
        ).astype(jnp.float32),
        lax.psum_scatter(
            gate_expand_grad.astype(jnp.bfloat16), "dp", scatter_dimension=0, tiled=True
        ).astype(jnp.float32),
        lax.psum_scatter(
            up_expand_grad.astype(jnp.bfloat16), "dp", scatter_dimension=0, tiled=True
        ).astype(jnp.float32),
        lax.psum_scatter(
            down_shrink_grad.astype(jnp.bfloat16), "dp", scatter_dimension=0, tiled=True
        ).astype(jnp.float32),
        lax.psum_scatter(
            down_expand_grad.astype(jnp.bfloat16), "dp", scatter_dimension=0, tiled=True
        ).astype(jnp.float32),
    )
    gate_weight_own, up_weight_own = (feed_split[0], feed_split[1])
    down_weight_own, gate_expand_own, up_expand_own, down_shrink_own, down_expand_own = (
        feed_split[2],
        feed_split[3],
        feed_split[4],
        feed_split[5],
        feed_split[6],
    )
    feed_shared = (
        lax.psum_scatter(feed_gain_grad, ("dp", "mp"), scatter_dimension=0, tiled=True),
        lax.psum_scatter(gate_shrink_grad, ("dp", "mp"), scatter_dimension=0, tiled=True),
        lax.psum_scatter(up_shrink_grad, ("dp", "mp"), scatter_dimension=0, tiled=True),
    )
    attention_params = gather_attention()
    attention_saved = attention_forward(rows_in, attention_params)[1]
    (
        gain_one,
        w_query,
        w_key,
        w_value,
        w_output,
        query_a,
        query_b,
        key_a,
        key_b,
        value_a,
        value_b,
        output_a,
        output_b,
    ) = attention_params
    normed, query_low, key_low, value_low, queries, keys_rot, values, logsum, mixed, reduced = (
        attention_saved
    )
    tokens = normed.shape[0]
    head_size = w_key.shape[1]
    heads = w_query.shape[1] // head_size
    grad_branch = gather_grads(grad_middle.astype(jnp.bfloat16))
    output_weight_grad = outer_sum(mixed, grad_branch)
    output_expand_grad = outer_sum(reduced, grad_branch)
    grad_reduced = against(grad_branch, output_b).astype(jnp.bfloat16)
    output_shrink_grad = outer_sum(mixed, grad_reduced)
    grad_mixed = (against(grad_branch, w_output) + against(grad_reduced, output_a)).astype(
        jnp.bfloat16
    )
    grad_mixed = grad_mixed.reshape(tokens, heads, head_size)
    probability = jnp.exp(masked_scores(queries, keys_rot) - logsum)
    grad_values = jnp.einsum(
        "hts,thd->sd",
        probability.astype(jnp.bfloat16),
        grad_mixed,
        preferred_element_type=jnp.float32,
    )
    grad_probability = jnp.einsum(
        "thd,sd->hts", grad_mixed, values, preferred_element_type=jnp.float32
    )
    grad_scores = probability * (
        grad_probability - jnp.sum(probability * grad_probability, axis=-1, keepdims=True)
    )
    grad_scores = grad_scores.astype(jnp.bfloat16)
    grad_queries_rot = jnp.einsum(
        "hts,sd->thd", grad_scores, keys_rot, preferred_element_type=jnp.float32
    )
    grad_keys_rot = jnp.einsum(
        "hts,thd->sd", grad_scores, queries, preferred_element_type=jnp.float32
    )
    grad_query = (
        rotary(grad_queries_rot * head_size ** (-0.5), positions, -1.0)
        .reshape(tokens, heads * head_size)
        .astype(jnp.bfloat16)
    )
    grad_key = rotary(grad_keys_rot[:, None, :], positions, -1.0)[:, 0, :]
    normed_wide = normed.astype(jnp.float32)
    query_weight_grad = outer_sum(normed, grad_query)
    query_expand_grad = outer_sum(query_low, grad_query)
    grad_query_low = against(grad_query, query_b)
    query_shrink_grad = outer_exact(normed_wide, grad_query_low)
    key_weight_grad = outer_exact(normed_wide, grad_key)
    key_expand_grad = outer_exact(key_low.astype(jnp.float32), grad_key)
    grad_key_low = against_exact(grad_key, key_b.astype(jnp.float32))
    key_shrink_grad = outer_exact(normed_wide, grad_key_low)
    value_weight_grad = outer_exact(normed_wide, grad_values)
    value_expand_grad = outer_exact(value_low.astype(jnp.float32), grad_values)
    grad_value_low = against_exact(grad_values, value_b.astype(jnp.float32))
    value_shrink_grad = outer_exact(normed_wide, grad_value_low)
    query_a_wide = query_a.astype(jnp.float32)
    key_wide = w_key.astype(jnp.float32)
    key_a_wide = key_a.astype(jnp.float32)
    value_wide = w_value.astype(jnp.float32)
    value_a_wide = value_a.astype(jnp.float32)

    def attention_term(start, count):

        def pick(rows):
            return rows

        total = against(pick(grad_query), w_query) + against_exact(
            pick(grad_query_low), query_a_wide
        )
        total = (
            total
            + against_exact(pick(grad_key), key_wide)
            + against_exact(pick(grad_key_low), key_a_wide)
        )
        return (
            total
            + against_exact(pick(grad_values), value_wide)
            + against_exact(pick(grad_value_low), value_a_wide)
        )

    grad_normed = scatter_grads(attention_term)
    unused, norm_pull_one = jax.vjp(norm_rows, rows_in, gain_one.astype(jnp.float32))
    grad_input_part, attention_gain_grad = norm_pull_one(grad_normed)
    input_grad = grad_middle + grad_input_part
    attention_split = (
        lax.psum_scatter(
            query_weight_grad.astype(jnp.bfloat16), "dp", scatter_dimension=0, tiled=True
        ).astype(jnp.float32),
        lax.psum_scatter(
            output_weight_grad.astype(jnp.bfloat16), "dp", scatter_dimension=1, tiled=True
        ).astype(jnp.float32),
        lax.psum_scatter(
            query_expand_grad.astype(jnp.bfloat16), "dp", scatter_dimension=0, tiled=True
        ).astype(jnp.float32),
        lax.psum_scatter(
            output_shrink_grad.astype(jnp.bfloat16), "dp", scatter_dimension=0, tiled=True
        ).astype(jnp.float32),
        lax.psum_scatter(
            output_expand_grad.astype(jnp.bfloat16), "dp", scatter_dimension=0, tiled=True
        ).astype(jnp.float32),
    )
    attention_shared = (
        lax.psum_scatter(attention_gain_grad, ("dp", "mp"), scatter_dimension=0, tiled=True),
        lax.psum_scatter(key_weight_grad, ("dp", "mp"), scatter_dimension=0, tiled=True),
        lax.psum_scatter(value_weight_grad, ("dp", "mp"), scatter_dimension=0, tiled=True),
        lax.psum_scatter(query_shrink_grad, ("dp", "mp"), scatter_dimension=0, tiled=True),
        lax.psum_scatter(key_shrink_grad, ("dp", "mp"), scatter_dimension=0, tiled=True),
        lax.psum_scatter(key_expand_grad, ("dp", "mp"), scatter_dimension=0, tiled=True),
        lax.psum_scatter(value_shrink_grad, ("dp", "mp"), scatter_dimension=0, tiled=True),
        lax.psum_scatter(value_expand_grad, ("dp", "mp"), scatter_dimension=0, tiled=True),
    )
    return (
        result.astype(jnp.bfloat16),
        input_grad,
        attention_shared[0],
        attention_split[0],
        attention_shared[1],
        attention_shared[2],
        attention_split[1],
        attention_shared[3],
        attention_split[2],
        attention_shared[4],
        attention_shared[5],
        attention_shared[6],
        attention_shared[7],
        attention_split[3],
        attention_split[4],
        feed_shared[0],
        gate_weight_own,
        up_weight_own,
        down_weight_own,
        feed_shared[1],
        gate_expand_own,
        feed_shared[2],
        up_expand_own,
        down_shrink_own,
        down_expand_own,
    )


def solution(mesh):
    levels = mesh.shape["dp"] // 2
    few = mesh.shape["mp"] == 4 and mesh.shape["dp"] % 2 == 0 and levels <= 4
    step = functools.partial(by_unit, levels) if few else body
    placed = (
        P(("dp", "mp"), None),
        P(("dp", "mp"), None),
        P("dp"),
        P("dp", "mp"),
        P("dp", None),
        P("dp", None),
        P("mp", "dp"),
        P("dp", None),
        P("dp", "mp"),
        P("dp", None),
        P("dp", None),
        P("dp", None),
        P("dp", None),
        P(("mp", "dp"), None),
        P("dp", None),
        P("dp"),
        P("dp", "mp"),
        P("dp", "mp"),
        P("mp", "dp"),
        P("dp", None),
        P("dp", "mp"),
        P("dp", None),
        P("dp", "mp"),
        P(("mp", "dp"), None),
        P("dp", None),
        P("dp"),
        P("dp"),
        P("dp"),
    )
    return jax.shard_map(
        step,
        mesh=mesh,
        in_specs=placed,
        out_specs=(
            P(("dp", "mp"), None),
            P(("dp", "mp"), None),
            P(("dp", "mp")),
            P("dp", "mp"),
            P(("dp", "mp"), None),
            P(("dp", "mp"), None),
            P("mp", "dp"),
            P(("dp", "mp"), None),
            P("dp", "mp"),
            P(("dp", "mp"), None),
            P(("dp", "mp"), None),
            P(("dp", "mp"), None),
            P(("dp", "mp"), None),
            P(("mp", "dp"), None),
            P("dp", None),
            P(("dp", "mp")),
            P("dp", "mp"),
            P("dp", "mp"),
            P("mp", "dp"),
            P(("dp", "mp"), None),
            P("dp", "mp"),
            P(("dp", "mp"), None),
            P("dp", "mp"),
            P(("mp", "dp"), None),
            P("dp", None),
        ),
        check_vma=False,
    )
```

```python
import functools
import math
from types import SimpleNamespace

import jax
import jax.numpy as jnp
from jax import lax
from jax.experimental import pallas as pl
from jax.experimental.pallas import tpu as pltpu
from jax.sharding import PartitionSpec as P

MESH = pl.DeviceIdType.MESH
MIB = 1 << 20

EPS = 1e-06


def matmul(left, right):
    return jnp.dot(left, right, preferred_element_type=jnp.float32)


def against(left, right):
    return lax.dot_general(
        left, right, (((1,), (1,)), ((), ())), preferred_element_type=jnp.float32
    )


def outer_sum(left, right):
    return lax.dot_general(
        left, right, (((0,), (0,)), ((), ())), preferred_element_type=jnp.float32
    )


def against_exact(left, right):
    return lax.dot_general(
        left,
        right,
        (((1,), (1,)), ((), ())),
        precision=lax.Precision.HIGHEST,
        preferred_element_type=jnp.float32,
    )


def outer_exact(left, right):
    return lax.dot_general(
        left,
        right,
        (((0,), (0,)), ((), ())),
        precision=lax.Precision.HIGHEST,
        preferred_element_type=jnp.float32,
    )


def norm_rows(rows, gain):
    return rows * lax.rsqrt(jnp.mean(rows * rows, axis=-1, keepdims=True) + EPS) * gain


def rotary(entries, places, sign):
    half = entries.shape[-1] // 2
    freq = 10000.0 ** (-jnp.arange(half).astype(jnp.float32) * 2.0 / entries.shape[-1])
    angle = places.astype(jnp.float32)[:, None] * freq[None, :]
    cosine = jnp.cos(angle)[:, None, :]
    sine = sign * jnp.sin(angle)[:, None, :]
    first = entries[..., :half]
    second = entries[..., half:]
    return jnp.concatenate(
        [first * cosine - second * sine, second * cosine + first * sine], axis=-1
    )


class Wires:
    def __init__(self, levels, sends, lands, locals_=None):
        self.sends, self.lands, self.locals = sends, lands, locals_
        self.levels = levels
        self.count = self.local_count = 0
        self.open = []
        dp, mp = lax.axis_index("dp"), lax.axis_index("mp")
        self.dp, self.mp = dp, mp
        self.z, self.y, self.x, self.c = dp // 2, dp % 2, mp // 2, mp % 2

    def take(self, number=1):
        first = self.count
        self.count += number
        assert self.count <= self.sends.shape[0], self.count
        return first

    def at(self, z, y, x, c):
        return (z * 2 + y, x * 2 + c)

    def up(self):
        return self.at(self.z + 1, self.y, self.x, self.c)

    def down(self):
        return self.at(self.z - 1, self.y, self.x, self.c)

    def over_x(self):
        return self.at(self.z, self.y, 1 - self.x, self.c)

    def over_y(self):
        return self.at(self.z, 1 - self.y, self.x, self.c)

    def over_core(self):
        return self.at(self.z, self.y, self.x, 1 - self.c)

    def copy(self, source, target, out, land, device):
        return pltpu.make_async_remote_copy(
            src_ref=source,
            dst_ref=target,
            send_sem=self.sends.at[out],
            recv_sem=self.lands.at[land],
            device_id=device,
            device_id_type=MESH,
        )

    def send(self, source, target, out, land, device, when=True):
        made = self.copy(source, target, out, land, device)
        under(when, made.start)
        self.open.append((when, made.wait_send))

    def landed(self, target, land):
        self.copy(target, target, land, land, self.over_x()).wait_recv()

    def local(self, source, target):
        made = pltpu.make_async_copy(source, target, self.locals.at[self.local_count])
        self.local_count += 1
        assert self.local_count <= self.locals.shape[0], self.local_count
        made.start()
        return made

    def take_local(self, number):
        first = self.local_count
        self.local_count += number
        assert self.local_count <= self.locals.shape[0], self.local_count
        return first

    def finish(self):
        for when, wait in self.open:
            under(when, wait)

    def greet(self, far=False, flat=False):
        barrier = pltpu.get_barrier_semaphore()

        def call(device):
            pl.semaphore_signal(barrier, inc=1, device_id=device, device_id_type=MESH)

        call(self.over_x())
        call(self.over_core())
        if far:
            call(self.at(self.z, self.y, 1 - self.x, 1 - self.c))
            for step in range(1, 2 * self.levels):
                call((lax.rem(self.dp + step, 2 * self.levels), self.mp))
            pl.semaphore_wait(barrier, 2 + 2 * self.levels)
            return
        if flat:
            pl.semaphore_wait(barrier, 2)
            return
        call(self.over_y())
        pl.when(self.z > 0)(lambda: call(self.down()))
        pl.when(self.z < self.levels - 1)(lambda: call(self.up()))
        ends = jnp.where(self.z > 0, 1, 0) + jnp.where(self.z < self.levels - 1, 1, 0)
        pl.semaphore_wait(barrier, 3 + ends)


def under(when, act):
    if when is True:
        act()
    else:
        pl.when(when)(act)


def sides(w, step):
    yield (True, w.z - step, w.z >= step)
    yield (False, w.z + step, w.z < w.levels - step)


def gather_all(w, own, at, parts):
    z, y, x, c = w.z, w.y, w.x, w.c
    n = w.levels
    rise, fall, by_x, by_y, last_x, last_y = (w.take(n) for _ in range(6))
    by_core = w.take(4 * n)

    def core(block, zs, ys, xs):
        place = by_core + zs * 4 + ys * 2 + xs
        return (block, block, place, place, w.over_core())

    here = at(z, y, x, c)
    kept = w.local(own, here) if own is not None else None
    own = here if own is None else own
    w.send(own, here, rise + z, rise + z, w.up(), z < n - 1)
    w.send(own, here, fall + z, fall + z, w.down(), z > 0)
    w.send(own, here, by_x + z, by_x + z, w.over_x())
    w.send(own, here, by_y + z, by_y + z, w.over_y())
    place = by_core + z * 4 + y * 2 + x
    w.send(own, here, place, place, w.over_core())
    yield

    def plane(zs, ok):
        block = at(zs, y, 1 - x, c)
        under(ok, lambda: w.landed(block, by_x + zs))
        for piece in parts(block)[:1]:
            if piece is not None:
                w.send(piece, piece, last_y + zs, last_y + zs, w.over_y(), ok)
        w.send(*core(block, zs, y, 1 - x), ok)
        block = at(zs, 1 - y, x, c)
        under(ok, lambda: w.landed(block, by_y + zs))
        for piece in parts(block)[1:]:
            if piece is not None:
                w.send(piece, piece, last_x + zs, last_x + zs, w.over_x(), ok)
        w.send(*core(block, zs, 1 - y, x), ok)

    plane(z, True)
    yield
    for step in range(1, n):
        for rising, zs, ok in sides(w, step):
            block = at(zs, y, x, c)
            lane = rise if rising else fall
            under(ok, lambda: w.landed(block, lane + zs))
            if rising:
                w.send(block, block, rise + zs, rise + zs, w.up(), jnp.logical_and(ok, z < n - 1))
            else:
                w.send(block, block, fall + zs, fall + zs, w.down(), jnp.logical_and(ok, z > 0))
            w.send(block, block, by_x + zs, by_x + zs, w.over_x(), ok)
            w.send(block, block, by_y + zs, by_y + zs, w.over_y(), ok)
            w.send(*core(block, zs, y, x), ok)
        yield
        for _, zs, ok in sides(w, step):
            plane(zs, ok)
        yield
    for step in range(n):
        for _, zs, ok in sides(w, step) if step else [(True, z, True)]:
            block = at(zs, 1 - y, 1 - x, c)
            for piece, lane in zip(parts(block), (last_y, last_x)):
                if piece is not None:
                    under(ok, lambda: w.landed(piece, lane + zs))
            w.send(*core(block, zs, 1 - y, 1 - x), ok)
        yield
    for zs in range(n):
        for ys in range(2):
            for xs in range(2):
                w.landed(at(zs, ys, xs, 1 - c), by_core + zs * 4 + ys * 2 + xs)
    if kept is not None:
        kept.wait()


def gather_dp(w, own, at):
    z, y, n = w.z, w.y, w.levels
    rise, fall, by_y = (w.take(n) for _ in range(3))
    here = at(z, y)
    kept = w.local(own, here)
    w.send(own, here, rise + z, rise + z, w.up(), z < n - 1)
    w.send(own, here, fall + z, fall + z, w.down(), z > 0)
    w.send(own, here, by_y + z, by_y + z, w.over_y())
    yield
    yield
    for step in range(1, n):
        for rising, zs, ok in sides(w, step):
            block = at(zs, y)
            lane = rise if rising else fall
            under(ok, lambda: w.landed(block, lane + zs))
            if rising:
                w.send(block, block, rise + zs, rise + zs, w.up(), jnp.logical_and(ok, z < n - 1))
            else:
                w.send(block, block, fall + zs, fall + zs, w.down(), jnp.logical_and(ok, z > 0))
            w.send(block, block, by_y + zs, by_y + zs, w.over_y(), ok)
        yield
        yield
    for zs in range(n):
        w.landed(at(zs, 1 - y), by_y + zs)
    kept.wait()


def gather_mp(w, own, at):
    x, c = w.x, w.c
    first, second = w.take(), w.take(2)
    here = at(x, c)
    kept = w.local(own, here)
    w.send(own, here, first, first, w.over_x())
    w.send(own, here, second, second, w.over_core())
    yield
    block = at(1 - x, c)
    w.landed(block, first)
    w.send(block, block, second + 1, second + 1, w.over_core())
    yield
    w.landed(at(x, 1 - c), second)
    w.landed(at(1 - x, 1 - c), second + 1)
    kept.wait()


def exchange_dp(w, source, target):
    count = 2 * w.levels
    first = w.take(count)
    kept = w.local(source(w.dp), target(w.dp))
    for step in range(1, count):
        there = lax.rem(w.dp + step, count)
        w.send(source(there), target(w.dp), first + step, first + step, (there, w.mp))
        yield
    for step in range(1, count):
        w.landed(target(lax.rem(w.dp + count - step, count)), first + step)
    kept.wait()


PACE = 4


def turn(steps, after=(), pace=PACE):
    spare = [one for one in after for _ in range(7)]
    turn_on(steps, spare, pace)
    for one in spare:
        next(one)
    turn_on(after)


def turn_on(steps, spare=(), pace=0):
    steps = list(steps)
    while steps:
        for _ in range(min(pace, len(spare))):
            next(spare.pop(0))
        left = []
        for one in steps:
            try:
                next(one)
                left.append(one)
            except StopIteration:
                pass
        steps = left


CHUNK = 16


def add_up(target, *sources):
    rows = target.shape[0]

    def one(i, unused):
        part = pl.ds(pl.multiple_of(i * CHUNK, CHUNK), CHUNK)
        total = sources[0][part, :].astype(jnp.float32)
        for source in sources[1:]:
            total = total + source[part, :].astype(jnp.float32)
        target[part, :] = total.astype(target.dtype)
        return unused

    lax.fori_loop(0, rows // CHUNK, one, 0)


def planes(w):
    z, n = w.z, w.levels
    for k in range(n - 1):
        falling = n - 1 - k
        low_half = jnp.where(falling > z, falling, falling - 1)
        high_half = jnp.where(k < z, k, k + 1)
        yield jnp.where(z < n // 2, low_half, high_half)
    yield z


def scatter_all(w, part, landing, own, core, half_x, half_y, full_x, full_y, below, above, out, make=None):
    z, y, x, c, n = w.z, w.y, w.x, w.c, w.levels
    to_core, to_hx, to_hy, to_fx, to_fy = (w.take(4 * n), w.take(n), w.take(n), w.take(n), w.take(n))
    rise, fall = w.take(n), w.take(n)
    from_part, from_landing = w.take_local(4 * n), w.take_local(4 * n)
    rows = own.shape[1]
    cut = rows // 2 // CHUNK * CHUNK
    first, second = pl.ds(0, cut), pl.ds(cut, rows - cut)
    kinds = ((1 - y, 1 - x), (1 - y, x), (y, 1 - x), (y, x))
    order = list(planes(w))
    kept = {}

    def start(k):
        zs = order[k]
        for kind, (ys, xs) in enumerate(kinds):
            here = k * 4 + kind
            lane = to_core + here
            for source, into in part(zs, ys, xs, 1 - c):
                w.copy(source, into(landing.at[here]), lane, lane, w.over_core()).start()
            w.open.append((True, w.copy(landing.at[here], landing.at[here], lane, lane, w.over_core()).wait_send))
            for source, into in part(zs, ys, xs, c):
                pltpu.make_async_copy(source, into(own.at[here]), w.locals.at[from_part + here]).start()
            kept[here] = pltpu.make_async_copy(landing.at[here], own.at[here], w.locals.at[from_part + here])

    def join(k):
        loads = []
        for kind in range(4):
            here = k * 4 + kind
            w.landed(landing.at[here], to_core + here)
            load = pltpu.make_async_copy(landing.at[here], core.at[kind], w.locals.at[from_landing + here])
            load.start()
            loads.append(load)
        for kind in range(4):
            here = k * 4 + kind
            kept[here].wait()
            loads[kind].wait()
            add_up(own.at[here], own.at[here], core.at[kind])
            if kind == 0:
                w.send(own.at[here, first], half_x.at[k], to_hx + k, to_hx + k, w.over_x())
                w.send(own.at[here, second], half_y.at[k], to_hy + k, to_hy + k, w.over_y())

    def across(k):
        here = k * 4 + 1
        w.landed(half_x.at[k], to_hx + k)
        add_up(own.at[here, first], own.at[here, first], half_x.at[k])
        w.send(own.at[here], full_y.at[k], to_fy + k, to_fy + k, w.over_y())
        here = k * 4 + 2
        w.landed(half_y.at[k], to_hy + k)
        add_up(own.at[here, second], own.at[here, second], half_y.at[k])
        w.send(own.at[here], full_x.at[k], to_fx + k, to_fx + k, w.over_x())

    def along(k):
        zs, here = order[k], own.at[k * 4 + 3]
        w.landed(full_x.at[k], to_fx + k)
        w.landed(full_y.at[k], to_fy + k)
        if k == n - 1:
            add_up(here, here, full_x.at[k], full_y.at[k])
            return
        pass_on(w, zs, here, (full_x.at[k], full_y.at[k]), below, above, rise, fall)

    for k in range(n + 3):
        if make is not None:
            yield from make(k)
        if k < n:
            start(k)
            yield
        for lag, act in ((1, join), (2, across), (3, along)):
            if 0 <= k - lag < n:
                act(k - lag)
                yield
    last_sum(w, own.at[4 * n - 1], (), below, above, rise, fall, out)


def pass_on(w, zs, here, sources, below, above, rise, fall):
    z, n = w.z, w.levels
    rising, falling = zs > z, zs < z
    more_up, more_down = jnp.logical_and(rising, z > 0), jnp.logical_and(falling, z < n - 1)

    def take_below():
        w.landed(below.at[zs - 1], rise + zs)
        add_up(here, here, *sources, below.at[zs - 1])

    def take_above():
        w.landed(above.at[zs], fall + zs)
        add_up(here, here, *sources, above.at[zs])

    under(more_up, take_below)
    under(more_down, take_above)
    under(
        jnp.logical_not(jnp.logical_or(more_up, more_down)), lambda: add_up(here, here, *sources)
    )
    w.send(here, below.at[zs - 1], rise + zs, rise + zs, w.up(), rising)
    w.send(here, above.at[zs], fall + zs, fall + zs, w.down(), falling)


def last_sum(w, here, sources, below, above, rise, fall, out):
    z, n = w.z, w.levels
    under(z > 0, lambda: w.landed(below.at[z - 1], rise + z))
    under(z < n - 1, lambda: w.landed(above.at[z], fall + z))
    under(z == 0, lambda: add_up(out, here, *sources, above.at[z]))
    under(z == n - 1, lambda: add_up(out, here, *sources, below.at[z - 1]))
    under(
        jnp.logical_and(z > 0, z < n - 1),
        lambda: add_up(out, here, *sources, below.at[z - 1], above.at[z]),
    )


def scatter_all_scratch(n, rows, columns):
    cut = rows // 2 // CHUNK * CHUNK
    shapes = [(4 * n, rows), (4, rows), (n, cut), (n, rows - cut)] + [(n, rows)] * 2 + [(n - 1, rows)] * 2
    return [pltpu.VMEM(shape + (columns,), jnp.bfloat16) for shape in shapes]


def scatter_dp(w, part, own, over, below, above, out):
    y, n = w.y, w.levels
    by_y, rise, fall, spare = w.take(n), w.take(n), w.take(n), w.take_local(n)
    order = list(planes(w))
    for k, zs in enumerate(order):
        for source, into in part(zs, 1 - y):
            w.copy(source, into(over.at[k]), by_y + k, by_y + k, w.over_y()).start()
        w.open.append((True, w.copy(over.at[k], over.at[k], by_y + k, by_y + k, w.over_y()).wait_send))
        for source, into in part(zs, y):
            pltpu.make_async_copy(source, into(own.at[k]), w.locals.at[spare + k]).start()
        yield
    for k, zs in enumerate(order):
        pltpu.make_async_copy(over.at[k], own.at[k], w.locals.at[spare + k]).wait()
        w.landed(over.at[k], by_y + k)
        if k < n - 1:
            pass_on(w, zs, own.at[k], (over.at[k],), below, above, rise, fall)
            yield
    last_sum(w, own.at[n - 1], (over.at[n - 1],), below, above, rise, fall, out)


def scatter_mp(w, part, own, first, second, out):
    x, c = w.x, w.c
    core, cross = w.take(2), w.take()
    kept = []
    for i, xs in enumerate((1 - x, x)):
        w.send(part.at[xs * 2 + 1 - c], first.at[i], core + i, core + i, w.over_core())
        kept.append(w.local(part.at[xs * 2 + c], own.at[i]))
    yield
    kept[0].wait()
    w.landed(first.at[0], core)
    add_up(own.at[0], own.at[0], first.at[0])
    w.send(own.at[0], second, cross, cross, w.over_x())
    yield
    yield
    yield
    kept[1].wait()
    w.landed(first.at[1], core + 1)
    w.landed(second, cross)
    add_up(out, own.at[1], first.at[1], second)


VMEM = 62 * MIB
ANY = pl.BlockSpec(memory_space=pl.ANY)
WHOLE = pl.BlockSpec(memory_space=pltpu.VMEM)


def call(kernel, identity, arrays, outs, scratch, signals, locals_, in_vmem=False, name=None):
    return pl.pallas_call(
        kernel,
        out_shape=[jax.ShapeDtypeStruct(shape, kind) for shape, kind, _ in outs],
        in_specs=[ANY] * len(arrays),
        out_specs=[WHOLE if near else ANY for _, _, near in outs],
        scratch_shapes=list(scratch)
        + [
            pltpu.SemaphoreType.DMA((signals,)),
            pltpu.SemaphoreType.DMA((signals,)),
            pltpu.SemaphoreType.DMA((max(locals_, 1),)),
        ],
        compiler_params=pltpu.CompilerParams(
            collective_id=identity, has_side_effects=True, vmem_limit_bytes=VMEM
        ),
        name=name,
    )(*arrays)


def halves(block):
    rows = block.shape[0]
    cut = rows // 2 // CHUNK * CHUNK
    return (block.at[pl.ds(0, cut)], block.at[pl.ds(cut, rows - cut)])


def by_x_last(block):
    return (None, block)


def rows_of(ref, index, rows):
    return ref.at[pl.ds(pl.multiple_of(index * rows, rows), rows)]


def columns_of(ref, index, columns):
    return ref.at[:, pl.ds(pl.multiple_of(index * columns, columns), columns)]


def flat(z, y, x, c):
    return (z * 2 + y) * 4 + x * 2 + c


def one_block(array):
    return lambda z, y, x, c: [(array.at[flat(z, y, x, c)], lambda ref: ref)]


def corner(first, rows, column, columns):
    return lambda ref: ref.at[pl.ds(first, rows), pl.ds(column, columns)]


LAST = by_x_last


def begin(levels, tensors):
    names = list(vars(tensors))
    count = 2 * levels
    wide = tensors.query_weight.shape[1]
    unit = tensors.gate_weight.shape[1] // count
    deep = tensors.gate_weight.shape[0] * count
    rows = tensors.layer_input.shape[0]
    maps = list(tensors.maps)
    share = maps[0].shape[0] // 4
    packed = (share, sum(piece.shape[1] for piece in maps))
    del tensors.maps
    names = list(vars(tensors))
    low = tensors.gate_expand.shape[0] * count
    piece = deep // 4
    shapes = dict(
        layer_input=(4, rows, deep),
        maps=(4 * count * packed[0], packed[1]),
        output_expand=(low, deep),
        down_expand=(low, deep),
        query_weight=(deep, wide),
        output_weight=(wide, deep),
        expands=(low, tensors.expands.shape[1]),
        output_shrink=(tensors.output_shrink.shape[0] * count, low),
        output_grad=(4 * count, rows, deep),
        gate_weight=(deep, unit),
        up_weight=(deep, unit),
        down_weight=(unit, deep),
        gate_expand=(low, unit),
        up_expand=(low, unit),
    )

    def kernel(*refs):
        given = SimpleNamespace(**dict(zip(names, refs)))
        pieces = refs[len(names) : len(names) + len(maps)]
        refs = refs[len(names) + len(maps) :]
        got = SimpleNamespace(**dict(zip(shapes, refs)))
        w = Wires(levels, *refs[len(shapes) :])
        block = rows_of(got.maps, w.dp * 4 + w.mp, share)
        placed, column = [], 0
        for ref in pieces:
            target = block.at[:, pl.ds(column, ref.shape[1])]
            placed.append(w.local(rows_of(ref, w.mp, share), target))
            column += ref.shape[1]
        w.greet(far=True)
        for copy in placed:
            copy.wait()

        def expand_at(into):
            def at(z, y, x, c):
                return into.at[
                    pl.ds(pl.multiple_of((z * 2 + y) * (low // count), low // count), low // count),
                    pl.ds(pl.multiple_of((x * 2 + c) * piece, piece), piece),
                ]

            return at

        steps = [
            gather_mp(w, given.layer_input, lambda x, c: got.layer_input.at[x * 2 + c]),
            gather_dp(w, given.query_weight, lambda z, y: rows_of(got.query_weight, z * 2 + y, deep // count)),
            gather_dp(w, given.output_weight, lambda z, y: columns_of(got.output_weight, z * 2 + y, deep // count)),
            gather_all(w, None, lambda z, y, x, c: rows_of(got.maps, flat(z, y, x, c), packed[0]), LAST),
            gather_dp(w, given.expands, lambda z, y: rows_of(got.expands, z * 2 + y, low // count)),
            gather_dp(
                w,
                given.output_shrink,
                lambda z, y: rows_of(got.output_shrink, z * 2 + y, given.output_shrink.shape[0]),
            ),
        ]
        for own, into in ((given.output_expand, got.output_expand), (given.down_expand, got.down_expand)):
            steps.append(gather_all(w, columns_of(own, w.mp, piece), expand_at(into), LAST))
        steps.append(gather_all(w, given.output_grad, lambda z, y, x, c: got.output_grad.at[flat(z, y, x, c)], LAST))
        after = [
            exchange_dp(w, lambda dp: columns_of(given.gate_weight, dp, unit), lambda dp: rows_of(got.gate_weight, dp, deep // count)),
            exchange_dp(w, lambda dp: columns_of(given.up_weight, dp, unit), lambda dp: rows_of(got.up_weight, dp, deep // count)),
            exchange_dp(w, lambda dp: rows_of(given.down_weight, dp, unit), lambda dp: columns_of(got.down_weight, dp, deep // count)),
            exchange_dp(w, lambda dp: columns_of(given.gate_expand, dp, unit), lambda dp: rows_of(got.gate_expand, dp, low // count)),
            exchange_dp(w, lambda dp: columns_of(given.up_expand, dp, unit), lambda dp: rows_of(got.up_expand, dp, low // count)),
        ]
        turn(steps, after)
        w.finish()

    kind = jnp.bfloat16
    given = call(
        kernel,
        0,
        list(vars(tensors).values()) + maps,
        [(shape, kind, False) for shape in shapes.values()],
        [],
        64 * levels + 48 * levels * 3,
        32,
        name="begin",
    )
    return SimpleNamespace(**dict(zip(shapes, given)))


def spread(levels, rows):
    here, wide = rows.shape

    def kernel(own, out, *sems):
        w = Wires(levels, *sems)
        w.greet()
        turn([gather_all(w, own, lambda z, y, x, c: out.at[flat(z, y, x, c)], halves)])
        w.finish()

    (out,) = call(
        kernel, 1, [rows], [((8 * levels, here, wide), rows.dtype, False)], [], 40 * levels, 4, name="spread"
    )
    return out


def gelu_pair(gate):
    inner = GELU * (gate + 0.044715 * gate * gate * gate)
    bend = jnp.tanh(inner)
    slope = GELU * (1.0 + 3.0 * 0.044715 * gate * gate)
    return 0.5 * gate * (1.0 + bend), 0.5 * (1.0 + bend) + 0.5 * gate * (1.0 - bend * bend) * slope


GELU = (2.0 / math.pi) ** 0.5
TALL = 256
GRIP = 4


def feed(levels, rows, tokens, grads, gate_up, down):
    deep, both = gate_up.shape
    unit = both // 2
    total = tokens.shape[0]
    level = total // levels
    count = 2 * levels
    strip = deep // count
    half = total // 2
    steps = level // TALL
    kind = jnp.bfloat16
    scratch = scatter_all_scratch(levels, rows, deep)
    each = len(scratch)

    def kernel(tokens_ref, grads_ref, gate_up_hbm, down_hbm, *refs):
        grad_out, branch_out, pair_hbm, single_hbm, gate_own, up_own = refs[:6]
        hidden_hbm, pre_hbm, grad_part, branch_part, grad_land, branch_land = refs[6:12]
        buffers = refs[12:]
        one, two = buffers[:each], buffers[each : 2 * each - 1]
        two = two[:1] + (one[1],) + two[1:]
        gate_up_ref, down_ref, arena, hidden_stage, pre_stage, columns, down_stage, loads, stores = buffers[
            2 * each - 1 : -3
        ]

        def space(number, slot):
            return arena.at[pl.ds(pl.multiple_of((2 * number + slot) * TALL, TALL), TALL)]

        w = Wires(levels, *buffers[-3:])
        weights = [w.local(gate_up_hbm, gate_up_ref), w.local(down_hbm, down_ref)]
        order = list(planes(w))

        def load(k, j, slot):
            start = pl.ds(pl.multiple_of(order[k] * level + j * TALL, TALL), TALL)
            return (
                pltpu.make_async_copy(tokens_ref.at[start], space(0, slot), loads.at[0, slot]),
                pltpu.make_async_copy(grads_ref.at[start], space(1, slot), loads.at[1, slot]),
            )

        def store(k, j, slot):
            start = pl.multiple_of(order[k] * level + j * TALL, TALL)
            block = order[k] * (level // rows) + j * (TALL // rows)
            made = [
                pltpu.make_async_copy(hidden_stage.at[slot], hidden_hbm.at[pl.ds(start, TALL)], stores.at[0, slot]),
                pltpu.make_async_copy(pre_stage.at[slot], pre_hbm.at[pl.ds(start, TALL)], stores.at[1, slot]),
            ]
            for i in range(TALL // rows):
                piece = pl.ds(i * rows, rows)
                made += [
                    pltpu.make_async_copy(space(2, slot).at[piece], grad_part.at[block + i], stores.at[2 + 2 * i, slot]),
                    pltpu.make_async_copy(space(3, slot).at[piece], branch_part.at[block + i], stores.at[3 + 2 * i, slot]),
                ]
            return made

        for copy in load(0, 0, 0):
            copy.start()
        w.greet(far=True)
        for copy in weights:
            copy.wait()

        lanes = w.take(2 * count)

        def there(i):
            return lax.rem(w.dp + 1 + i, count)

        def strip_of(ref, i):
            return columns_of(ref, there(i), strip)

        def strip_load(ref, i):
            slot = lax.rem(i, 2)
            return pltpu.make_async_copy(strip_of(ref, i), columns.at[slot], loads.at[0, slot])

        def pair_store(i):
            slot = lax.rem(i, 2)
            return pltpu.make_async_copy(pre_stage.at[slot], rows_of(pair_hbm, there(i), strip), stores.at[0, slot])

        def single_store(i):
            slot = lax.rem(i, 2)
            return pltpu.make_async_copy(down_stage.at[slot], strip_of(single_hbm, i), stores.at[1, slot])

        def pair_pieces(i):
            both_rows = rows_of(pair_hbm, there(i), strip)
            yield both_rows.at[:, pl.ds(0, unit)], columns_of(gate_own, w.dp, unit), lanes + i
            yield both_rows.at[:, pl.ds(unit, unit)], columns_of(up_own, w.dp, unit), lanes + count + i

        def give(pieces, i):
            for source, target, lane in pieces(i):
                w.copy(source, target, lane, lane, (there(i), w.mp)).start()

        def keep(pieces):
            for source, target, _ in pieces(count - 1):
                w.local(source, target).wait()

        def product(left, right, left_wide, right_wide):
            return sum(
                lax.dot_general(
                    left[pl.ds(0, half), pl.ds(i * left_wide[0], left_wide[1])] if left_wide[0] else left[pl.ds(i * half, half), :],
                    right[pl.ds(0, half), pl.ds(i * right_wide[0], right_wide[1])] if right_wide[0] else right[pl.ds(i * half, half), :],
                    (((0,), (0,)), ((), ())),
                    preferred_element_type=jnp.float32,
                )
                for i in range(2)
            )

        def pair_strip(i, carry):
            slot = lax.rem(i, 2)
            strip_load(tokens_ref, i).wait()

            @pl.when(i < count - 1)
            def _():
                strip_load(tokens_ref, i + 1).start()

            @pl.when(i == count - 1)
            def _():
                strip_load(grads_ref, count - 1 - i).start()

            pre_stage[slot] = product(columns.at[slot], arena, (0, 0), (both, both)).astype(kind)
            pair_store(i).start()

            @pl.when(i > 0)
            def _():
                pair_store(i - 1).wait()
                give(pair_pieces, i - 1)

            return carry

        def single_strip(i, carry):
            slot = lax.rem(i, 2)
            strip_load(grads_ref, i).wait()

            @pl.when(i < count - 1)
            def _():
                strip_load(grads_ref, i + 1).start()

            down_stage[slot] = product(gate_up_ref, columns.at[slot], (unit, unit), (0, 0)).astype(kind)
            single_store(i).start()

            @pl.when(i > 0)
            def _():
                single_store(i - 1).wait()

            return carry

        made = []

        def gradients():
            while len(made) < levels:
                yield
            held = []
            for i in range(2):
                piece = pl.ds(i * half, half)
                held.append(w.local(pre_hbm.at[piece], arena.at[:, pl.ds(i * both, both)]))
                held.append(w.local(hidden_hbm.at[piece], gate_up_ref.at[:, pl.ds(i * unit, unit)]))
            strip_load(tokens_ref, 0).start()
            for copy in held:
                copy.wait()
            for i in range(0, count, GRIP):
                lax.fori_loop(i, i + GRIP, pair_strip, 0)
                if i + GRIP == count:
                    pair_store(count - 1).wait()
                    keep(pair_pieces)
                yield
            for i in range(0, count, count):
                lax.fori_loop(i, i + count, single_strip, 0)
                yield
            single_store(count - 1).wait()

        def make(k):
            if k >= levels:
                return

            def chunk(j, carry):
                slot = lax.rem(j, 2)
                for copy in load(k, j, slot):
                    copy.wait()

                @pl.when(j < steps - 1)
                def _():
                    for copy in load(k, j + 1, 1 - slot):
                        copy.start()

                if k < levels - 1:

                    @pl.when(j == steps - 1)
                    def _():
                        for copy in load(k + 1, 0, 0):
                            copy.start()

                @pl.when(j >= 2)
                def _():
                    for copy in store(k, j - 2, slot):
                        copy.wait()

                pre = jnp.dot(space(0, slot)[...], gate_up_ref[...], preferred_element_type=jnp.float32)
                back = against(space(1, slot)[...], down_ref[...])
                gate, up = pre[:, :unit], pre[:, unit:]
                bent, slope = gelu_pair(gate)
                hidden = (bent * up).astype(kind)
                grad_pre = jnp.concatenate([back * up * slope, back * bent], axis=1).astype(kind)
                hidden_stage[slot] = hidden
                pre_stage[slot] = grad_pre
                space(2, slot)[...] = against(grad_pre, gate_up_ref[...]).astype(kind)
                space(3, slot)[...] = jnp.dot(hidden, down_ref[...], preferred_element_type=jnp.float32).astype(kind)
                for copy in store(k, j, slot):
                    copy.start()
                return carry

            lax.fori_loop(0, steps, chunk, 0)
            for j in range(max(steps - 2, 0), steps):
                for copy in store(k, j, j % 2):
                    copy.wait()
            made.append(k)
            yield

        def idle(k):
            if k < levels:
                yield

        turn(
            [
                scatter_all(w, one_block(grad_part), grad_land, *one, grad_out, make=make),
                scatter_all(w, one_block(branch_part), branch_land, *two, branch_out, make=idle),
                gradients(),
            ]
        )
        for i in range(count - 1):
            source = lax.rem(w.dp + count - 1 - i, count)
            for sent, (_, _, lane) in zip(
                (columns_of(gate_own, source, unit), columns_of(up_own, source, unit)),
                pair_pieces(i),
            ):
                w.landed(sent, lane)
                w.copy(sent, sent, lane, lane, w.over_x()).wait_send()
        w.finish()

    assert total == 2 * deep and 2 * both == deep and 8 * TALL == deep and strip == TALL
    tall = [(deep, deep), (2, TALL, unit), (2, TALL, both), (2, total, strip), (2, unit, strip)]
    outs = [((rows, deep), jnp.float32, True)] * 2
    outs += [((deep, both), kind, False), ((unit, deep), kind, False)]
    outs += [((strip, unit * count), kind, False)] * 2
    outs += [((total, unit), kind, False), ((total, both), kind, False)]
    outs += [((total // rows, rows, deep), kind, False)] * 2 + [((4 * levels, rows, deep), kind, False)] * 2
    made = call(
        kernel,
        2,
        [tokens, grads, gate_up, down],
        outs,
        scratch
        + scratch[:1]
        + scratch[2:]
        + [pltpu.VMEM(gate_up.shape, kind), pltpu.VMEM(down.shape, kind)]
        + [pltpu.VMEM(shape, kind) for shape in tall]
        + [pltpu.SemaphoreType.DMA((2, 2)), pltpu.SemaphoreType.DMA((2 + 2 * (TALL // rows), 2))],
        2 * 10 * levels + 6 * levels + 4,
        16 * levels + 12,
        name="feed",
    )
    return made[:6]


def share_mp(levels, rows):
    def kernel(own, out, *sems):
        w = Wires(levels, *sems)
        w.greet(flat=True)
        turn([gather_mp(w, own, lambda x, c: out.at[x * 2 + c])])
        w.finish()

    (out,) = call(kernel, 3, [rows], [((4,) + rows.shape, rows.dtype, False)], [], 16, 4, name="share_mp")
    return out


def sum_mp(levels, part):
    _, here, wide = part.shape

    def kernel(given, out, own, first, second, *sems):
        w = Wires(levels, *sems)
        w.greet(flat=True)
        turn([scatter_mp(w, given, own, first, second, out)])
        w.finish()

    (out,) = call(
        kernel,
        4,
        [part],
        [((here, wide), jnp.float32, True)],
        [pltpu.VMEM((2, here, wide), part.dtype)] * 2 + [pltpu.VMEM((here, wide), part.dtype)],
        16,
        4,
        name="sum_mp",
    )
    return out


BACK = 2


def end(levels, rank, small, wides, query, output, rows, units):
    count = 2 * levels
    here = rows.shape[1]
    deep, narrow = small.shape
    few, piece = deep // (4 * count), deep // 4
    wide = narrow + piece
    high = rank // count
    strip = deep // count
    unit = units.down_weight.shape[0]
    names = list(vars(units))
    shapes = dict(
        down_weight=(unit * count, strip),
        gate_expand=(high, unit * count),
        up_expand=(high, unit * count),
    )
    heads = query[0].shape[1]
    query_shape = (strip + high, heads)
    output_shape = (heads + heads // count, strip)
    scratch = scatter_all_scratch(levels, few, wide)
    each = len(scratch)
    scratch += [pltpu.VMEM((levels,) + query_shape, jnp.bfloat16)] * 4
    scratch += [pltpu.VMEM((levels,) + output_shape, jnp.bfloat16)] * 4
    scratch += [pltpu.VMEM((2, here, deep), jnp.bfloat16)] * 2 + [pltpu.VMEM((here, deep), jnp.bfloat16)]

    def kernel(*refs):
        small_ref, wide_one, wide_two, query_w, query_b, output_w, output_a, rows_ref = refs[:8]
        given = SimpleNamespace(**dict(zip(names, refs[8:])))
        refs = refs[8 + len(names) :]
        got = SimpleNamespace(**dict(zip(shapes, refs)))
        small_out, query_out, output_out, shared, rows_out, landing = refs[len(names) : len(names) + 6]
        buffers = refs[len(names) + 6 :]
        w = Wires(levels, *buffers[-3:])
        w.greet(far=True)

        def blocks(z, y, x, c):
            place = (pl.ds(pl.multiple_of((z * 2 + y) * high, high), high), pl.ds(pl.multiple_of((x * 2 + c) * piece, piece), piece))
            yield rows_of(small_ref, flat(z, y, x, c), few), corner(0, few, 0, narrow)
            yield wide_one.at[place], corner(0, high, narrow, piece)
            yield wide_two.at[place], corner(high, high, narrow, piece)

        def query_blocks(z, y):
            yield rows_of(query_w, z * 2 + y, strip), corner(0, strip, 0, heads)
            yield rows_of(query_b, z * 2 + y, high), corner(strip, high, 0, heads)

        def output_blocks(z, y):
            yield columns_of(output_w, z * 2 + y, strip), corner(0, heads, 0, strip)
            yield rows_of(output_a, z * 2 + y, heads // count), corner(heads, heads // count, 0, strip)

        def over_all():
            yield from scatter_all(w, blocks, landing, *buffers[:each], small_out)
            mine = small_out.at[:, pl.ds(narrow, piece)]
            yield from gather_mp(w, mine, lambda x, c: shared.at[x * 2 + c])

        after = [
            exchange_dp(w, lambda dp: columns_of(given.down_weight, dp, strip), lambda dp: rows_of(got.down_weight, dp, unit)),
            exchange_dp(w, lambda dp: rows_of(given.gate_expand, dp, high), lambda dp: columns_of(got.gate_expand, dp, unit)),
            exchange_dp(w, lambda dp: rows_of(given.up_expand, dp, high), lambda dp: columns_of(got.up_expand, dp, unit)),
        ]
        steps = [
            scatter_mp(w, rows_ref, *buffers[each + 8 : each + 11], rows_out),
            over_all(),
            scatter_dp(w, query_blocks, *buffers[each : each + 4], query_out),
            scatter_dp(w, output_blocks, *buffers[each + 4 : each + 8], output_out),
        ]
        turn(steps, after, BACK)
        w.finish()

    outs = [(shape, jnp.bfloat16, False) for shape in shapes.values()]
    outs += [((few, wide), jnp.float32, True), (query_shape, jnp.float32, True), (output_shape, jnp.float32, True)]
    outs += [((4, few, piece), jnp.float32, True), ((here, deep), jnp.float32, True)]
    outs += [((4 * levels, few, wide), jnp.bfloat16, False)]
    made = call(
        kernel,
        5,
        [small, *wides, *query, *output, rows, *vars(units).values()],
        outs,
        scratch,
        32 * levels + 3,
        10 * levels + 18,
        name="end",
    )
    return SimpleNamespace(**dict(zip(shapes, made))), *made[3:8]


def low(rows):
    return rows.astype(jnp.bfloat16)


def unit_rows(rows):
    scale = lax.rsqrt(jnp.mean(rows * rows, axis=-1, keepdims=True) + EPS)
    return rows * scale, scale


def norm_back(grad, normed, scale):
    return scale * (grad - normed * jnp.mean(grad * normed, axis=-1, keepdims=True))


def ones_in(rows, column):
    columns = jnp.arange(128)[None, :]
    return jnp.broadcast_to((columns >= column) & (columns < column + 32), (rows, 128)).astype(jnp.bfloat16)


def by_unit(
    levels,
    layer_input,
    output_grad,
    attention_gain,
    query_weight,
    key_weight,
    value_weight,
    output_weight,
    query_shrink,
    query_expand,
    key_shrink,
    key_expand,
    value_shrink,
    value_expand,
    output_shrink,
    output_expand,
    feedforward_gain,
    gate_weight,
    up_weight,
    down_weight,
    gate_shrink,
    gate_expand,
    up_shrink,
    up_expand,
    down_shrink,
    down_expand,
    group_ids,
    positions,
    segments,
):
    count = 2 * levels
    rows = layer_input.shape[0]
    tokens = 4 * rows
    deep = layer_input.shape[1]
    head = key_weight.shape[1]
    heads = query_weight.shape[1] // head
    rank = query_expand.shape[0] * count
    mp = lax.axis_index("mp")
    share = query_shrink.shape[0] // 4

    gains = jnp.stack([attention_gain, feedforward_gain], axis=1)
    gains = jnp.pad(gains, ((0, 0), (0, 126)))
    maps = [key_weight, value_weight, query_shrink, key_shrink, value_shrink, gate_shrink, up_shrink, gains]
    expands = jnp.concatenate([query_expand, key_expand, value_expand], axis=1)
    got = begin(
        levels,
        SimpleNamespace(
            layer_input=layer_input,
            maps=maps,
            output_expand=output_expand,
            down_expand=down_expand,
            query_weight=query_weight,
            output_weight=output_weight,
            expands=expands,
            output_shrink=output_shrink,
            output_grad=output_grad,
            gate_weight=gate_weight,
            up_weight=up_weight,
            down_weight=down_weight,
            gate_expand=gate_expand,
            up_expand=up_expand,
        ),
    )
    maps = got.maps
    key_w, value_w = maps[:, :head], maps[:, head : 2 * head]
    query_a, key_a, value_a, gate_a, up_a = (
        maps[:, 2 * head + i * rank : 2 * head + (i + 1) * rank] for i in range(5)
    )
    gain_one = maps[:, 2 * head + 5 * rank : 2 * head + 5 * rank + 1].astype(jnp.float32)
    gain_two = maps[:, 2 * head + 5 * rank + 1 : 2 * head + 5 * rank + 2].astype(jnp.float32)
    query_b = got.expands[:, : heads * head]
    key_b = got.expands[:, heads * head : (heads + 1) * head]
    value_b = got.expands[:, (heads + 1) * head :]
    output_a, output_b = got.output_shrink, got.output_expand
    query_full = low(gain_one * (got.query_weight.astype(jnp.float32) + matmul(query_a, query_b)))
    key_full = low(gain_one * (key_w.astype(jnp.float32) + matmul(key_a, key_b)))
    value_full = low(gain_one * (value_w.astype(jnp.float32) + matmul(value_a, value_b)))
    inward = jnp.concatenate([query_full, key_full, value_full], axis=1)
    outward = low(got.output_weight.astype(jnp.float32) + matmul(output_a, output_b))

    allowed = (
        (group_ids[:, None] == group_ids[None, :])
        & (positions[None, :] <= positions[:, None])
        & ((segments[None, :] == 0) | (segments[None, :] == segments[:, None]))
    )
    group_rows = got.layer_input.reshape(tokens, deep).astype(jnp.float32)
    normed = low(unit_rows(group_rows)[0])
    lin = matmul(normed, inward)
    wide = heads * head
    queries = low(rotary(lin[:, :wide].reshape(tokens, heads, head), positions, 1.0) * head ** (-0.5))
    keys = low(rotary(lin[:, None, wide : wide + head], positions, 1.0)[:, 0, :])
    values = low(lin[:, wide + head :])
    scores = jnp.einsum("thd,sd->hts", queries, keys, preferred_element_type=jnp.float32)
    scores = jnp.where(allowed[None], scores, -1e30)
    expo = jnp.exp(scores - jnp.max(scores, axis=-1, keepdims=True))
    probability = expo / jnp.sum(expo, axis=-1, keepdims=True)
    probability_low = low(probability)
    mixed = low(
        jnp.einsum("hts,sd->thd", probability_low, values, preferred_element_type=jnp.float32)
    ).reshape(tokens, wide)
    branch = sum_mp(levels, low(matmul(mixed, outward)).reshape(4, rows, deep))
    own_rows = layer_input.astype(jnp.float32)
    middle = own_rows + branch

    gate_up = low(
        gain_two
        * (
            jnp.concatenate([got.gate_weight, got.up_weight], axis=1).astype(jnp.float32)
            + jnp.concatenate([matmul(gate_a, got.gate_expand), matmul(up_a, got.up_expand)], axis=1)
        )
    )
    unit = got.gate_weight.shape[1]
    down_a, down_b = down_shrink, got.down_expand
    down_full = low(got.down_weight.astype(jnp.float32) + matmul(down_a, down_b))
    normed_middle, scale_middle = unit_rows(middle)
    normed_all = spread(levels, low(normed_middle)).reshape(4 * count * rows, deep)
    grads = got.output_grad.reshape(4 * count * rows, deep)
    grad_normed, branch, pair_grad, down_grad_low, gate_own, up_own = feed(levels, rows, normed_all, grads, gate_up, down_full)
    result = low(middle + branch)
    grad_middle = output_grad.astype(jnp.float32) + norm_back(grad_normed, normed_middle, scale_middle)

    down_shrink_grad = against(down_grad_low, down_b)
    gate_b_grad = low(outer_sum(low(gain_two * gate_a.astype(jnp.float32)), pair_grad[:, :unit]))
    up_b_grad = low(outer_sum(low(gain_two * up_a.astype(jnp.float32)), pair_grad[:, unit:]))
    gate_a_part = gain_two * against(pair_grad[:, :unit], got.gate_expand)
    up_a_part = gain_two * against(pair_grad[:, unit:], got.up_expand)

    grad_branch = share_mp(levels, low(grad_middle)).reshape(tokens, deep)
    output_grad_w = outer_sum(mixed, grad_branch)
    grad_mixed = low(against(grad_branch, outward)).reshape(tokens, heads, head)
    grad_values = jnp.einsum("hts,thd->sd", probability_low, grad_mixed, preferred_element_type=jnp.float32)
    grad_probability = jnp.einsum("thd,sd->hts", grad_mixed, values, preferred_element_type=jnp.float32)
    grad_scores = low(
        probability * (grad_probability - jnp.sum(probability * grad_probability, axis=-1, keepdims=True))
    )
    grad_queries = jnp.einsum("hts,sd->thd", grad_scores, keys, preferred_element_type=jnp.float32)
    grad_keys = jnp.einsum("hts,thd->sd", grad_scores, queries, preferred_element_type=jnp.float32)
    grad_query = rotary(grad_queries * head ** (-0.5), positions, -1.0).reshape(tokens, wide)
    grad_key = rotary(grad_keys[:, None, :], positions, -1.0)[:, 0, :]
    grad_lin = low(jnp.concatenate([grad_query, grad_key, grad_values], axis=1))
    lin_normed = outer_sum(normed, grad_lin)
    lin_grad = low(lin_normed * gain_one)
    query_part, key_part, value_part = (
        lin_grad[:, :wide],
        lin_grad[:, wide : wide + head],
        lin_grad[:, wide + head :],
    )
    output_low = low(output_grad_w)
    gain_parts = matmul(low(lin_normed) * inward, ones_in(inward.shape[1], 0)) + matmul(
        pair_grad * gate_up, ones_in(2 * unit, 32)
    )

    def fold(array):
        return low(array).reshape(4 * count, array.shape[0] // (4 * count), head).reshape(deep, -1)

    folded = jnp.concatenate(
        [fold(outer_sum(key_a, key_part)), fold(outer_sum(value_a, value_part))], axis=1
    )
    small = jnp.concatenate(
        [
            lin_grad[:, wide:],
            low(against(query_part, query_b)),
            low(gate_a_part),
            low(up_a_part),
            low(gain_parts[:, :64]),
            folded,
        ],
        axis=1,
    )
    units, few, query_sum, output_sum, shared, grad_rows = end(
        levels,
        rank,
        small,
        (low(outer_sum(output_a, output_low)), low(outer_sum(down_a, down_grad_low))),
        (query_part, low(outer_sum(query_a, query_part))),
        (output_low, low(against(output_low, output_b))),
        low(against(grad_lin, inward)).reshape(4, rows, deep),
        SimpleNamespace(down_weight=down_grad_low, gate_expand=gate_b_grad, up_expand=up_b_grad),
    )
    normed_own, scale_own = unit_rows(own_rows)
    input_grad = grad_middle + norm_back(grad_rows, normed_own, scale_own)
    key_own, value_own = few[:, :head], few[:, head : 2 * head]
    query_a_own, gate_a_own, up_a_own = (
        few[:, 2 * head + i * rank : 2 * head + (i + 1) * rank] for i in range(3)
    )
    place = 2 * head + 3 * rank
    key_b_own = few[:, place + 64 : place + 96].reshape(-1, head)
    value_b_own = few[:, place + 96 : place + 128].reshape(-1, head)
    high = rank // count

    def unfold(array):
        return jnp.concatenate([array[i] for i in range(4)], axis=1)

    def own_part(gain):
        return lax.dynamic_slice_in_dim(gain.astype(jnp.float32), mp * share, share, 0)

    key_a_own = against(low(key_own), key_b)
    value_a_own = against(low(value_own), value_b)
    wider = jnp.float32
    own_gain = feedforward_gain.astype(wider)[:, None]
    return (
        result,
        input_grad,
        few[:, place] / own_part(attention_gain),
        query_sum[: deep // count],
        key_own,
        value_own,
        output_sum[:wide],
        query_a_own,
        query_sum[deep // count :],
        key_a_own,
        key_b_own,
        value_a_own,
        value_b_own,
        output_sum[wide:],
        unfold(shared[:, :high]),
        few[:, place + 32] / own_part(feedforward_gain),
        own_gain * gate_own.astype(wider),
        own_gain * up_own.astype(wider),
        units.down_weight.astype(wider),
        gate_a_own,
        units.gate_expand.astype(wider),
        up_a_own,
        units.up_expand.astype(wider),
        down_shrink_grad,
        unfold(shared[:, high:]),
    )


def body(
    layer_input,
    output_grad,
    attention_gain,
    query_weight,
    key_weight,
    value_weight,
    output_weight,
    query_shrink,
    query_expand,
    key_shrink,
    key_expand,
    value_shrink,
    value_expand,
    output_shrink,
    output_expand,
    feedforward_gain,
    gate_weight,
    up_weight,
    down_weight,
    gate_shrink,
    gate_expand,
    up_shrink,
    up_expand,
    down_shrink,
    down_expand,
    group_ids,
    positions,
    segments,
):
    rows_local = layer_input.shape[0]
    own_start = lax.axis_index("mp") * rows_local
    allowed = (
        (group_ids[:, None] == group_ids[None, :])
        & (positions[None, :] <= positions[:, None])
        & ((segments[None, :] == 0) | (segments[None, :] == segments[:, None]))
    )

    def gather_attention():
        return (
            lax.all_gather(attention_gain, "dp", axis=0, tiled=True),
            lax.all_gather(query_weight, "dp", axis=0, tiled=True),
            lax.all_gather(key_weight, "dp", axis=0, tiled=True),
            lax.all_gather(value_weight, "dp", axis=0, tiled=True),
            lax.all_gather(output_weight, "dp", axis=1, tiled=True),
            lax.all_gather(query_shrink, "dp", axis=0, tiled=True),
            lax.all_gather(query_expand, "dp", axis=0, tiled=True),
            lax.all_gather(key_shrink, "dp", axis=0, tiled=True),
            lax.all_gather(key_expand, "dp", axis=0, tiled=True),
            lax.all_gather(value_shrink, "dp", axis=0, tiled=True),
            lax.all_gather(value_expand, "dp", axis=0, tiled=True),
            lax.all_gather(output_shrink, "dp", axis=0, tiled=True),
            lax.all_gather(output_expand, "dp", axis=0, tiled=True),
        )

    def gather_feed():
        return (
            lax.all_gather(feedforward_gain, "dp", axis=0, tiled=True),
            lax.all_gather(gate_weight, "dp", axis=0, tiled=True),
            lax.all_gather(up_weight, "dp", axis=0, tiled=True),
            lax.all_gather(down_weight, "dp", axis=1, tiled=True),
            lax.all_gather(gate_shrink, "dp", axis=0, tiled=True),
            lax.all_gather(gate_expand, "dp", axis=0, tiled=True),
            lax.all_gather(up_shrink, "dp", axis=0, tiled=True),
            lax.all_gather(up_expand, "dp", axis=0, tiled=True),
            lax.all_gather(down_shrink, "dp", axis=0, tiled=True),
            lax.all_gather(down_expand, "dp", axis=0, tiled=True),
        )

    def gather_rows(rows):
        return lax.all_gather(rows, "mp", axis=0, tiled=True)

    def gather_grads(rows):
        return lax.all_gather(rows, "mp", axis=0, tiled=True)

    def scatter_grads(term):
        return lax.psum_scatter(
            term(jnp.int32(0), lax.axis_size("mp") * rows_local),
            "mp",
            scatter_dimension=0,
            tiled=True,
        )

    def project_out(mixed, weight, shrink, expand):
        reduced = lax.psum(matmul(mixed, shrink), "mp").astype(jnp.bfloat16)

        def term(start, count):
            return matmul(mixed, weight)

        branch = lax.psum_scatter(
            term(jnp.int32(0), lax.axis_size("mp") * rows_local),
            "mp",
            scatter_dimension=0,
            tiled=True,
        )
        own = lax.dynamic_slice_in_dim(reduced, own_start, rows_local, 0)
        return (branch + matmul(own, expand), reduced)

    def masked_scores(queries, keys_rot):
        scores = jnp.einsum("thd,sd->hts", queries, keys_rot, preferred_element_type=jnp.float32)
        return jnp.where(allowed[None], scores, -1e30)

    def attention_forward(rows_in, params):
        (
            gain_one,
            w_query,
            w_key,
            w_value,
            w_output,
            query_a,
            query_b,
            key_a,
            key_b,
            value_a,
            value_b,
            output_a,
            output_b,
        ) = params
        normed = gather_rows(norm_rows(rows_in, gain_one.astype(jnp.float32)).astype(jnp.bfloat16))
        tokens = normed.shape[0]
        head_size = w_key.shape[1]
        heads = w_query.shape[1] // head_size
        query_low = matmul(normed, query_a).astype(jnp.bfloat16)
        key_low = matmul(normed, key_a).astype(jnp.bfloat16)
        value_low = matmul(normed, value_a).astype(jnp.bfloat16)
        query_lin = matmul(normed, w_query) + matmul(query_low, query_b)
        key_lin = matmul(normed, w_key) + matmul(key_low, key_b)
        value_lin = matmul(normed, w_value) + matmul(value_low, value_b)
        queries = (
            rotary(query_lin.reshape(tokens, heads, head_size), positions, 1.0)
            * head_size ** (-0.5)
        ).astype(jnp.bfloat16)
        keys_rot = rotary(key_lin[:, None, :], positions, 1.0)[:, 0, :].astype(jnp.bfloat16)
        values = value_lin.astype(jnp.bfloat16)
        scores = masked_scores(queries, keys_rot)
        highest = jnp.max(scores, axis=-1, keepdims=True)
        expo = jnp.exp(scores - highest)
        totals = jnp.sum(expo, axis=-1, keepdims=True)
        probability = expo / totals
        logsum = highest + jnp.log(totals)
        mixed = jnp.einsum(
            "hts,sd->thd",
            probability.astype(jnp.bfloat16),
            values,
            preferred_element_type=jnp.float32,
        )
        mixed = mixed.reshape(tokens, heads * head_size).astype(jnp.bfloat16)
        branch, reduced = project_out(mixed, w_output, output_a, output_b)
        saved = (
            normed,
            query_low,
            key_low,
            value_low,
            queries,
            keys_rot,
            values,
            logsum,
            mixed,
            reduced,
        )
        return (rows_in + branch, saved)

    def feed_forward(middle, params):
        gain_two, w_gate, w_up, w_down, gate_a, gate_b, up_a, up_b, down_a, down_b = params
        normed = gather_rows(norm_rows(middle, gain_two.astype(jnp.float32)).astype(jnp.bfloat16))
        gate_low = matmul(normed, gate_a).astype(jnp.bfloat16)
        up_low = matmul(normed, up_a).astype(jnp.bfloat16)
        gate_pre = matmul(normed, w_gate) + matmul(gate_low, gate_b)
        up_pre = matmul(normed, w_up) + matmul(up_low, up_b)
        hidden = (jax.nn.gelu(gate_pre, approximate=True) * up_pre).astype(jnp.bfloat16)
        branch, reduced = project_out(hidden, w_down, down_a, down_b)
        return (middle + branch, (normed, gate_low, up_low, gate_pre, up_pre, hidden, reduced))

    rows_in = layer_input.astype(jnp.float32)
    attention_params = gather_attention()
    middle, attention_saved = attention_forward(rows_in, attention_params)
    feed_params = gather_feed()
    result, feed_saved = feed_forward(middle, feed_params)
    feed_params = gather_feed()
    feed_saved = feed_forward(middle, feed_params)[1]
    gain_two, w_gate, w_up, w_down, gate_a, gate_b, up_a, up_b, down_a, down_b = feed_params
    normed_feed, gate_low, up_low, gate_pre, up_pre, hidden, reduced_feed = feed_saved
    grad_branch_feed = gather_grads(output_grad)
    down_weight_grad = outer_sum(hidden, grad_branch_feed)
    down_expand_grad = outer_sum(reduced_feed, grad_branch_feed)
    grad_reduced_feed = against(grad_branch_feed, down_b).astype(jnp.bfloat16)
    down_shrink_grad = outer_sum(hidden, grad_reduced_feed)
    grad_hidden = against(grad_branch_feed, w_down) + against(grad_reduced_feed, down_a)
    unused, gelu_pull = jax.vjp(
        lambda gated, upper: jax.nn.gelu(gated, approximate=True) * upper, gate_pre, up_pre
    )
    grad_gate, grad_up = gelu_pull(grad_hidden)
    grad_gate = grad_gate.astype(jnp.bfloat16)
    grad_up = grad_up.astype(jnp.bfloat16)
    gate_expand_grad = outer_sum(gate_low, grad_gate)
    up_expand_grad = outer_sum(up_low, grad_up)
    grad_gate_low = against(grad_gate, gate_b)
    grad_up_low = against(grad_up, up_b)
    feed_wide = normed_feed.astype(jnp.float32)
    gate_shrink_grad = outer_exact(feed_wide, grad_gate_low)
    up_shrink_grad = outer_exact(feed_wide, grad_up_low)
    gate_a_wide = gate_a.astype(jnp.float32)
    up_a_wide = up_a.astype(jnp.float32)

    def feed_term(start, count):

        def pick(rows):
            return rows

        total = against(pick(grad_gate), w_gate) + against(pick(grad_up), w_up)
        return (
            total
            + against_exact(pick(grad_gate_low), gate_a_wide)
            + against_exact(pick(grad_up_low), up_a_wide)
        )

    grad_normed_feed = scatter_grads(feed_term)
    unused, norm_pull = jax.vjp(norm_rows, middle, gain_two.astype(jnp.float32))
    grad_middle_part, feed_gain_grad = norm_pull(grad_normed_feed)
    grad_middle = output_grad.astype(jnp.float32) + grad_middle_part
    gate_weight_grad = outer_sum(normed_feed, grad_gate)
    up_weight_grad = outer_sum(normed_feed, grad_up)
    feed_split = (
        lax.psum_scatter(
            gate_weight_grad.astype(jnp.bfloat16), "dp", scatter_dimension=0, tiled=True
        ).astype(jnp.float32),
        lax.psum_scatter(
            up_weight_grad.astype(jnp.bfloat16), "dp", scatter_dimension=0, tiled=True
        ).astype(jnp.float32),
        lax.psum_scatter(
            down_weight_grad.astype(jnp.bfloat16), "dp", scatter_dimension=1, tiled=True
        ).astype(jnp.float32),
        lax.psum_scatter(
            gate_expand_grad.astype(jnp.bfloat16), "dp", scatter_dimension=0, tiled=True
        ).astype(jnp.float32),
        lax.psum_scatter(
            up_expand_grad.astype(jnp.bfloat16), "dp", scatter_dimension=0, tiled=True
        ).astype(jnp.float32),
        lax.psum_scatter(
            down_shrink_grad.astype(jnp.bfloat16), "dp", scatter_dimension=0, tiled=True
        ).astype(jnp.float32),
        lax.psum_scatter(
            down_expand_grad.astype(jnp.bfloat16), "dp", scatter_dimension=0, tiled=True
        ).astype(jnp.float32),
    )
    gate_weight_own, up_weight_own = (feed_split[0], feed_split[1])
    down_weight_own, gate_expand_own, up_expand_own, down_shrink_own, down_expand_own = (
        feed_split[2],
        feed_split[3],
        feed_split[4],
        feed_split[5],
        feed_split[6],
    )
    feed_shared = (
        lax.psum_scatter(feed_gain_grad, ("dp", "mp"), scatter_dimension=0, tiled=True),
        lax.psum_scatter(gate_shrink_grad, ("dp", "mp"), scatter_dimension=0, tiled=True),
        lax.psum_scatter(up_shrink_grad, ("dp", "mp"), scatter_dimension=0, tiled=True),
    )
    attention_params = gather_attention()
    attention_saved = attention_forward(rows_in, attention_params)[1]
    (
        gain_one,
        w_query,
        w_key,
        w_value,
        w_output,
        query_a,
        query_b,
        key_a,
        key_b,
        value_a,
        value_b,
        output_a,
        output_b,
    ) = attention_params
    normed, query_low, key_low, value_low, queries, keys_rot, values, logsum, mixed, reduced = (
        attention_saved
    )
    tokens = normed.shape[0]
    head_size = w_key.shape[1]
    heads = w_query.shape[1] // head_size
    grad_branch = gather_grads(grad_middle.astype(jnp.bfloat16))
    output_weight_grad = outer_sum(mixed, grad_branch)
    output_expand_grad = outer_sum(reduced, grad_branch)
    grad_reduced = against(grad_branch, output_b).astype(jnp.bfloat16)
    output_shrink_grad = outer_sum(mixed, grad_reduced)
    grad_mixed = (against(grad_branch, w_output) + against(grad_reduced, output_a)).astype(
        jnp.bfloat16
    )
    grad_mixed = grad_mixed.reshape(tokens, heads, head_size)
    probability = jnp.exp(masked_scores(queries, keys_rot) - logsum)
    grad_values = jnp.einsum(
        "hts,thd->sd",
        probability.astype(jnp.bfloat16),
        grad_mixed,
        preferred_element_type=jnp.float32,
    )
    grad_probability = jnp.einsum(
        "thd,sd->hts", grad_mixed, values, preferred_element_type=jnp.float32
    )
    grad_scores = probability * (
        grad_probability - jnp.sum(probability * grad_probability, axis=-1, keepdims=True)
    )
    grad_scores = grad_scores.astype(jnp.bfloat16)
    grad_queries_rot = jnp.einsum(
        "hts,sd->thd", grad_scores, keys_rot, preferred_element_type=jnp.float32
    )
    grad_keys_rot = jnp.einsum(
        "hts,thd->sd", grad_scores, queries, preferred_element_type=jnp.float32
    )
    grad_query = (
        rotary(grad_queries_rot * head_size ** (-0.5), positions, -1.0)
        .reshape(tokens, heads * head_size)
        .astype(jnp.bfloat16)
    )
    grad_key = rotary(grad_keys_rot[:, None, :], positions, -1.0)[:, 0, :]
    normed_wide = normed.astype(jnp.float32)
    query_weight_grad = outer_sum(normed, grad_query)
    query_expand_grad = outer_sum(query_low, grad_query)
    grad_query_low = against(grad_query, query_b)
    query_shrink_grad = outer_exact(normed_wide, grad_query_low)
    key_weight_grad = outer_exact(normed_wide, grad_key)
    key_expand_grad = outer_exact(key_low.astype(jnp.float32), grad_key)
    grad_key_low = against_exact(grad_key, key_b.astype(jnp.float32))
    key_shrink_grad = outer_exact(normed_wide, grad_key_low)
    value_weight_grad = outer_exact(normed_wide, grad_values)
    value_expand_grad = outer_exact(value_low.astype(jnp.float32), grad_values)
    grad_value_low = against_exact(grad_values, value_b.astype(jnp.float32))
    value_shrink_grad = outer_exact(normed_wide, grad_value_low)
    query_a_wide = query_a.astype(jnp.float32)
    key_wide = w_key.astype(jnp.float32)
    key_a_wide = key_a.astype(jnp.float32)
    value_wide = w_value.astype(jnp.float32)
    value_a_wide = value_a.astype(jnp.float32)

    def attention_term(start, count):

        def pick(rows):
            return rows

        total = against(pick(grad_query), w_query) + against_exact(
            pick(grad_query_low), query_a_wide
        )
        total = (
            total
            + against_exact(pick(grad_key), key_wide)
            + against_exact(pick(grad_key_low), key_a_wide)
        )
        return (
            total
            + against_exact(pick(grad_values), value_wide)
            + against_exact(pick(grad_value_low), value_a_wide)
        )

    grad_normed = scatter_grads(attention_term)
    unused, norm_pull_one = jax.vjp(norm_rows, rows_in, gain_one.astype(jnp.float32))
    grad_input_part, attention_gain_grad = norm_pull_one(grad_normed)
    input_grad = grad_middle + grad_input_part
    attention_split = (
        lax.psum_scatter(
            query_weight_grad.astype(jnp.bfloat16), "dp", scatter_dimension=0, tiled=True
        ).astype(jnp.float32),
        lax.psum_scatter(
            output_weight_grad.astype(jnp.bfloat16), "dp", scatter_dimension=1, tiled=True
        ).astype(jnp.float32),
        lax.psum_scatter(
            query_expand_grad.astype(jnp.bfloat16), "dp", scatter_dimension=0, tiled=True
        ).astype(jnp.float32),
        lax.psum_scatter(
            output_shrink_grad.astype(jnp.bfloat16), "dp", scatter_dimension=0, tiled=True
        ).astype(jnp.float32),
        lax.psum_scatter(
            output_expand_grad.astype(jnp.bfloat16), "dp", scatter_dimension=0, tiled=True
        ).astype(jnp.float32),
    )
    attention_shared = (
        lax.psum_scatter(attention_gain_grad, ("dp", "mp"), scatter_dimension=0, tiled=True),
        lax.psum_scatter(key_weight_grad, ("dp", "mp"), scatter_dimension=0, tiled=True),
        lax.psum_scatter(value_weight_grad, ("dp", "mp"), scatter_dimension=0, tiled=True),
        lax.psum_scatter(query_shrink_grad, ("dp", "mp"), scatter_dimension=0, tiled=True),
        lax.psum_scatter(key_shrink_grad, ("dp", "mp"), scatter_dimension=0, tiled=True),
        lax.psum_scatter(key_expand_grad, ("dp", "mp"), scatter_dimension=0, tiled=True),
        lax.psum_scatter(value_shrink_grad, ("dp", "mp"), scatter_dimension=0, tiled=True),
        lax.psum_scatter(value_expand_grad, ("dp", "mp"), scatter_dimension=0, tiled=True),
    )
    return (
        result.astype(jnp.bfloat16),
        input_grad,
        attention_shared[0],
        attention_split[0],
        attention_shared[1],
        attention_shared[2],
        attention_split[1],
        attention_shared[3],
        attention_split[2],
        attention_shared[4],
        attention_shared[5],
        attention_shared[6],
        attention_shared[7],
        attention_split[3],
        attention_split[4],
        feed_shared[0],
        gate_weight_own,
        up_weight_own,
        down_weight_own,
        feed_shared[1],
        gate_expand_own,
        feed_shared[2],
        up_expand_own,
        down_shrink_own,
        down_expand_own,
    )


def solution(mesh):
    levels = mesh.shape["dp"] // 2
    few = mesh.shape["mp"] == 4 and mesh.shape["dp"] % 2 == 0 and levels <= 4
    step = functools.partial(by_unit, levels) if few else body
    placed = (
        P(("dp", "mp"), None),
        P(("dp", "mp"), None),
        P("dp"),
        P("dp", "mp"),
        P("dp", None),
        P("dp", None),
        P("mp", "dp"),
        P("dp", None),
        P("dp", "mp"),
        P("dp", None),
        P("dp", None),
        P("dp", None),
        P("dp", None),
        P(("mp", "dp"), None),
        P("dp", None),
        P("dp"),
        P("dp", "mp"),
        P("dp", "mp"),
        P("mp", "dp"),
        P("dp", None),
        P("dp", "mp"),
        P("dp", None),
        P("dp", "mp"),
        P(("mp", "dp"), None),
        P("dp", None),
        P("dp"),
        P("dp"),
        P("dp"),
    )
    return jax.shard_map(
        step,
        mesh=mesh,
        in_specs=placed,
        out_specs=(
            P(("dp", "mp"), None),
            P(("dp", "mp"), None),
            P(("dp", "mp")),
            P("dp", "mp"),
            P(("dp", "mp"), None),
            P(("dp", "mp"), None),
            P("mp", "dp"),
            P(("dp", "mp"), None),
            P("dp", "mp"),
            P(("dp", "mp"), None),
            P(("dp", "mp"), None),
            P(("dp", "mp"), None),
            P(("dp", "mp"), None),
            P(("mp", "dp"), None),
            P("dp", None),
            P(("dp", "mp")),
            P("dp", "mp"),
            P("dp", "mp"),
            P("mp", "dp"),
            P(("dp", "mp"), None),
            P("dp", "mp"),
            P(("dp", "mp"), None),
            P("dp", "mp"),
            P(("mp", "dp"), None),
            P("dp", None),
        ),
        check_vma=False,
    )
```
